32 devices in a mesh: groups: 2 (over x), seq: 16 (over z, y, core).
Axes of the slice: x: 2, y: 2, z: 4, core: 2. Of those that a mesh axis runs over, the one named last changes fastest.
Arguments:
- first_inputs: float32 [288, 32768], P(None, ('groups', 'seq')), parts along dimension 1, may hold values from -6 to 6
- second_inputs: float32 [288, 32768], P(None, ('groups', 'seq')), parts along dimension 1, may hold values from -6 to 6
- out_grad: float32 [288, 32768], P(None, ('groups', 'seq')), parts along dimension 1, may hold values from -6 to 6
- weight_in: float32 [2, 288, 384], replicated, may hold values from -0.375 to 0.375
- bias_in: float32 [2, 384], replicated, may hold values from -4 to 4
- weight_out: float32 [2, 384, 288], replicated, may hold values from -0.3125 to 0.3125
- distances: int32 [2, 18], replicated, may hold values from 0 to 8192, as said below
Outputs:
- input_grad: float32 [288, 32768], P(None, ('groups', 'seq')), parts along dimension 1
- weight_in_grad: float32 [4, 288, 384], P('groups'), parts along dimension 0
- bias_in_grad: float32 [4, 384], P('groups'), parts along dimension 0
- weight_out_grad: float32 [4, 384, 288], P('groups'), parts along dimension 0
The draws below stay inside these ranges and needn't reach their ends.
There are 2 independent parts, one for each index of `groups`. The reference program is written for one: setup_inputs(seed, part) draws one part's arguments, and reference() takes and returns one part's arrays. A program takes and returns all parts, laid end to end along the dimension named above; an argument that names none is the same for every part. Nothing has to cross between parts.
Inputs may be any that keep to these rules, and one draw needn't show every extreme that they name: `distances`: every entry is 0 or a power of two. In each layer no more than 3 tracks share a distance; 3 tracks have distance 16384 // 2 and one track has distance 1024 // 2.
All inputs are finite; a program needn't handle non-finite values.
Results may differ from the reference program's by a relative error of at most 0.0001.
Values sent between devices are 32-bit elements; how exact they have to be, the bound alone decides.
No kernel may reach another device: no remote copies, remote signals or barrier semaphores. Data moves between devices by JAX's collectives and lax.ppermute only.
A program may use at most 64 MiB of HBM per device.

```python
import jax
import jax.numpy as jnp
import numpy as np
from jax import lax

TRACKS = 18
TW = 16
HIDDEN_SIZE = 384
LAYERS = 2
MOST = 3
POS_DEV = 1024
D = 288
LENGTH = 16384


def draw_distances(key, part):
    largest = LENGTH // 2
    top_power = largest.bit_length() - 1
    inner = POS_DEV // 2
    values = [0] + [2 ** k for k in range(top_power) if 2 ** k != inner]
    pool = jnp.asarray(np.repeat(np.array(values, dtype=np.int32), MOST), dtype=jnp.int32)
    layer_rows = []
    for layer_index in range(LAYERS):
        layer_key = jax.random.fold_in(key, 101 + layer_index)
        pool_key = jax.random.fold_in(layer_key, 7)
        order_key = jax.random.fold_in(layer_key, 11)
        mixed = jax.random.permutation(pool_key, pool)
        fixed_part = jnp.concatenate([jnp.full((MOST,), largest, dtype=jnp.int32), jnp.full((1,), inner, dtype=jnp.int32)])
        picks = jnp.concatenate([fixed_part, mixed[:TRACKS - MOST - 1]])
        order = jax.random.permutation(order_key, TRACKS)
        layer_rows.append(picks[order])
    return jnp.stack(layer_rows).astype(jnp.int32)


def steps_of(rng, shape, shards, smallest, top_value):
    def one(dim, blocks):
        heights = jax.random.uniform(jax.random.fold_in(jax.random.fold_in(rng, 6), dim), (blocks,), jnp.float32, smallest / len(shards), top_value / len(shards))
        return jnp.repeat(jnp.exp(heights), shape[dim] // blocks).reshape((-1,) + (1,) * (len(shape) - dim - 1))

    level = one(*shards[0])
    for cut in shards[1:]:
        level = level * one(*cut)
    return level


def bell_draw(own_key, extent, spread, most, shards=(), kind=jnp.bfloat16):
    entries = jax.random.normal(own_key, extent, jnp.float32) * spread
    if len(shards) > 0:
        entries = steps_of(own_key, extent, shards, -0.22, 0.18) * entries
    return jnp.clip(entries, min=-most, max=most).astype(kind)


def setup_inputs(seed: int = 0, part: int = 0) -> dict:
    key_of = jax.random.split(jax.random.key(seed), 8)
    part_splits = jax.random.split(jax.random.fold_in(key_of[7], part), 8)
    return {
        "first_inputs": bell_draw(part_splits[0], (D, LENGTH), 1.0, 6.0, ((1, 16),), jnp.float32),
        "second_inputs": bell_draw(part_splits[1], (D, LENGTH), 1.0, 6.0, ((1, 16),), jnp.float32),
        "out_grad": bell_draw(part_splits[2], (D, LENGTH), 1.0, 6.0, ((1, 16),), jnp.float32),
        "weight_in": bell_draw(key_of[3], (LAYERS, D, HIDDEN_SIZE), D ** -0.5, 0.375, (), jnp.float32),
        "bias_in": bell_draw(key_of[4], (LAYERS, HIDDEN_SIZE), 1.0, 4.0, (), jnp.float32),
        "weight_out": bell_draw(key_of[5], (LAYERS, HIDDEN_SIZE, D), HIDDEN_SIZE ** -0.5, 0.3125, (), jnp.float32),
        "distances": draw_distances(jax.random.fold_in(key_of[7], 71), part),
    }


root_half = 0.7071067811865476
inv_root_two_pi = 0.3989422804014327


def rotate_back(grad, shifts):
    tracks = grad.reshape(TRACKS, TW, LENGTH)
    doubled = jnp.concatenate([tracks, tracks], axis=2)

    def one_track(track_data, offset):
        return lax.dynamic_slice_in_dim(track_data, offset, LENGTH, axis=1)

    rolled = jax.vmap(one_track)(doubled, shifts.astype(jnp.int32))
    return rolled.reshape(TRACKS * TW, LENGTH)


def layer_backward(saved, grad_out, weight_a, bias_a, weight_b, shifts, factor):
    highest = lax.Precision.HIGHEST
    preact = jnp.einsum("dh,dp->hp", weight_a, saved, precision=highest) + bias_a[:, None]
    normal_cdf = 0.5 * (1.0 + lax.erf(preact * root_half))
    hidden_act = preact * normal_cdf
    slope = normal_cdf + preact * jnp.exp(-0.5 * preact * preact) * inv_root_two_pi
    grad_mid = rotate_back(grad_out, shifts)
    grad_hidden = jnp.dot(weight_b, grad_mid, precision=highest) * slope
    grad_in = grad_mid + jnp.dot(weight_a, grad_hidden, precision=highest)
    weight_a_grad = jnp.einsum("dp,hp->dh", saved, grad_hidden, precision=highest) * factor
    bias_a_grad = jnp.sum(grad_hidden, axis=1) * factor
    weight_b_grad = jnp.einsum("hp,dp->hd", hidden_act, grad_mid, precision=highest) * factor
    return grad_in, weight_a_grad, bias_a_grad, weight_b_grad


def reference(first_inputs, second_inputs, out_grad, weight_in, bias_in, weight_out, distances):
    factor = 1.0 / (float(LENGTH) ** 0.5)
    saved_list = [first_inputs, second_inputs]
    grad_now = out_grad
    results_a = [None, None]
    results_b = [None, None]
    results_c = [None, None]
    for layer_index in [1, 0]:
        grad_now, grad_a, grad_b, grad_c = layer_backward(saved_list[layer_index], grad_now, weight_in[layer_index], bias_in[layer_index], weight_out[layer_index], distances[layer_index], factor)
        results_a[layer_index] = grad_a
        results_b[layer_index] = grad_b
        results_c[layer_index] = grad_c
    return grad_now, jnp.stack(results_a), jnp.stack(results_b), jnp.stack(results_c)
```

```python
import math

import jax
import jax.numpy as jnp
from jax import lax
from jax.experimental import pallas as pl
from jax.experimental.pallas import tpu as pltpu
from jax.sharding import PartitionSpec as P

TRACKS = 18
TW = 16
MOST = 3
D = TRACKS * TW
HID = 384
INNER = TRACKS - MOST
LANES = 128
MIB = 1 << 20

ROOT_HALF = 0.7071067811865476
INV_ROOT_TWO_PI = 0.3989422804014327

f32, bf16, i32 = jnp.float32, jnp.bfloat16, jnp.int32
VM = pl.BlockSpec(memory_space=pltpu.VMEM)
SM = pl.BlockSpec(memory_space=pltpu.SMEM)


def params(mib):
    return pltpu.CompilerParams(vmem_limit_bytes=mib * MIB)


def near_slots(pos):
    slots, offset = [], 0
    for slot in range(INNER):
        width = max(LANES, pos >> (slot // MOST))
        slots.append((offset, width))
        offset += width
    return slots, offset


def halves(value):
    high = value.astype(bf16)
    return high, (value - high.astype(f32)).astype(bf16)


def put_triple(ref, value, rows, cols, order):
    pair = halves(value)
    for place, which in enumerate(order):
        ref[place * rows:(place + 1) * rows, cols] = pair[which]


def fill_tables(dist, tab, layer, hops, pos):
    d = [dist[layer, t] for t in range(TRACKS)]
    key = [d[t] * 32 + (31 - t) for t in range(TRACKS)]
    rank = [jnp.int32(0)] * TRACKS
    for t in range(TRACKS):
        for u in range(t + 1, TRACKS):
            above = (key[u] > key[t]).astype(i32)
            rank[t] = rank[t] + above
            rank[u] = rank[u] + (1 - above)
    for t in range(TRACKS):
        tab[layer, rank[t]] = jnp.int32(t)
    for k in range(hops):
        first = jnp.int32(0)
        for t in range(TRACKS):
            first = first + (d[t] > (pos << k)).astype(i32)
        tab[layer, TRACKS + k] = first


def track_at(tab, layer, k, slot):
    place = tab[layer, TRACKS + k] + slot
    return place, tab[layer, jnp.minimum(place, TRACKS - 1)]


def rows_of(track):
    return pl.ds(pl.multiple_of(track * TW, TW), TW)


def pack(src, tab, layer, far, near, hops, pos):
    for k in range(1, hops):
        for slot in range(MOST):
            _, t = track_at(tab, layer, k, slot)
            far[k - 1][slot * TW:(slot + 1) * TW, :] = src[rows_of(t), :]
    for slot, (offset, width) in enumerate(near_slots(pos)[0]):
        _, t = track_at(tab, layer, 0, slot)
        near[:, offset:offset + width] = src[rows_of(t), :width]


def unpack(src, dist, tab, layer, far, near, out, join, hops, pos):
    for k in range(1, hops):
        for slot in range(MOST):
            place, t = track_at(tab, layer, k, slot)

            @pl.when((place < TRACKS) & (dist[layer, t] == (pos << k)))
            def _(k=k, slot=slot, t=t):
                out[rows_of(t), :] = far[k - 1][slot * TW:(slot + 1) * TW, :]

    for slot, (offset, width) in enumerate(near_slots(pos)[0]):
        place, t = track_at(tab, layer, 0, slot)

        @pl.when(place < TRACKS)
        def _(slot=slot, t=t, offset=offset, width=width):
            shift = dist[layer, t]
            join[:, :pos] = src[rows_of(t), :]
            join[:, pos:pos + width] = near[:, offset:offset + width]
            base = pl.multiple_of(shift // LANES * LANES, LANES)
            rest = shift % LANES
            window = join[:, pl.ds(base, pos + LANES)]
            turned = pltpu.roll(window, jnp.where(rest == 0, 0, pos + LANES - rest), 1)
            out[rows_of(t), :] = turned[:, :pos]


def pack_kernel(hops, pos, dist, src, tab, near, *far):
    for layer in (1, 0):
        fill_tables(dist, tab, layer, hops, pos)
    pack(src, tab, 1, far, near, hops, pos)


def act_kernel(pos, x, w_in, bias, w_out, x2, h2, slope, wi3, wo3, xs):
    step = 256
    wt = jnp.transpose(w_in[...], (1, 0))
    wt_hi, wt_lo = halves(wt)
    wt3 = jnp.concatenate([wt_hi, wt_hi, wt_lo], axis=1)
    w_hi, w_lo = halves(w_in[...])
    wi3[...] = jnp.concatenate([w_hi, w_hi, w_lo], axis=1)
    w_hi, w_lo = halves(w_out[...])
    wo3[...] = jnp.concatenate([w_hi, w_hi, w_lo], axis=1)
    for start in range(0, pos, step):
        cols = slice(start, start + step)
        x_hi, x_lo = halves(x[:, cols])
        x2[0:D, cols] = x_hi
        x2[D:D + 16, cols] = jnp.ones((16, step), bf16)
        x2[D + 16:2 * D + 16, cols] = x_lo
        x2[2 * D + 16:2 * D + 32, cols] = jnp.zeros((16, step), bf16)
        xs[0:D, :] = x_hi
        xs[D:2 * D, :] = x_lo
        xs[2 * D:3 * D, :] = x_hi
        pre = jnp.dot(wt3, xs[...], preferred_element_type=f32) + bias[...]
        cdf = 0.5 * (1.0 + lax.erf(pre * ROOT_HALF))
        put_triple(h2, pre * cdf, HID, cols, (0, 1))
        slope[:, cols] = cdf + pre * jnp.exp(-0.5 * pre * pre) * INV_ROOT_TWO_PI


def hidden(pos, wo3, slope, gm, gm3, gh3):
    step = 512
    for start in range(0, pos, step):
        cols = slice(start, start + step)
        put_triple(gm3, gm[:, cols], D, cols, (0, 1, 0))
        gh = jnp.dot(wo3[...], gm3[:, cols], preferred_element_type=f32) * slope[:, cols]
        put_triple(gh3, gh, HID, cols, (0, 1, 0))


def inward(pos, wi3, gm, gh3, out):
    step = 512
    for start in range(0, pos, step):
        cols = slice(start, start + step)
        out[:, cols] = gm[:, cols] + jnp.dot(wi3[...], gh3[:, cols], preferred_element_type=f32)


def weight_terms(factor, x2, gh3, h2, gm3, terms):
    def nt(a, b):
        return lax.dot_general(a, b, (((1,), (1,)), ((), ())), preferred_element_type=f32)

    d1 = D + 16
    first = nt(x2[0:d1, :], gh3[0:HID, :]) + nt(x2[0:d1, :], gh3[HID:2 * HID, :]) + nt(x2[d1:2 * d1, :], gh3[0:HID, :])
    first = first[0:D + 8] * factor
    second = nt(gm3[0:D, :], h2[0:HID, :]) + nt(gm3[0:D, :], h2[HID:2 * HID, :]) + nt(gm3[D:2 * D, :], h2[0:HID, :])
    second = second * factor
    used = 0
    for part in (first, second):
        rows = part.shape[0]
        for j in range(HID // LANES):
            terms[used:used + rows, :] = part[:, j * LANES:(j + 1) * LANES]
            used += rows
    terms[used:, :] = jnp.zeros((terms.shape[0] - used, LANES), f32)


def upper_kernel(hops, pos, dist, tab, src, near_in, *refs):
    far_in, refs = refs[:hops - 1], refs[hops - 1:]
    wo3, wi3, slope, grad, near, *refs = refs
    far, refs = refs[:hops - 1], refs[hops - 1:]
    gm3, gh3, gm, join = refs
    unpack(src, dist, tab, 1, far_in, near_in, gm, join, hops, pos)
    hidden(pos, wo3, slope, gm, gm3, gh3)
    inward(pos, wi3, gm, gh3, grad)
    pack(grad, tab, 0, far, near, hops, pos)


def terms_kernel(factor, x2, gh3, h2, gm3, terms):
    weight_terms(factor, x2, gh3, h2, gm3, terms)


def lower_kernel(hops, pos, factor, dist, tab, src, near_in, *refs):
    far_in, refs = refs[:hops - 1], refs[hops - 1:]
    wo3, slope, x2, h2, gm, gh3, terms, gm3, join = refs
    unpack(src, dist, tab, 0, far_in, near_in, gm, join, hops, pos)
    hidden(pos, wo3, slope, gm, gm3, gh3)
    weight_terms(factor, x2, gh3, h2, gm3, terms)


def input_kernel(pos, wi3, gm, gh3, out):
    inward(pos, wi3, gm, gh3, out)


def finish_kernel(sum0, sum1, w_in_grad, bias_grad, w_out_grad):
    blocks = HID // LANES
    rows = D + 8
    for layer, total in enumerate((sum0, sum1)):
        for j in range(blocks):
            lanes = slice(j * LANES, (j + 1) * LANES)
            w_in_grad[layer, :, lanes] = total[j * rows:j * rows + D, :]
            bias_grad[layer:layer + 1, lanes] = total[j * rows + D:j * rows + D + 1, :]
            start = blocks * rows + j * D
            w_out_grad[layer, lanes, :] = jnp.transpose(total[start:start + D, :], (1, 0))


def from_ahead(value, steps):
    count = lax.axis_size("seq")
    return lax.ppermute(value, "seq", [(s, (s - steps) % count) for s in range(count)])


def exchange(value, mask):
    count = lax.axis_size("seq")
    return lax.ppermute(value, "seq", [(s, s ^ mask) for s in range(count)])


def total_over_seq(x):
    index = lax.axis_index("seq")
    count = lax.axis_size("seq")
    masks = [1 << b for b in range(count.bit_length() - 1)]
    for mask in masks:
        half = x.shape[0] // 2
        bit = (index // mask) % 2
        keep = lax.dynamic_slice_in_dim(x, bit * half, half, 0)
        send = lax.dynamic_slice_in_dim(x, (1 - bit) * half, half, 0)
        x = keep + exchange(send, mask)
    for mask in masks[::-1]:
        bit = (index // mask) % 2
        other = exchange(x, mask)
        x = jnp.concatenate([jnp.where(bit == 0, x, other), jnp.where(bit == 0, other, x)], 0)
    return x


def shape(*dims, dtype=f32):
    return jax.ShapeDtypeStruct(dims, dtype)


def body(first_inputs, second_inputs, out_grad, weight_in, bias_in, weight_out, distances):
    pos = first_inputs.shape[1]
    count = lax.axis_size("seq")
    hops = count.bit_length() - 1
    factor = 1.0 / math.sqrt(pos * count)
    near_width = near_slots(pos)[1]
    saved = [first_inputs, second_inputs]
    far_shapes = [shape(MOST * TW, pos)] * (hops - 1)
    near_shape = shape(TW, near_width)
    rows = 3 * (D + 8) + 3 * D
    rows = -(-rows // (8 * count)) * 8 * count
    far_hops = [1 << k for k in range(1, hops)]

    def travel(near, far):
        moved = [from_ahead(f, h) for f, h in zip(far[::-1], far_hops[::-1])][::-1]
        return from_ahead(near, 1), moved

    tab, near, *far = pl.pallas_call(
        lambda *refs: pack_kernel(hops, pos, *refs),
        out_shape=[shape(2, 32, dtype=i32), near_shape] + far_shapes,
        in_specs=[SM, VM],
        out_specs=[SM, VM] + [VM] * (hops - 1),
        compiler_params=params(16),
        name="pack",
    )(distances, out_grad)
    near, far = travel(near, far)

    acts = []
    for layer in (1, 0):
        acts.append(pl.pallas_call(
            lambda *refs: act_kernel(pos, *refs),
            out_shape=[
                shape(2 * D + 32, pos, dtype=bf16),
                shape(2 * HID, pos, dtype=bf16),
                shape(HID, pos),
                shape(D, 3 * HID, dtype=bf16),
                shape(HID, 3 * D, dtype=bf16),
            ],
            in_specs=[VM] * 4,
            out_specs=[VM] * 5,
            scratch_shapes=[pltpu.VMEM((3 * D, 256), bf16)],
            compiler_params=params(24),
            name="act",
        )(saved[layer], weight_in[layer], bias_in[layer][:, None], weight_out[layer]))
    (x2_1, h2_1, slope_1, wi3_1, wo3_1), (x2_0, h2_0, slope_0, wi3_0, wo3_0) = acts

    grad_1, near, *rest = pl.pallas_call(
        lambda *refs: upper_kernel(hops, pos, *refs),
        out_shape=[shape(D, pos), near_shape] + far_shapes + [shape(3 * D, pos, dtype=bf16), shape(3 * HID, pos, dtype=bf16)],
        in_specs=[SM, SM] + [VM] * (hops + 4),
        out_specs=[VM] * (hops + 3),
        scratch_shapes=[pltpu.VMEM((D, pos), f32), pltpu.VMEM((TW, 2 * pos + LANES), f32)],
        compiler_params=params(32),
        name="upper",
    )(distances, tab, out_grad, near, *far, wo3_1, wi3_1, slope_1)
    far, (gm3_1, gh3_1) = rest[:hops - 1], rest[hops - 1:]
    near, far = travel(near, far)

    terms_1 = pl.pallas_call(
        lambda *refs: terms_kernel(factor, *refs),
        out_shape=shape(rows, LANES),
        in_specs=[VM] * 4,
        out_specs=VM,
        compiler_params=params(24),
        name="terms",
    )(x2_1, gh3_1, h2_1, gm3_1)
    sum_1 = total_over_seq(terms_1)

    gm_0, gh3_0, terms_0 = pl.pallas_call(
        lambda *refs: lower_kernel(hops, pos, factor, *refs),
        out_shape=[shape(D, pos), shape(3 * HID, pos, dtype=bf16), shape(rows, LANES)],
        in_specs=[SM, SM] + [VM] * (hops + 5),
        out_specs=[VM] * 3,
        scratch_shapes=[pltpu.VMEM((3 * D, pos), bf16), pltpu.VMEM((TW, 2 * pos + LANES), f32)],
        compiler_params=params(32),
        name="lower",
    )(distances, tab, grad_1, near, *far, wo3_0, slope_0, x2_0, h2_0)
    sum_0 = total_over_seq(terms_0)

    input_grad = pl.pallas_call(
        lambda *refs: input_kernel(pos, *refs),
        out_shape=shape(D, pos),
        in_specs=[VM] * 3,
        out_specs=VM,
        compiler_params=params(24),
        name="inward",
    )(wi3_0, gm_0, gh3_0)

    grads = pl.pallas_call(
        finish_kernel,
        out_shape=[shape(2, D, HID), shape(2, HID), shape(2, HID, D)],
        in_specs=[VM] * 2,
        out_specs=[VM] * 3,
        compiler_params=params(24),
        name="finish",
    )(sum_0, sum_1)
    return (input_grad, *grads)


def solution(mesh):
    whole = P(None, ("groups", "seq"))
    in_specs = (whole, whole, whole, P(), P(), P(), P())
    out_specs = (whole, P("groups", None, None), P("groups", None), P("groups", None, None))
    return jax.shard_map(body, mesh=mesh, in_specs=in_specs, out_specs=out_specs, check_vma=False)
```

```python
import math

import jax
import jax.numpy as jnp
from jax import lax
from jax.experimental import pallas as pl
from jax.experimental.pallas import tpu as pltpu
from jax.sharding import PartitionSpec as P

TRACKS = 18
TW = 16
MOST = 3
D = TRACKS * TW
HID = 384
INNER = TRACKS - MOST
LANES = 128
MIB = 1 << 20

ROOT_HALF = 0.7071067811865476
INV_ROOT_TWO_PI = 0.3989422804014327

f32, bf16, i32 = jnp.float32, jnp.bfloat16, jnp.int32
VM = pl.BlockSpec(memory_space=pltpu.VMEM)
SM = pl.BlockSpec(memory_space=pltpu.SMEM)
HB = pl.BlockSpec(memory_space=pltpu.HBM)


def kernel_options(name, mib, cost_us):
    return dict(
        name=name,
        compiler_params=pltpu.CompilerParams(vmem_limit_bytes=mib * MIB),
        cost_estimate=pl.CostEstimate(flops=int(cost_us * 1e9), bytes_accessed=int(cost_us * 3e6), transcendentals=0),
    )


def near_slots(pos):
    slots, offset = [], 0
    for slot in range(INNER):
        width = max(LANES, pos >> (slot // MOST))
        slots.append((offset, width))
        offset += width
    return slots, offset


def halves(value):
    high = value.astype(bf16)
    return high, (value - high.astype(f32)).astype(bf16)


def put_triple(ref, value, rows, cols, order):
    pair = halves(value)
    for place, which in enumerate(order):
        ref[place * rows:(place + 1) * rows, cols] = pair[which]


def fill_tables(dist, tab, layer, hops, pos):
    d = [dist[layer, t] for t in range(TRACKS)]
    key = [d[t] * 32 + (31 - t) for t in range(TRACKS)]
    rank = [jnp.int32(0)] * TRACKS
    for t in range(TRACKS):
        for u in range(t + 1, TRACKS):
            above = (key[u] > key[t]).astype(i32)
            rank[t] = rank[t] + above
            rank[u] = rank[u] + (1 - above)
    for t in range(TRACKS):
        tab[rank[t]] = jnp.int32(t)
    for k in range(hops):
        first = jnp.int32(0)
        for t in range(TRACKS):
            first = first + (d[t] > (pos << k)).astype(i32)
        tab[TRACKS + k] = first


def track_at(tab, k, slot):
    place = tab[TRACKS + k] + slot
    return place, tab[jnp.minimum(place, TRACKS - 1)]


def rows_of(track):
    return pl.ds(pl.multiple_of(track * TW, TW), TW)


class Copies:
    def __init__(self, sems):
        self.sems, self.used = sems, 0

    def start(self, src, dst):
        copy = pltpu.make_async_copy(src, dst, self.sems.at[self.used])
        self.used += 1
        copy.start()
        return copy


def pack(copies, src, tab, far, near, hops, pos):
    started = []
    for k in range(hops - 1, 0, -1):
        for slot in range(MOST):
            _, t = track_at(tab, k, slot)
            started.append(copies.start(src.at[rows_of(t), :], far[k - 1].at[slot * TW:(slot + 1) * TW, :]))
    for slot, (offset, width) in enumerate(near_slots(pos)[0]):
        _, t = track_at(tab, 0, slot)
        started.append(copies.start(src.at[rows_of(t), 0:width], near.at[:, offset:offset + width]))
    return started


def unpack(src, dist, tab, layer, far, near, out, join, hops, pos):
    for k in range(1, hops):
        for slot in range(MOST):
            place, t = track_at(tab, k, slot)

            @pl.when((place < TRACKS) & (dist[layer, t] == (pos << k)))
            def _(k=k, slot=slot, t=t):
                out[rows_of(t), :] = far[k - 1][slot * TW:(slot + 1) * TW, :]

    for slot, (offset, width) in enumerate(near_slots(pos)[0]):
        place, t = track_at(tab, 0, slot)

        @pl.when(place < TRACKS)
        def _(slot=slot, t=t, offset=offset, width=width):
            shift = dist[layer, t]
            join[slot, :, :pos] = src[rows_of(t), :]
            join[slot, :, pos:pos + width] = near[:, offset:offset + width]
            base = pl.multiple_of(shift // LANES * LANES, LANES)
            rest = shift % LANES
            window = join[slot, :, pl.ds(base, pos + LANES)]
            turned = pltpu.roll(window, jnp.where(rest == 0, 0, pos + LANES - rest), 1)
            out[rows_of(t), :] = turned[:, :pos]


def pack_kernel(hops, pos, dist, src, tab, near, *refs):
    far, sems = refs[:-1], refs[-1]
    fill_tables(dist, tab, 1, hops, pos)
    for copy in pack(Copies(sems), src, tab, far, near, hops, pos):
        copy.wait()


def act_kernel(hops, pos, dist, *refs):
    ins, tab, outs, xs = refs[:8], refs[8], refs[9:19], refs[19]
    fill_tables(dist, tab, 0, hops, pos)
    for layer in range(2):
        act(pos, *ins[4 * layer:4 * layer + 4], *outs[5 * layer:5 * layer + 5], xs)


def act(pos, x, w_in, bias, w_out_t, x2, h2, slope, wi3, wo3, xs):
    step = 256
    wt = jnp.transpose(w_in[...], (1, 0))
    wt_hi, wt_lo = halves(wt)
    wt3 = jnp.concatenate([wt_hi, wt_hi, wt_lo], axis=1)
    w_hi, w_lo = halves(w_in[...])
    wi3[...] = jnp.concatenate([w_hi, w_hi, w_lo], axis=1)
    w_hi, w_lo = halves(jnp.transpose(w_out_t[...], (1, 0)))
    wo3[...] = jnp.concatenate([w_hi, w_hi, w_lo], axis=1)
    for start in range(0, pos, step):
        cols = slice(start, start + step)
        x_hi, x_lo = halves(x[:, cols])
        x2[0:D, cols] = x_hi
        x2[D:D + 16, cols] = jnp.ones((16, step), bf16)
        x2[D + 16:2 * D + 16, cols] = x_lo
        x2[2 * D + 16:2 * D + 32, cols] = jnp.zeros((16, step), bf16)
        xs[0:D, :] = x_hi
        xs[D:2 * D, :] = x_lo
        xs[2 * D:3 * D, :] = x_hi
        pre = jnp.dot(wt3, xs[...], preferred_element_type=f32) + bias[...]
        cdf = 0.5 * (1.0 + lax.erf(pre * ROOT_HALF))
        put_triple(h2, pre * cdf, HID, cols, (0, 1))
        slope[:, cols] = cdf + pre * jnp.exp(-0.5 * pre * pre) * INV_ROOT_TWO_PI


def hidden(pos, wo3, slope, gm, gm3, gh3):
    step = 512
    for start in range(0, pos, step):
        cols = slice(start, start + step)
        put_triple(gm3, gm[:, cols], D, cols, (0, 1, 0))
        gh = jnp.dot(wo3[...], gm3[:, cols], preferred_element_type=f32) * slope[:, cols]
        put_triple(gh3, gh, HID, cols, (0, 1, 0))


def inward(pos, wi3, gm, gh3, out):
    step = 512
    for start in range(0, pos, step):
        cols = slice(start, start + step)
        out[:, cols] = gm[:, cols] + jnp.dot(wi3[...], gh3[:, cols], preferred_element_type=f32)


def weight_terms(factor, odd, x2, gh, h2, gm, keep, send):
    def nt(a, b):
        return lax.dot_general(a, b, (((1,), (1,)), ((), ())), preferred_element_type=f32)

    d1 = D + 16
    first = nt(x2[0:d1, :], gh[0:HID, :]) + nt(x2[0:d1, :], gh[HID:2 * HID, :]) + nt(x2[d1:2 * d1, :], gh[0:HID, :])
    second = nt(gm[0:D, :], h2[0:HID, :]) + nt(gm[0:D, :], h2[HID:2 * HID, :]) + nt(gm[D:2 * D, :], h2[0:HID, :])
    first, second = first[0:D + 8] * factor, second * factor

    def put(part, out):
        rows, used = part.shape[0], 0
        for j in range(HID // LANES):
            out[used:used + rows, :] = part[:, j * LANES:(j + 1) * LANES]
            used += rows
        out[used:, :] = jnp.zeros((out.shape[0] - used, LANES), f32)

    @pl.when(odd == 0)
    def _():
        put(first, keep)
        put(second, send)

    @pl.when(odd == 1)
    def _():
        put(second, keep)
        put(first, send)


def upper_kernel(hops, pos, dist, tab1, tab0, src_h, wo3_h, wi3_h, slope_h, near_in, *refs):
    far_in, refs = refs[:hops - 1], refs[hops - 1:]
    near, refs = refs[0], refs[1:]
    far, refs = refs[:hops - 1], refs[hops - 1:]
    grad_h, gm_h, gh_h, src, wo3, wi3, slope, gm3, gh3, gm, grad, join, sems = refs
    copies = Copies(sems)
    loads = [copies.start(*pair) for pair in ((src_h, src), (wo3_h, wo3), (slope_h, slope), (wi3_h, wi3))]
    loads[0].wait()
    unpack(src, dist, tab1, 1, far_in, near_in, gm, join, hops, pos)
    loads[1].wait()
    loads[2].wait()
    hidden(pos, wo3, slope, gm, gm3, gh3)
    stores = [copies.start(gm3.at[0:2 * D, :], gm_h), copies.start(gh3.at[0:2 * HID, :], gh_h)]
    loads[3].wait()
    inward(pos, wi3, gm, gh3, grad)
    stores = pack(copies, grad, tab0, far, near, hops, pos) + stores
    stores.append(copies.start(grad, grad_h))
    for copy in stores:
        copy.wait()


def terms_kernel(factor, odd, *refs):
    held_ins, (keep, send), scratch, sems = refs[:4], refs[4:6], refs[6:10], refs[10]
    copies = Copies(sems)
    for copy in [copies.start(*pair) for pair in zip(held_ins, scratch)]:
        copy.wait()
    weight_terms(factor, odd[0], *scratch, keep, send)


def lower_kernel(hops, pos, factor, odd, dist, tab0, src_h, wo3_h, slope_h, x2_h, h2_h, near_in, *refs):
    far_in, refs = refs[:hops - 1], refs[hops - 1:]
    keep, send, gm_h, gh_h, src, wo3, slope, x2, h2, gm3, gh3, gm, join, sems = refs
    copies = Copies(sems)
    loads = [copies.start(*pair) for pair in ((src_h, src), (wo3_h, wo3), (slope_h, slope), (x2_h, x2), (h2_h, h2))]
    loads[0].wait()
    unpack(src, dist, tab0, 0, far_in, near_in, gm, join, hops, pos)
    stores = [copies.start(gm, gm_h)]
    loads[1].wait()
    loads[2].wait()
    hidden(pos, wo3, slope, gm, gm3, gh3)
    stores.append(copies.start(gh3, gh_h))
    loads[3].wait()
    loads[4].wait()
    weight_terms(factor, odd[0], x2, gh3, h2, gm3, keep, send)
    for copy in stores:
        copy.wait()


def input_kernel(pos, *refs):
    held_ins, out, scratch, sems = refs[:3], refs[3], refs[4:7], refs[7]
    copies = Copies(sems)
    for copy in [copies.start(*pair) for pair in zip(held_ins, scratch)]:
        copy.wait()
    inward(pos, *scratch, out)


def finish_kernel(odd, *refs):
    sums, (w_in_grad, bias_grad, w_out_t_grad) = refs[:4], refs[4:]
    rows = D + 8

    def put(layer, first, second):
        for j in range(HID // LANES):
            lanes = slice(j * LANES, (j + 1) * LANES)
            w_in_grad[layer, :, lanes] = first[j * rows:j * rows + D, :]
            bias_grad[layer:layer + 1, lanes] = first[j * rows + D:j * rows + D + 1, :]
            w_out_t_grad[layer, :, lanes] = second[j * D:(j + 1) * D, :]

    for layer in range(2):
        mine, other = sums[2 * layer], sums[2 * layer + 1]

        @pl.when(odd[0] == 0)
        def _(layer=layer, mine=mine, other=other):
            put(layer, mine, other)

        @pl.when(odd[0] == 1)
        def _(layer=layer, mine=mine, other=other):
            put(layer, other, mine)


def from_ahead(value, steps):
    count = lax.axis_size("seq")
    return lax.ppermute(value, "seq", [(s, (s - steps) % count) for s in range(count)])


def exchange(value, mask):
    count = lax.axis_size("seq")
    return lax.ppermute(value, "seq", [(s, s ^ mask) for s in range(count)])


def fold(x, mask, send=None):
    half = x.shape[0] // 2
    bit = (lax.axis_index("seq") & mask) != 0
    low, high = x[:half], x[half:]
    return jnp.where(bit, high, low) + exchange(jnp.where(bit, low, high), mask)


def spread(x, mask):
    bit = (lax.axis_index("seq") & mask) != 0
    other = exchange(x, mask)
    return jnp.concatenate([jnp.where(bit, other, x), jnp.where(bit, x, other)], 0)


def shape(*dims, dtype=f32):
    return jax.ShapeDtypeStruct(dims, dtype)


def stay(*values):
    return [pltpu.with_memory_space_constraint(v, pltpu.HBM) for v in values]


def held(*dims, dtype=f32):
    return pltpu.HBM(dims, dtype)


def body(first_inputs, second_inputs, out_grad, weight_in, bias_in, weight_out, distances):
    pos = first_inputs.shape[1]
    count = lax.axis_size("seq")
    hops = count.bit_length() - 1
    factor = 1.0 / math.sqrt(pos * count)
    near_width = near_slots(pos)[1]
    far_shapes = [shape(MOST * TW, pos)] * (hops - 1)
    near_shape = shape(TW, near_width)
    half = -(-3 * (D + 8) // (8 * count)) * 8 * count
    masks = [1 << b for b in range(1, hops)]
    far_hops = [1 << k for k in range(1, hops)]
    odd = (lax.axis_index("seq") & 1).astype(i32).reshape(1)
    copy_sems = pltpu.SemaphoreType.DMA((MOST * hops + INNER + 16,))

    def travel(near, far):
        moved = [from_ahead(f, h) for f, h in zip(far[::-1], far_hops[::-1])][::-1]
        return from_ahead(near, 1), moved

    tab_1, near, *far = pl.pallas_call(
        lambda *refs: pack_kernel(hops, pos, *refs),
        out_shape=[shape(32, dtype=i32), near_shape] + far_shapes,
        in_specs=[SM, HB],
        out_specs=[SM] + [HB] * hops,
        scratch_shapes=[copy_sems],
        **kernel_options("pack", 4, 2),
    )(distances, *stay(out_grad))
    near, far = travel(near, far)

    w_out_t = jnp.transpose(weight_out, (0, 2, 1))
    saved = [first_inputs, second_inputs]
    act_ins = []
    for layer in range(2):
        act_ins += [saved[layer], weight_in[layer], bias_in[layer][:, None], w_out_t[layer]]
    act_shapes = [
        held(2 * D + 32, pos, dtype=bf16),
        held(2 * HID, pos, dtype=bf16),
        held(HID, pos),
        held(D, 3 * HID, dtype=bf16),
        held(HID, 3 * D, dtype=bf16),
    ]
    tab_0, *acts = pl.pallas_call(
        lambda *refs: act_kernel(hops, pos, *refs),
        out_shape=[shape(32, dtype=i32)] + act_shapes * 2,
        in_specs=[SM] + [VM] * 8,
        out_specs=[SM] + [VM] * 10,
        scratch_shapes=[pltpu.VMEM((3 * D, 256), bf16)],
        **kernel_options("act", 28, 5),
    )(distances, *act_ins)
    x2_0, h2_0, slope_0, wi3_0, wo3_0, x2_1, h2_1, slope_1, wi3_1, wo3_1 = acts

    x2_s = pltpu.VMEM((2 * D + 32, pos), bf16)
    h2_s = pltpu.VMEM((2 * HID, pos), bf16)
    slope_s = pltpu.VMEM((HID, pos), f32)
    wi3_s = pltpu.VMEM((D, 3 * HID), bf16)
    wo3_s = pltpu.VMEM((HID, 3 * D), bf16)
    gm3_s = pltpu.VMEM((3 * D, pos), bf16)
    gh3_s = pltpu.VMEM((3 * HID, pos), bf16)
    whole_s = pltpu.VMEM((D, pos), f32)
    join_s = pltpu.VMEM((INNER, TW, 2 * pos + LANES), f32)

    near, *rest = pl.pallas_call(
        lambda *refs: upper_kernel(hops, pos, *refs),
        out_shape=[near_shape] + far_shapes + [held(D, pos), held(2 * D, pos, dtype=bf16), held(2 * HID, pos, dtype=bf16)],
        in_specs=[SM] * 3 + [HB] * 4 + [VM] * hops,
        out_specs=[HB] * (hops + 3),
        scratch_shapes=[whole_s, wo3_s, wi3_s, slope_s, gm3_s, gh3_s, whole_s, whole_s, join_s, copy_sems],
        **kernel_options("upper", 24, 5),
    )(distances, tab_1, tab_0, *stay(out_grad, wo3_1, wi3_1, slope_1), near, *far)
    far, (grad_1, gm2_1, gh2_1) = rest[:hops - 1], rest[hops - 1:]
    near, far = travel(near, far)

    keep_1, send_1 = pl.pallas_call(
        lambda *refs: terms_kernel(factor, *refs),
        out_shape=[shape(half, LANES)] * 2,
        in_specs=[SM] + [HB] * 4,
        out_specs=[VM] * 2,
        scratch_shapes=[x2_s, pltpu.VMEM((2 * HID, pos), bf16), h2_s, pltpu.VMEM((2 * D, pos), bf16), copy_sems],
        **kernel_options("terms", 16, 0.001),
    )(odd, *stay(x2_1, gh2_1, h2_1, gm2_1))
    send_1, near, far = lax.optimization_barrier((send_1, near, far))
    sum_1 = keep_1 + exchange(send_1, 1)

    keep, send, gm_0, gh3_0 = pl.pallas_call(
        lambda *refs: lower_kernel(hops, pos, factor, *refs),
        out_shape=[shape(half, LANES)] * 2 + [held(D, pos), held(3 * HID, pos, dtype=bf16)],
        in_specs=[SM] * 3 + [HB] * 5 + [VM] * hops,
        out_specs=[VM] * 2 + [HB] * 2,
        scratch_shapes=[whole_s, wo3_s, slope_s, x2_s, h2_s, gm3_s, gh3_s, whole_s, join_s, copy_sems],
        **kernel_options("lower", 24, 5),
    )(odd, distances, tab_0, *stay(grad_1, wo3_0, slope_0, x2_0, h2_0), near, *far)

    sum_0 = keep + exchange(send, 1)
    sum_0, gm_0 = lax.optimization_barrier((sum_0, gm_0))

    input_grad = pl.pallas_call(
        lambda *refs: input_kernel(pos, *refs),
        out_shape=shape(D, pos),
        in_specs=[HB] * 3,
        out_specs=VM,
        scratch_shapes=[wi3_s, whole_s, gh3_s, copy_sems],
        **kernel_options("inward", 12, 3),
    )(*stay(wi3_0, gm_0, gh3_0))

    for number, mask in enumerate(masks):
        sum_1 = fold(sum_1, mask)
        if number == 1:
            sum_0, input_grad = lax.optimization_barrier((sum_0, input_grad))
        sum_0 = fold(sum_0, mask)
    for mask in masks[::-1]:
        sum_1 = spread(sum_1, mask)
        sum_0 = spread(sum_0, mask)
    other_1 = exchange(sum_1, 1)
    other_0 = exchange(sum_0, 1)

    w_in_grad, bias_grad, w_out_t_grad = pl.pallas_call(
        finish_kernel,
        out_shape=[shape(2, D, HID), shape(2, HID), shape(2, D, HID)],
        in_specs=[SM] + [VM] * 4,
        out_specs=[VM] * 3,
        **kernel_options("finish", 12, 1),
    )(odd, sum_0, other_0, sum_1, other_1)
    return input_grad, w_in_grad, bias_grad, jnp.transpose(w_out_t_grad, (0, 2, 1))


def solution(mesh):
    whole = P(None, ("groups", "seq"))
    in_specs = (whole, whole, whole, P(), P(), P(), P())
    out_specs = (whole, P("groups", None, None), P("groups", None), P("groups", None, None))
    return jax.shard_map(body, mesh=mesh, in_specs=in_specs, out_specs=out_specs, check_vma=False)
```

```python
import math

import jax
import jax.numpy as jnp
from jax import lax
from jax.experimental import pallas as pl
from jax.experimental.pallas import tpu as pltpu
from jax.sharding import PartitionSpec as P

TRACKS = 18
TW = 16
MOST = 3
D = TRACKS * TW
HID = 384
INNER = TRACKS - MOST
LANES = 128
MIB = 1 << 20

ROOT_HALF = 0.7071067811865476
INV_ROOT_TWO_PI = 0.3989422804014327

f32, bf16, i32 = jnp.float32, jnp.bfloat16, jnp.int32
VM = pl.BlockSpec(memory_space=pltpu.VMEM)
SM = pl.BlockSpec(memory_space=pltpu.SMEM)
HB = pl.BlockSpec(memory_space=pltpu.HBM)


def kernel_options(name, mib, cost_us):
    return dict(
        name=name,
        compiler_params=pltpu.CompilerParams(vmem_limit_bytes=mib * MIB),
        cost_estimate=pl.CostEstimate(flops=int(cost_us * 1e9), bytes_accessed=int(cost_us * 3e6), transcendentals=0),
    )


def near_slots(pos):
    slots, offset = [], 0
    for slot in range(INNER):
        width = max(LANES, pos >> (slot // MOST))
        slots.append((offset, width))
        offset += width
    return slots, offset


def halves(value):
    high = value.astype(bf16)
    return high, (value - high.astype(f32)).astype(bf16)


def put_triple(ref, value, rows, cols, order):
    pair = halves(value)
    for place, which in enumerate(order):
        ref[place * rows:(place + 1) * rows, cols] = pair[which]


def fill_tables(dist, tab, layer, hops, pos):
    d = [dist[layer, t] for t in range(TRACKS)]
    key = [d[t] * 32 + (31 - t) for t in range(TRACKS)]
    rank = [jnp.int32(0)] * TRACKS
    for t in range(TRACKS):
        for u in range(t + 1, TRACKS):
            above = (key[u] > key[t]).astype(i32)
            rank[t] = rank[t] + above
            rank[u] = rank[u] + (1 - above)
    for t in range(TRACKS):
        tab[rank[t]] = jnp.int32(t)
    for k in range(hops):
        first = jnp.int32(0)
        for t in range(TRACKS):
            first = first + (d[t] > (pos << k)).astype(i32)
        tab[TRACKS + k] = first


def track_at(tab, k, slot):
    place = tab[TRACKS + k] + slot
    return place, tab[jnp.minimum(place, TRACKS - 1)]


def rows_of(track):
    return pl.ds(pl.multiple_of(track * TW, TW), TW)


def pack(src, tab, far, near, hops, pos):
    for k in range(hops - 1, 0, -1):
        for slot in range(MOST):
            _, t = track_at(tab, k, slot)
            far[k - 1][slot * TW:(slot + 1) * TW, :] = src[rows_of(t), :]
    for slot, (offset, width) in enumerate(near_slots(pos)[0]):
        _, t = track_at(tab, 0, slot)
        near[:, offset:offset + width] = src[rows_of(t), 0:width]


def unpack(src, dist, tab, layer, far, near, out, join, hops, pos):
    for k in range(1, hops):
        for slot in range(MOST):
            place, t = track_at(tab, k, slot)

            @pl.when((place < TRACKS) & (dist[layer, t] == (pos << k)))
            def _(k=k, slot=slot, t=t):
                out[rows_of(t), :] = far[k - 1][slot * TW:(slot + 1) * TW, :]

    for slot, (offset, width) in enumerate(near_slots(pos)[0]):
        place, t = track_at(tab, 0, slot)

        @pl.when(place < TRACKS)
        def _(slot=slot, t=t, offset=offset, width=width):
            shift = dist[layer, t]
            join[slot, :, :pos] = src[rows_of(t), :]
            join[slot, :, pos:pos + width] = near[:, offset:offset + width]
            base = pl.multiple_of(shift // LANES * LANES, LANES)
            rest = shift % LANES
            window = join[slot, :, pl.ds(base, pos + LANES)]
            turned = pltpu.roll(window, jnp.where(rest == 0, 0, pos + LANES - rest), 1)
            out[rows_of(t), :] = turned[:, :pos]


def pack_kernel(hops, pos, dist, src_h, tab, near, *refs):
    far, (src, sem) = refs[:-2], refs[-2:]
    load = pltpu.make_async_copy(src_h, src, sem)
    load.start()
    fill_tables(dist, tab, 1, hops, pos)
    load.wait()
    pack(src, tab, far, near, hops, pos)


def act_kernel(hops, pos, dist, *refs):
    ins, tab, outs, xs = refs[:8], refs[8], refs[9:19], refs[19]
    fill_tables(dist, tab, 0, hops, pos)
    for layer in range(2):
        act(pos, *ins[4 * layer:4 * layer + 4], *outs[5 * layer:5 * layer + 5], xs)


def act(pos, x, w_in, bias, w_out_t, x2, h2, slope, wi3, wo3, xs):
    step = 256
    wt = jnp.transpose(w_in[...], (1, 0))
    wt_hi, wt_lo = halves(wt)
    wt3 = jnp.concatenate([wt_hi, wt_hi, wt_lo], axis=1)
    w_hi, w_lo = halves(w_in[...])
    wi3[...] = jnp.concatenate([w_hi, w_hi, w_lo], axis=1)
    w_hi, w_lo = halves(jnp.transpose(w_out_t[...], (1, 0)))
    wo3[...] = jnp.concatenate([w_hi, w_hi, w_lo], axis=1)
    for start in range(0, pos, step):
        cols = slice(start, start + step)
        x_hi, x_lo = halves(x[:, cols])
        x2[0:D, cols] = x_hi
        x2[D:D + 16, cols] = jnp.ones((16, step), bf16)
        x2[D + 16:2 * D + 16, cols] = x_lo
        x2[2 * D + 16:2 * D + 32, cols] = jnp.zeros((16, step), bf16)
        xs[0:D, :] = x_hi
        xs[D:2 * D, :] = x_lo
        xs[2 * D:3 * D, :] = x_hi
        pre = jnp.dot(wt3, xs[...], preferred_element_type=f32) + bias[...]
        cdf = 0.5 * (1.0 + lax.erf(pre * ROOT_HALF))
        put_triple(h2, pre * cdf, HID, cols, (0, 1))
        slope[:, cols] = cdf + pre * jnp.exp(-0.5 * pre * pre) * INV_ROOT_TWO_PI


def hidden(pos, wo3, slope, gm, gm3, gh3):
    step = 512
    for start in range(0, pos, step):
        cols = slice(start, start + step)
        put_triple(gm3, gm[:, cols], D, cols, (0, 1, 0))
        gh = jnp.dot(wo3[...], gm3[:, cols], preferred_element_type=f32) * slope[:, cols]
        put_triple(gh3, gh, HID, cols, (0, 1, 0))


def inward(pos, wi3, gm, gh3, out):
    step = 512
    for start in range(0, pos, step):
        cols = slice(start, start + step)
        out[:, cols] = gm[:, cols] + jnp.dot(wi3[...], gh3[:, cols], preferred_element_type=f32)


def weight_terms(factor, odd, x2, gh, h2, gm, keep, send):
    def nt(a, b):
        return lax.dot_general(a, b, (((1,), (1,)), ((), ())), preferred_element_type=f32)

    d1 = D + 16
    first = nt(x2[0:d1, :], gh[0:HID, :]) + nt(x2[0:d1, :], gh[HID:2 * HID, :]) + nt(x2[d1:2 * d1, :], gh[0:HID, :])
    second = nt(gm[0:D, :], h2[0:HID, :]) + nt(gm[0:D, :], h2[HID:2 * HID, :]) + nt(gm[D:2 * D, :], h2[0:HID, :])
    first, second = first[0:D + 8] * factor, second * factor

    def put(part, out):
        rows, used = part.shape[0], 0
        for j in range(HID // LANES):
            out[used:used + rows, :] = part[:, j * LANES:(j + 1) * LANES]
            used += rows
        out[used:, :] = jnp.zeros((out.shape[0] - used, LANES), f32)

    @pl.when(odd == 0)
    def _():
        put(first, keep)
        put(second, send)

    @pl.when(odd == 1)
    def _():
        put(second, keep)
        put(first, send)


def fetch(sems, refs, count):
    loads = [pltpu.make_async_copy(refs[n], refs[count + n], sems.at[n]) for n in range(count)]
    for load in loads:
        load.start()
    for load in loads:
        load.wait()
    return refs[count:2 * count]


def upper_kernel(hops, pos, dist, tab1, tab0, src, wo3, wi3, slope, near_in, *refs):
    far_in, refs = refs[:hops - 1], refs[hops - 1:]
    near, refs = refs[0], refs[1:]
    far, refs = refs[:hops - 1], refs[hops - 1:]
    grad_h, gm_h, gh_h, grad, gm3, gh3, gm, join, sems = refs
    unpack(src, dist, tab1, 1, far_in, near_in, gm, join, hops, pos)
    hidden(pos, wo3, slope, gm, gm3, gh3)
    stores = [
        pltpu.make_async_copy(gm3.at[0:2 * D, :], gm_h, sems.at[0]),
        pltpu.make_async_copy(gh3.at[0:2 * HID, :], gh_h, sems.at[1]),
        pltpu.make_async_copy(grad, grad_h, sems.at[2]),
    ]
    stores[0].start()
    stores[1].start()
    inward(pos, wi3, gm, gh3, grad)
    stores[2].start()
    pack(grad, tab0, far, near, hops, pos)
    for store in stores:
        store.wait()


def terms_kernel(factor, odd, x2_h, gh_h, h2_h, gm_h, keep, send, x2, gh, h2, gm, sems):
    fetch(sems, (x2_h, gh_h, h2_h, gm_h, x2, gh, h2, gm), 4)
    weight_terms(factor, odd[0], x2, gh, h2, gm, keep, send)


def lower_kernel(hops, pos, factor, odd, dist, tab0, wo3_h, src, slope, x2, h2, near_in, *refs):
    far_in, refs = refs[:hops - 1], refs[hops - 1:]
    keep, send, gm_h, gh_h, gm, gh3, gm3, join, wo3, sems = refs
    load = pltpu.make_async_copy(wo3_h, wo3, sems.at[2])
    load.start()
    unpack(src, dist, tab0, 0, far_in, near_in, gm, join, hops, pos)
    stores = [pltpu.make_async_copy(gm, gm_h, sems.at[0]), pltpu.make_async_copy(gh3, gh_h, sems.at[1])]
    stores[0].start()
    load.wait()
    hidden(pos, wo3, slope, gm, gm3, gh3)
    stores[1].start()
    weight_terms(factor, odd[0], x2, gh3, h2, gm3, keep, send)
    for store in stores:
        store.wait()


def input_kernel(pos, wi3_h, gm_h, gh_h, out, wi3, gm, gh3, sems):
    fetch(sems, (wi3_h, gm_h, gh_h, wi3, gm, gh3), 3)
    inward(pos, wi3, gm, gh3, out)


def finish_kernel(odd, *refs):
    sums, (w_in_grad, bias_grad, w_out_t_grad) = refs[:4], refs[4:]
    rows = D + 8

    def put(layer, first, second):
        for j in range(HID // LANES):
            lanes = slice(j * LANES, (j + 1) * LANES)
            w_in_grad[layer, :, lanes] = first[j * rows:j * rows + D, :]
            bias_grad[layer:layer + 1, lanes] = first[j * rows + D:j * rows + D + 1, :]
            w_out_t_grad[layer, :, lanes] = second[j * D:(j + 1) * D, :]

    for layer in range(2):
        mine, other = sums[2 * layer], sums[2 * layer + 1]

        @pl.when(odd[0] == 0)
        def _(layer=layer, mine=mine, other=other):
            put(layer, mine, other)

        @pl.when(odd[0] == 1)
        def _(layer=layer, mine=mine, other=other):
            put(layer, other, mine)


def from_ahead(value, steps):
    count = lax.axis_size("seq")
    return lax.ppermute(value, "seq", [(s, (s - steps) % count) for s in range(count)])


def exchange(value, mask):
    count = lax.axis_size("seq")
    return lax.ppermute(value, "seq", [(s, s ^ mask) for s in range(count)])


def fold(x, mask, send=None):
    half = x.shape[0] // 2
    bit = (lax.axis_index("seq") & mask) != 0
    low, high = x[:half], x[half:]
    return jnp.where(bit, high, low) + exchange(jnp.where(bit, low, high), mask)


def spread(x, mask):
    bit = (lax.axis_index("seq") & mask) != 0
    other = exchange(x, mask)
    return jnp.concatenate([jnp.where(bit, other, x), jnp.where(bit, x, other)], 0)


def shape(*dims, dtype=f32):
    return jax.ShapeDtypeStruct(dims, dtype)


def stay(*values, where=pltpu.VMEM):
    return [pltpu.with_memory_space_constraint(v, where) for v in values]


def stored(*dims, dtype=f32):
    return pltpu.HBM(dims, dtype)


def held(*dims, dtype=f32):
    return pltpu.VMEM(dims, dtype)


def body(first_inputs, second_inputs, out_grad, weight_in, bias_in, weight_out, distances):
    pos = first_inputs.shape[1]
    count = lax.axis_size("seq")
    hops = count.bit_length() - 1
    factor = 1.0 / math.sqrt(pos * count)
    near_width = near_slots(pos)[1]
    far_shapes = [shape(MOST * TW, pos)] * (hops - 1)
    near_shape = shape(TW, near_width)
    half = -(-3 * (D + 8) // (8 * count)) * 8 * count
    masks = [1 << b for b in range(1, hops)]
    far_hops = [1 << k for k in range(1, hops)]
    odd = (lax.axis_index("seq") & 1).astype(i32).reshape(1)

    def travel(near, far):
        moved = [from_ahead(f, h) for f, h in zip(far[::-1], far_hops[::-1])][::-1]
        return from_ahead(near, 1), moved

    whole_s = pltpu.VMEM((D, pos), f32)
    gm3_s = pltpu.VMEM((3 * D, pos), bf16)
    join_s = pltpu.VMEM((INNER, TW, 2 * pos + LANES), f32)
    distances, out_grad_h = [pltpu.with_memory_space_constraint(v, pltpu.HBM) for v in (distances, out_grad)]
    tab_1, near, *far = pl.pallas_call(
        lambda *refs: pack_kernel(hops, pos, *refs),
        out_shape=[shape(32, dtype=i32), near_shape] + far_shapes,
        in_specs=[SM, HB],
        out_specs=[SM] + [VM] * hops,
        scratch_shapes=[whole_s, pltpu.SemaphoreType.DMA],
        **kernel_options("pack", 3, 2),
    )(distances, out_grad_h)
    near, far = travel(near, far)

    w_out_t = jnp.transpose(weight_out, (0, 2, 1))
    saved = [first_inputs, second_inputs]
    act_ins = []
    for layer in range(2):
        act_ins += [saved[layer], weight_in[layer], bias_in[layer][:, None], w_out_t[layer]]
    def act_shapes(of):
        return [
            stored(2 * D + 32, pos, dtype=bf16),
            stored(2 * HID, pos, dtype=bf16),
            of(HID, pos),
            of(D, 3 * HID, dtype=bf16),
            of(HID, 3 * D, dtype=bf16),
        ]

    tab_0, *acts = pl.pallas_call(
        lambda *refs: act_kernel(hops, pos, *refs),
        out_shape=[shape(32, dtype=i32)] + act_shapes(stored) + act_shapes(held),
        in_specs=[SM] + [VM] * 8,
        out_specs=[SM] + [VM] * 10,
        scratch_shapes=[pltpu.VMEM((3 * D, 256), bf16)],
        **kernel_options("act", 24, 5),
    )(distances, *act_ins)
    x2_0, h2_0, slope_0, wi3_0, wo3_0, x2_1, h2_1, slope_1, wi3_1, wo3_1 = acts

    x2_s = pltpu.VMEM((2 * D + 32, pos), bf16)
    h2_s = pltpu.VMEM((2 * HID, pos), bf16)
    gm2_s = pltpu.VMEM((2 * D, pos), bf16)
    gh3_s = pltpu.VMEM((3 * HID, pos), bf16)
    sems_s = pltpu.SemaphoreType.DMA((4,))
    near, *rest = pl.pallas_call(
        lambda *refs: upper_kernel(hops, pos, *refs),
        out_shape=[near_shape] + far_shapes + [stored(D, pos), stored(2 * D, pos, dtype=bf16), stored(2 * HID, pos, dtype=bf16)],
        in_specs=[SM] * 3 + [VM] * (hops + 4),
        out_specs=[VM] * hops + [HB] * 3,
        scratch_shapes=[whole_s, gm3_s, gh3_s, whole_s, join_s, sems_s],
        **kernel_options("upper", 14, 5),
    )(distances, tab_1, tab_0, out_grad, *stay(wo3_1, wi3_1, slope_1), near, *far)
    far, (grad_1, gm2_1, gh2_1) = rest[:hops - 1], rest[hops - 1:]
    near, far = travel(near, far)

    keep_1, send_1 = pl.pallas_call(
        lambda *refs: terms_kernel(factor, *refs),
        out_shape=[shape(half, LANES)] * 2,
        in_specs=[SM] + [HB] * 4,
        out_specs=[VM] * 2,
        scratch_shapes=[x2_s, h2_s, h2_s, gm2_s, sems_s],
        **kernel_options("terms", 14, 0.001),
    )(odd, *stay(x2_1, gh2_1, h2_1, gm2_1, where=pltpu.HBM))
    send_1, near, far = lax.optimization_barrier((send_1, near, far))
    sum_1 = keep_1 + exchange(send_1, 1)

    keep, send, gm_0, gh3_0 = pl.pallas_call(
        lambda *refs: lower_kernel(hops, pos, factor, *refs),
        out_shape=[shape(half, LANES)] * 2 + [stored(D, pos), stored(3 * HID, pos, dtype=bf16)],
        in_specs=[SM] * 3 + [HB] + [VM] * (hops + 4),
        out_specs=[VM] * 2 + [HB] * 2,
        scratch_shapes=[whole_s, gh3_s, gm3_s, join_s, pltpu.VMEM((HID, 3 * D), bf16), sems_s],
        **kernel_options("lower", 16, 5),
    )(odd, distances, tab_0, *stay(wo3_0, where=pltpu.HBM), grad_1, slope_0, x2_0, h2_0, near, *far)
    sum_0 = keep + exchange(send, 1)
    sum_0, gm_0 = lax.optimization_barrier((sum_0, gm_0))

    input_grad = pl.pallas_call(
        lambda *refs: input_kernel(pos, *refs),
        out_shape=shape(D, pos),
        in_specs=[HB] * 3,
        out_specs=VM,
        scratch_shapes=[pltpu.VMEM((D, 3 * HID), bf16), whole_s, gh3_s, sems_s],
        **kernel_options("inward", 12, 3),
    )(*stay(wi3_0, gm_0, gh3_0, where=pltpu.HBM))
    for number, mask in enumerate(masks):
        sum_1 = fold(sum_1, mask)
        if number == 1:
            sum_0, input_grad = lax.optimization_barrier((sum_0, input_grad))
        sum_0 = fold(sum_0, mask)
    for mask in masks[::-1]:
        sum_1 = spread(sum_1, mask)
        sum_0 = spread(sum_0, mask)
    other_1 = exchange(sum_1, 1)
    other_0 = exchange(sum_0, 1)

    w_in_grad, bias_grad, w_out_t_grad = pl.pallas_call(
        finish_kernel,
        out_shape=[shape(2, D, HID), shape(2, HID), shape(2, D, HID)],
        in_specs=[SM] + [VM] * 4,
        out_specs=[VM] * 3,
        **kernel_options("finish", 4, 1),
    )(odd, sum_0, other_0, sum_1, other_1)
    return input_grad, w_in_grad, bias_grad, jnp.transpose(w_out_t_grad, (0, 2, 1))


def solution(mesh):
    whole = P(None, ("groups", "seq"))
    in_specs = (whole, whole, whole, P(), P(), P(), P())
    out_specs = (whole, P("groups", None, None), P("groups", None), P("groups", None, None))
    return jax.shard_map(body, mesh=mesh, in_specs=in_specs, out_specs=out_specs, check_vma=False)
```

```python
import math

import jax
import jax.numpy as jnp
from jax import lax
from jax.experimental import pallas as pl
from jax.experimental.pallas import tpu as pltpu
from jax.sharding import PartitionSpec as P

TRACKS = 18
TW = 16
MOST = 3
D = TRACKS * TW
HID = 384
INNER = TRACKS - MOST
LANES = 128
MIB = 1 << 20

ROOT_HALF = 0.7071067811865476
INV_ROOT_TWO_PI = 0.3989422804014327

f32, bf16, i32 = jnp.float32, jnp.bfloat16, jnp.int32
VM = pl.BlockSpec(memory_space=pltpu.VMEM)
SM = pl.BlockSpec(memory_space=pltpu.SMEM)
HB = pl.BlockSpec(memory_space=pltpu.HBM)


def kernel_options(name, mib, cost_us):
    return dict(
        name=name,
        compiler_params=pltpu.CompilerParams(vmem_limit_bytes=mib * MIB),
        cost_estimate=pl.CostEstimate(flops=int(cost_us * 1e9), bytes_accessed=int(cost_us * 3e6), transcendentals=0),
    )


def near_slots(pos):
    slots, offset = [], 0
    for slot in range(INNER):
        width = max(LANES, pos >> (slot // MOST))
        slots.append((offset, width))
        offset += width
    return slots, offset


def halves(value):
    high = value.astype(bf16)
    return high, (value - high.astype(f32)).astype(bf16)


def put_triple(ref, value, rows, cols, order):
    pair = halves(value)
    for place, which in enumerate(order):
        ref[place * rows:(place + 1) * rows, cols] = pair[which]


def fill_tables(dist, tab, layer, hops, pos):
    d = [dist[layer, t] for t in range(TRACKS)]
    key = [d[t] * 32 + (31 - t) for t in range(TRACKS)]
    rank = [jnp.int32(0)] * TRACKS
    for t in range(TRACKS):
        for u in range(t + 1, TRACKS):
            above = (key[u] > key[t]).astype(i32)
            rank[t] = rank[t] + above
            rank[u] = rank[u] + (1 - above)
    for t in range(TRACKS):
        tab[rank[t]] = jnp.int32(t)
    for k in range(hops):
        first = jnp.int32(0)
        for t in range(TRACKS):
            first = first + (d[t] > (pos << k)).astype(i32)
        tab[TRACKS + k] = first


def track_at(tab, k, slot):
    place = tab[TRACKS + k] + slot
    return place, tab[jnp.minimum(place, TRACKS - 1)]


def rows_of(track):
    return pl.ds(pl.multiple_of(track * TW, TW), TW)


def pack(src, tab, far, near, hops, pos):
    for k in range(hops - 1, 0, -1):
        for slot in range(MOST):
            _, t = track_at(tab, k, slot)
            far[k - 1][slot * TW:(slot + 1) * TW, :] = src[rows_of(t), :]
    for slot, (offset, width) in enumerate(near_slots(pos)[0]):
        _, t = track_at(tab, 0, slot)
        near[:, offset:offset + width] = src[rows_of(t), 0:width]


def unpack_far(dist, tab, layer, far, out, hops, pos):
    for k in range(1, hops):
        for slot in range(MOST):
            place, t = track_at(tab, k, slot)

            @pl.when((place < TRACKS) & (dist[layer, t] == (pos << k)))
            def _(k=k, slot=slot, t=t):
                out[rows_of(t), :] = far[k - 1][slot * TW:(slot + 1) * TW, :]


def unpack_near(src, dist, tab, layer, near, out, join, pos):
    for slot, (offset, width) in enumerate(near_slots(pos)[0]):
        place, t = track_at(tab, 0, slot)

        @pl.when(place < TRACKS)
        def _(slot=slot, t=t, offset=offset, width=width):
            shift = dist[layer, t]
            join[slot % 4, :, :pos] = src[rows_of(t), :]
            join[slot % 4, :, pos:pos + width] = near[:, offset:offset + width]
            base = pl.multiple_of(shift // LANES * LANES, LANES)
            rest = shift % LANES
            window = join[slot % 4, :, pl.ds(base, pos + LANES)]
            turned = pltpu.roll(window, jnp.where(rest == 0, 0, pos + LANES - rest), 1)
            out[rows_of(t), :] = turned[:, :pos]


def pack_kernel(hops, pos, dist, src_h, tab, near, *refs):
    far, (src, sem) = refs[:-2], refs[-2:]
    load = pltpu.make_async_copy(src_h, src, sem)
    load.start()
    fill_tables(dist, tab, 1, hops, pos)
    load.wait()
    pack(src, tab, far, near, hops, pos)


def act_kernel(hops, pos, dist, *refs):
    ins, tab, outs, xs = refs[:8], refs[8], refs[9:19], refs[19]
    fill_tables(dist, tab, 0, hops, pos)
    for layer in range(2):
        act(pos, *ins[4 * layer:4 * layer + 4], *outs[5 * layer:5 * layer + 5], xs)


def act(pos, x, w_in, bias, w_out_t, x2, h2, slope, wi3, wo3, xs):
    step = 256
    wt = jnp.transpose(w_in[...], (1, 0))
    wt_hi, wt_lo = halves(wt)
    wt3 = jnp.concatenate([wt_hi, wt_hi, wt_lo], axis=1)
    w_hi, w_lo = halves(w_in[...])
    wi3[...] = jnp.concatenate([w_hi, w_hi, w_lo], axis=1)
    w_hi, w_lo = halves(jnp.transpose(w_out_t[...], (1, 0)))
    wo3[...] = jnp.concatenate([w_hi, w_hi, w_lo], axis=1)
    for start in range(0, pos, step):
        cols = slice(start, start + step)
        x_hi, x_lo = halves(x[:, cols])
        x2[0:D, cols] = x_hi
        x2[D:D + 16, cols] = jnp.ones((16, step), bf16)
        x2[D + 16:2 * D + 16, cols] = x_lo
        x2[2 * D + 16:2 * D + 32, cols] = jnp.zeros((16, step), bf16)
        xs[0:D, :] = x_hi
        xs[D:2 * D, :] = x_lo
        xs[2 * D:3 * D, :] = x_hi
        pre = jnp.dot(wt3, xs[...], preferred_element_type=f32) + bias[...]
        cdf = 0.5 * (1.0 + lax.erf(pre * ROOT_HALF))
        put_triple(h2, pre * cdf, HID, cols, (0, 1))
        slope[:, cols] = cdf + pre * jnp.exp(-0.5 * pre * pre) * INV_ROOT_TWO_PI


def hidden(pos, wo3, slope, gm, gm3, gh3):
    step = 512
    for start in range(0, pos, step):
        cols = slice(start, start + step)
        put_triple(gm3, gm[:, cols], D, cols, (0, 1, 0))
        gh = jnp.dot(wo3[...], gm3[:, cols], preferred_element_type=f32) * slope[:, cols]
        put_triple(gh3, gh, HID, cols, (0, 1, 0))


def inward(pos, wi3, gm, gh3, out):
    step = 512
    for start in range(0, pos, step):
        cols = slice(start, start + step)
        out[:, cols] = gm[:, cols] + jnp.dot(wi3[...], gh3[:, cols], preferred_element_type=f32)


def weight_terms(factor, odd, x2, gh, h2, gm, keep, send):
    def nt(a, b):
        return lax.dot_general(a, b, (((1,), (1,)), ((), ())), preferred_element_type=f32)

    d1 = D + 16
    first = nt(x2[0:d1, :], gh[0:HID, :]) + nt(x2[0:d1, :], gh[HID:2 * HID, :]) + nt(x2[d1:2 * d1, :], gh[0:HID, :])
    second = nt(gm[0:D, :], h2[0:HID, :]) + nt(gm[0:D, :], h2[HID:2 * HID, :]) + nt(gm[D:2 * D, :], h2[0:HID, :])
    first, second = first[0:D + 8] * factor, second * factor

    def put(part, out):
        rows, used = part.shape[0], 0
        for j in range(HID // LANES):
            out[used:used + rows, :] = part[:, j * LANES:(j + 1) * LANES]
            used += rows
        out[used:, :] = jnp.zeros((out.shape[0] - used, LANES), f32)

    @pl.when(odd == 0)
    def _():
        put(first, keep)
        put(second, send)

    @pl.when(odd == 1)
    def _():
        put(second, keep)
        put(first, send)


def start_loads(sems, sources, targets):
    loads = [pltpu.make_async_copy(src, dst, sems.at[n]) for n, (src, dst) in enumerate(zip(sources, targets))]
    for load in loads:
        load.start()
    return loads


def upper_kernel(hops, pos, factor, odd, dist, tab1, tab0, src_h, wo3_h, slope_h, wi3_h, x2_h, h2_h, near_in, *refs):
    far_in, refs = refs[:hops - 1], refs[hops - 1:]
    near, refs = refs[0], refs[1:]
    far, refs = refs[:hops - 1], refs[hops - 1:]
    keep, send, grad_h, src, grad, wo3, slope, wi3, x2, h2, gm3, gh3, gm, join, sems = refs
    first, *loads = start_loads(sems, (src_h, wo3_h, slope_h, wi3_h, x2_h, h2_h), (src, wo3, slope, wi3, x2, h2))
    unpack_far(dist, tab1, 1, far_in, gm, hops, pos)
    first.wait()
    unpack_near(src, dist, tab1, 1, near_in, gm, join, pos)
    loads[0].wait()
    loads[1].wait()
    hidden(pos, wo3, slope, gm, gm3, gh3)
    loads[2].wait()
    inward(pos, wi3, gm, gh3, grad)
    store = pltpu.make_async_copy(grad, grad_h, sems.at[6])
    store.start()
    pack(grad, tab0, far, near, hops, pos)
    loads[3].wait()
    loads[4].wait()
    weight_terms(factor, odd[0], x2, gh3, h2, gm3, keep, send)
    store.wait()


def lower_kernel(hops, pos, factor, odd, dist, tab0, src_h, wo3_h, slope_h, x2_h, h2_h, near_in, *refs):
    far_in, refs = refs[:hops - 1], refs[hops - 1:]
    keep, send, gm_h, gh_h, src, gm, gh3, wo3, slope, x2, h2, gm3, join, sems = refs
    first, *loads = start_loads(sems, (src_h, wo3_h, slope_h, x2_h, h2_h), (src, wo3, slope, x2, h2))
    unpack_far(dist, tab0, 0, far_in, gm, hops, pos)
    first.wait()
    unpack_near(src, dist, tab0, 0, near_in, gm, join, pos)
    stores = [pltpu.make_async_copy(gm, gm_h, sems.at[5]), pltpu.make_async_copy(gh3, gh_h, sems.at[6])]
    stores[0].start()
    loads[0].wait()
    loads[1].wait()
    hidden(pos, wo3, slope, gm, gm3, gh3)
    stores[1].start()
    loads[2].wait()
    loads[3].wait()
    weight_terms(factor, odd[0], x2, gh3, h2, gm3, keep, send)
    for store in stores:
        store.wait()


def input_kernel(pos, wi3_h, gm_h, gh_h, out, wi3, gm, gh3, sems):
    for load in start_loads(sems, (wi3_h, gm_h, gh_h), (wi3, gm, gh3)):
        load.wait()
    inward(pos, wi3, gm, gh3, out)


def finish_kernel(odd, *refs):
    sums, (w_in_grad, bias_grad, w_out_t_grad) = refs[:4], refs[4:]
    rows = D + 8

    def put(layer, first, second):
        for j in range(HID // LANES):
            lanes = slice(j * LANES, (j + 1) * LANES)
            w_in_grad[layer, :, lanes] = first[j * rows:j * rows + D, :]
            bias_grad[layer:layer + 1, lanes] = first[j * rows + D:j * rows + D + 1, :]
            w_out_t_grad[layer, :, lanes] = second[j * D:(j + 1) * D, :]

    for layer in range(2):
        mine, other = sums[2 * layer], sums[2 * layer + 1]

        @pl.when(odd[0] == 0)
        def _(layer=layer, mine=mine, other=other):
            put(layer, mine, other)

        @pl.when(odd[0] == 1)
        def _(layer=layer, mine=mine, other=other):
            put(layer, other, mine)


def from_ahead(value, steps):
    count = lax.axis_size("seq")
    return lax.ppermute(value, "seq", [(s, (s - steps) % count) for s in range(count)])


def exchange(value, mask):
    count = lax.axis_size("seq")
    return lax.ppermute(value, "seq", [(s, s ^ mask) for s in range(count)])


def fold(x, mask, send=None):
    half = x.shape[0] // 2
    bit = (lax.axis_index("seq") & mask) != 0
    low, high = x[:half], x[half:]
    return jnp.where(bit, high, low) + exchange(jnp.where(bit, low, high), mask)


def spread(x, mask):
    bit = (lax.axis_index("seq") & mask) != 0
    other = exchange(x, mask)
    return jnp.concatenate([jnp.where(bit, other, x), jnp.where(bit, x, other)], 0)


def shape(*dims, dtype=f32):
    return jax.ShapeDtypeStruct(dims, dtype)


def stay(*values, where=pltpu.VMEM):
    return [pltpu.with_memory_space_constraint(v, where) for v in values]


def stored(*dims, dtype=f32):
    return pltpu.HBM(dims, dtype)


def held(*dims, dtype=f32):
    return pltpu.VMEM(dims, dtype)


def body(first_inputs, second_inputs, out_grad, weight_in, bias_in, weight_out, distances):
    pos = first_inputs.shape[1]
    count = lax.axis_size("seq")
    hops = count.bit_length() - 1
    factor = 1.0 / math.sqrt(pos * count)
    near_width = near_slots(pos)[1]
    far_shapes = [shape(MOST * TW, pos)] * (hops - 1)
    near_shape = shape(TW, near_width)
    half = -(-3 * (D + 8) // (8 * count)) * 8 * count
    masks = [1 << b for b in range(1, hops)]
    far_hops = [1 << k for k in range(1, hops)]
    odd = (lax.axis_index("seq") & 1).astype(i32).reshape(1)

    def travel(near, far):
        moved = [from_ahead(f, h) for f, h in zip(far[::-1], far_hops[::-1])][::-1]
        return from_ahead(near, 1), moved

    whole_s = pltpu.VMEM((D, pos), f32)
    gm3_s = pltpu.VMEM((3 * D, pos), bf16)
    join_s = pltpu.VMEM((4, TW, 2 * pos + LANES), f32)
    distances, out_grad_h = [pltpu.with_memory_space_constraint(v, pltpu.HBM) for v in (distances, out_grad)]
    tab_1, near, *far = pl.pallas_call(
        lambda *refs: pack_kernel(hops, pos, *refs),
        out_shape=[shape(32, dtype=i32), near_shape] + far_shapes,
        in_specs=[SM, HB],
        out_specs=[SM] + [VM] * hops,
        scratch_shapes=[whole_s, pltpu.SemaphoreType.DMA],
        **kernel_options("pack", 3, 2),
    )(distances, out_grad_h)
    near, far = travel(near, far)

    w_out_t = jnp.transpose(weight_out, (0, 2, 1))
    saved = [first_inputs, second_inputs]
    act_ins = []
    for layer in range(2):
        act_ins += [saved[layer], weight_in[layer], bias_in[layer][:, None], w_out_t[layer]]
    act_shapes = [
        stored(2 * D + 32, pos, dtype=bf16),
        stored(2 * HID, pos, dtype=bf16),
        stored(HID, pos),
        stored(D, 3 * HID, dtype=bf16),
        stored(HID, 3 * D, dtype=bf16),
    ]
    tab_0, *acts = pl.pallas_call(
        lambda *refs: act_kernel(hops, pos, *refs),
        out_shape=[shape(32, dtype=i32)] + act_shapes * 2,
        in_specs=[SM] + [VM] * 8,
        out_specs=[SM] + [VM] * 10,
        scratch_shapes=[pltpu.VMEM((3 * D, 256), bf16)],
        **kernel_options("act", 24, 5),
    )(distances, *act_ins)
    x2_0, h2_0, slope_0, wi3_0, wo3_0, x2_1, h2_1, slope_1, wi3_1, wo3_1 = acts

    gh3_s = pltpu.VMEM((3 * HID, pos), bf16)
    x2_s = pltpu.VMEM((2 * D + 32, pos), bf16)
    h2_s = pltpu.VMEM((2 * HID, pos), bf16)
    slope_s = pltpu.VMEM((HID, pos), f32)
    wi3_s = pltpu.VMEM((D, 3 * HID), bf16)
    wo3_s = pltpu.VMEM((HID, 3 * D), bf16)
    sems_s = pltpu.SemaphoreType.DMA((7,))
    near, *rest = pl.pallas_call(
        lambda *refs: upper_kernel(hops, pos, factor, *refs),
        out_shape=[near_shape] + far_shapes + [shape(half, LANES)] * 2 + [stored(D, pos)],
        in_specs=[SM] * 4 + [HB] * 6 + [VM] * hops,
        out_specs=[VM] * (hops + 2) + [HB],
        scratch_shapes=[whole_s, whole_s, wo3_s, slope_s, wi3_s, x2_s, h2_s, gm3_s, gh3_s, whole_s, join_s, sems_s],
        **kernel_options("upper", 16, 6),
    )(odd, distances, tab_1, tab_0, *stay(out_grad, wo3_1, slope_1, wi3_1, x2_1, h2_1, where=pltpu.HBM), near, *far)
    far, (keep_1, send_1, grad_1) = rest[:hops - 1], rest[hops - 1:]
    near, far = travel(near, far)

    sum_1 = keep_1 + exchange(send_1, 1)
    sum_1, near, far = lax.optimization_barrier((sum_1, near, far))
    sum_1 = fold(sum_1, masks[0])

    keep, send, gm_0, gh3_0 = pl.pallas_call(
        lambda *refs: lower_kernel(hops, pos, factor, *refs),
        out_shape=[shape(half, LANES)] * 2 + [stored(D, pos), stored(3 * HID, pos, dtype=bf16)],
        in_specs=[SM] * 3 + [HB] * 5 + [VM] * hops,
        out_specs=[VM] * 2 + [HB] * 2,
        scratch_shapes=[whole_s, whole_s, gh3_s, wo3_s, slope_s, x2_s, h2_s, gm3_s, join_s, sems_s],
        **kernel_options("lower", 16, 5),
    )(odd, distances, tab_0, *stay(grad_1, wo3_0, slope_0, x2_0, h2_0, where=pltpu.HBM), near, *far)
    sum_1, send = lax.optimization_barrier((sum_1, send))
    sum_0 = keep + exchange(send, 1)
    sum_0, gm_0 = lax.optimization_barrier((sum_0, gm_0))

    input_grad = pl.pallas_call(
        lambda *refs: input_kernel(pos, *refs),
        out_shape=shape(D, pos),
        in_specs=[HB] * 3,
        out_specs=VM,
        scratch_shapes=[pltpu.VMEM((D, 3 * HID), bf16), whole_s, gh3_s, sems_s],
        **kernel_options("inward", 12, 3),
    )(*stay(wi3_0, gm_0, gh3_0, where=pltpu.HBM))
    for number, mask in enumerate(masks):
        if number == 1:
            sum_0, input_grad = lax.optimization_barrier((sum_0, input_grad))
        if number > 0:
            sum_1 = fold(sum_1, mask)
            sum_1, _ = lax.optimization_barrier((sum_1, early))
        early, sum_0 = sum_0, fold(sum_0, mask)
    for mask in masks[::-1]:
        sum_1 = spread(sum_1, mask)
        sum_0 = spread(sum_0, mask)
    other_1 = exchange(sum_1, 1)
    other_0 = exchange(sum_0, 1)

    w_in_grad, bias_grad, w_out_t_grad = pl.pallas_call(
        finish_kernel,
        out_shape=[shape(2, D, HID), shape(2, HID), shape(2, D, HID)],
        in_specs=[SM] + [VM] * 4,
        out_specs=[VM] * 3,
        **kernel_options("finish", 4, 1),
    )(odd, sum_0, other_0, sum_1, other_1)
    return input_grad, w_in_grad, bias_grad, jnp.transpose(w_out_t_grad, (0, 2, 1))


def solution(mesh):
    whole = P(None, ("groups", "seq"))
    in_specs = (whole, whole, whole, P(), P(), P(), P())
    out_specs = (whole, P("groups", None, None), P("groups", None), P("groups", None, None))
    return jax.shard_map(body, mesh=mesh, in_specs=in_specs, out_specs=out_specs, check_vma=False)
```

```python
import math

import jax
import jax.numpy as jnp
from jax import lax
from jax.experimental import pallas as pl
from jax.experimental.pallas import tpu as pltpu
from jax.sharding import PartitionSpec as P

TRACKS = 18
TW = 16
MOST = 3
D = TRACKS * TW
HID = 384
INNER = TRACKS - MOST
LANES = 128
MIB = 1 << 20

ROOT_HALF = 0.7071067811865476
INV_ROOT_TWO_PI = 0.3989422804014327

f32, bf16, i32 = jnp.float32, jnp.bfloat16, jnp.int32
VM = pl.BlockSpec(memory_space=pltpu.VMEM)
SM = pl.BlockSpec(memory_space=pltpu.SMEM)
HB = pl.BlockSpec(memory_space=pltpu.HBM)


def kernel_options(name, mib, cost_us):
    return dict(
        name=name,
        compiler_params=pltpu.CompilerParams(vmem_limit_bytes=mib * MIB),
        cost_estimate=pl.CostEstimate(flops=int(cost_us * 1e9), bytes_accessed=int(cost_us * 3e6), transcendentals=0),
    )


def near_slots(pos):
    slots, offset = [], 0
    for slot in range(INNER):
        width = max(LANES, pos >> (slot // MOST))
        slots.append((offset, width))
        offset += width
    return slots, offset


def halves(value):
    high = value.astype(bf16)
    return high, (value - high.astype(f32)).astype(bf16)


def put_triple(ref, value, rows, cols, order):
    pair = halves(value)
    for place, which in enumerate(order):
        ref[place * rows:(place + 1) * rows, cols] = pair[which]


def fill_tables(dist, tab, layer, hops, pos):
    d = [dist[layer, t] for t in range(TRACKS)]
    key = [d[t] * 32 + (31 - t) for t in range(TRACKS)]
    rank = [jnp.int32(0)] * TRACKS
    for t in range(TRACKS):
        for u in range(t + 1, TRACKS):
            above = (key[u] > key[t]).astype(i32)
            rank[t] = rank[t] + above
            rank[u] = rank[u] + (1 - above)
    for t in range(TRACKS):
        tab[rank[t]] = jnp.int32(t)
    for k in range(hops):
        first = jnp.int32(0)
        for t in range(TRACKS):
            first = first + (d[t] > (pos << k)).astype(i32)
        tab[TRACKS + k] = first


def track_at(tab, k, slot):
    place = tab[TRACKS + k] + slot
    return place, tab[jnp.minimum(place, TRACKS - 1)]


def rows_of(track):
    return pl.ds(pl.multiple_of(track * TW, TW), TW)


def pack(src, tab, far, near, hops, pos):
    for k in range(hops - 1, 0, -1):
        for slot in range(MOST):
            _, t = track_at(tab, k, slot)
            far[k - 1][slot * TW:(slot + 1) * TW, :] = src[rows_of(t), :]
    for slot, (offset, width) in enumerate(near_slots(pos)[0]):
        _, t = track_at(tab, 0, slot)
        near[:, offset:offset + width] = src[rows_of(t), 0:width]


def unpack_far(where, dist, tab, layer, far, out, hops, pos):
    for k in range(1, hops):
        for slot in range(MOST):
            place, t = track_at(tab, k, slot)
            mine = (place < TRACKS) & (dist[layer, t] == (pos << k))
            sources = [(far[0], where[1] == 0), (far[1], where[1] == 1)] if k == 1 else [(far[k], True)]
            for source, here in sources:
                @pl.when(mine & here)
                def _(source=source, slot=slot, t=t):
                    out[rows_of(t), :] = source[slot * TW:(slot + 1) * TW, :]


def unpack_near(src, dist, tab, layer, near, out, join, pos):
    for slot, (offset, width) in enumerate(near_slots(pos)[0]):
        place, t = track_at(tab, 0, slot)

        @pl.when(place < TRACKS)
        def _(slot=slot, t=t, offset=offset, width=width):
            shift = dist[layer, t]
            join[slot % 4, :, :pos] = src[rows_of(t), :]
            join[slot % 4, :, pos:pos + width] = near[:, offset:offset + width]
            base = pl.multiple_of(shift // LANES * LANES, LANES)
            rest = shift % LANES
            window = join[slot % 4, :, pl.ds(base, pos + LANES)]
            turned = pltpu.roll(window, jnp.where(rest == 0, 0, pos + LANES - rest), 1)
            out[rows_of(t), :] = turned[:, :pos]


def pack_kernel(hops, pos, dist, src_h, tab, near, *refs):
    far, (src, sem) = refs[:-2], refs[-2:]
    load = pltpu.make_async_copy(src_h, src, sem)
    load.start()
    fill_tables(dist, tab, 1, hops, pos)
    load.wait()
    pack(src, tab, far, near, hops, pos)


def act_kernel(hops, pos, dist, *refs):
    ins, tab, outs, xs = refs[:8], refs[8], refs[9:19], refs[19]
    fill_tables(dist, tab, 0, hops, pos)
    for layer in range(2):
        act(pos, *ins[4 * layer:4 * layer + 4], *outs[5 * layer:5 * layer + 5], xs)


def act(pos, x, w_in, bias, w_out_t, x2, h2, slope, wi3, wo3, xs):
    step = 256
    wt = jnp.transpose(w_in[...], (1, 0))
    wt_hi, wt_lo = halves(wt)
    wt3 = jnp.concatenate([wt_hi, wt_hi, wt_lo], axis=1)
    w_hi, w_lo = halves(w_in[...])
    wi3[...] = jnp.concatenate([w_hi, w_hi, w_lo], axis=1)
    w_hi, w_lo = halves(jnp.transpose(w_out_t[...], (1, 0)))
    wo3[...] = jnp.concatenate([w_hi, w_hi, w_lo], axis=1)
    for start in range(0, pos, step):
        cols = slice(start, start + step)
        x_hi, x_lo = halves(x[:, cols])
        x2[0:D, cols] = x_hi
        x2[D:D + 16, cols] = jnp.ones((16, step), bf16)
        x2[D + 16:2 * D + 16, cols] = x_lo
        x2[2 * D + 16:2 * D + 32, cols] = jnp.zeros((16, step), bf16)
        xs[0:D, :] = x_hi
        xs[D:2 * D, :] = x_lo
        xs[2 * D:3 * D, :] = x_hi
        pre = jnp.dot(wt3, xs[...], preferred_element_type=f32) + bias[...]
        cdf = 0.5 * (1.0 + lax.erf(pre * ROOT_HALF))
        put_triple(h2, pre * cdf, HID, cols, (0, 1))
        slope[:, cols] = cdf + pre * jnp.exp(-0.5 * pre * pre) * INV_ROOT_TWO_PI


def hidden(pos, wo3, slope, gm, gm3, gh3):
    step = 512
    for start in range(0, pos, step):
        cols = slice(start, start + step)
        put_triple(gm3, gm[:, cols], D, cols, (0, 1, 0))
        gh = jnp.dot(wo3[...], gm3[:, cols], preferred_element_type=f32) * slope[:, cols]
        put_triple(gh3, gh, HID, cols, (0, 1, 0))


def inward(pos, wi3, gm, gh3, out):
    step = 512
    for start in range(0, pos, step):
        cols = slice(start, start + step)
        out[:, cols] = gm[:, cols] + jnp.dot(wi3[...], gh3[:, cols], preferred_element_type=f32)


def weight_terms(factor, odd, x2, gh, h2, gm, keep, send):
    def nt(a, b):
        return lax.dot_general(a, b, (((1,), (1,)), ((), ())), preferred_element_type=f32)

    d1 = D + 16
    first = nt(x2[0:d1, :], gh[0:HID, :]) + nt(x2[0:d1, :], gh[HID:2 * HID, :]) + nt(x2[d1:2 * d1, :], gh[0:HID, :])
    second = nt(gm[0:D, :], h2[0:HID, :]) + nt(gm[0:D, :], h2[HID:2 * HID, :]) + nt(gm[D:2 * D, :], h2[0:HID, :])
    first, second = first[0:D + 8] * factor, second * factor

    def put(part, out):
        rows, used = part.shape[0], 0
        for j in range(HID // LANES):
            out[used:used + rows, :] = part[:, j * LANES:(j + 1) * LANES]
            used += rows
        out[used:, :] = jnp.zeros((out.shape[0] - used, LANES), f32)

    @pl.when(odd == 0)
    def _():
        put(first, keep)
        put(second, send)

    @pl.when(odd == 1)
    def _():
        put(second, keep)
        put(first, send)


def start_loads(sems, sources, targets):
    loads = [pltpu.make_async_copy(src, dst, sems.at[n]) for n, (src, dst) in enumerate(zip(sources, targets))]
    for load in loads:
        load.start()
    return loads


def upper_kernel(hops, pos, factor, where, dist, tab1, tab0, src_h, wo3_h, slope_h, wi3_h, x2_h, h2_h, near_in, *refs):
    far_in, refs = refs[:hops], refs[hops:]
    near, refs = refs[0], refs[1:]
    far, refs = refs[:hops - 1], refs[hops - 1:]
    keep, send, grad_h, src, grad, wo3, slope, wi3, x2, h2, gm3, gh3, gm, join, sems = refs
    first, *loads = start_loads(sems, (src_h, wo3_h, slope_h, wi3_h, x2_h, h2_h), (src, wo3, slope, wi3, x2, h2))
    unpack_far(where, dist, tab1, 1, far_in, gm, hops, pos)
    first.wait()
    unpack_near(src, dist, tab1, 1, near_in, gm, join, pos)
    loads[0].wait()
    loads[1].wait()
    hidden(pos, wo3, slope, gm, gm3, gh3)
    loads[2].wait()
    inward(pos, wi3, gm, gh3, grad)
    store = pltpu.make_async_copy(grad, grad_h, sems.at[6])
    store.start()
    pack(grad, tab0, far, near, hops, pos)
    loads[3].wait()
    loads[4].wait()
    weight_terms(factor, where[0], x2, gh3, h2, gm3, keep, send)
    store.wait()


def lower_kernel(hops, pos, factor, where, dist, tab0, src_h, wo3_h, slope_h, x2_h, h2_h, near_in, *refs):
    far_in, refs = refs[:hops], refs[hops:]
    keep, send, gm_h, gh_h, src, gm, gh3, wo3, slope, x2, h2, gm3, join, sems = refs
    first, *loads = start_loads(sems, (src_h, wo3_h, slope_h, x2_h, h2_h), (src, wo3, slope, x2, h2))
    unpack_far(where, dist, tab0, 0, far_in, gm, hops, pos)
    first.wait()
    unpack_near(src, dist, tab0, 0, near_in, gm, join, pos)
    stores = [pltpu.make_async_copy(gm, gm_h, sems.at[5]), pltpu.make_async_copy(gh3, gh_h, sems.at[6])]
    stores[0].start()
    loads[0].wait()
    loads[1].wait()
    hidden(pos, wo3, slope, gm, gm3, gh3)
    stores[1].start()
    loads[2].wait()
    loads[3].wait()
    weight_terms(factor, where[0], x2, gh3, h2, gm3, keep, send)
    for store in stores:
        store.wait()


def input_kernel(pos, wi3_h, gm_h, gh_h, out, wi3, gm, gh3, sems):
    for load in start_loads(sems, (wi3_h, gm_h, gh_h), (wi3, gm, gh3)):
        load.wait()
    inward(pos, wi3, gm, gh3, out)


def finish_kernel(odd, *refs):
    sums, (w_in_grad, bias_grad, w_out_t_grad) = refs[:4], refs[4:]
    rows = D + 8

    def put(layer, first, second):
        for j in range(HID // LANES):
            lanes = slice(j * LANES, (j + 1) * LANES)
            w_in_grad[layer, :, lanes] = first[j * rows:j * rows + D, :]
            bias_grad[layer:layer + 1, lanes] = first[j * rows + D:j * rows + D + 1, :]
            w_out_t_grad[layer, :, lanes] = second[j * D:(j + 1) * D, :]

    for layer in range(2):
        mine, other = sums[2 * layer], sums[2 * layer + 1]

        @pl.when(odd[0] == 0)
        def _(layer=layer, mine=mine, other=other):
            put(layer, mine, other)

        @pl.when(odd[0] == 1)
        def _(layer=layer, mine=mine, other=other):
            put(layer, other, mine)


def from_ahead(value, steps):
    count = lax.axis_size("seq")
    return lax.ppermute(value, "seq", [(s, (s - steps) % count) for s in range(count)])


def exchange(value, mask):
    count = lax.axis_size("seq")
    return lax.ppermute(value, "seq", [(s, s ^ mask) for s in range(count)])


def fold(x, mask, send=None):
    half = x.shape[0] // 2
    bit = (lax.axis_index("seq") & mask) != 0
    low, high = x[:half], x[half:]
    return jnp.where(bit, high, low) + exchange(jnp.where(bit, low, high), mask)


def spread(x, mask):
    bit = (lax.axis_index("seq") & mask) != 0
    other = exchange(x, mask)
    return jnp.concatenate([jnp.where(bit, other, x), jnp.where(bit, x, other)], 0)


def shape(*dims, dtype=f32):
    return jax.ShapeDtypeStruct(dims, dtype)


def stay(*values, where=pltpu.VMEM):
    return [pltpu.with_memory_space_constraint(v, where) for v in values]


def stored(*dims, dtype=f32):
    return pltpu.HBM(dims, dtype)


def held(*dims, dtype=f32):
    return pltpu.VMEM(dims, dtype)


def body(first_inputs, second_inputs, out_grad, weight_in, bias_in, weight_out, distances):
    pos = first_inputs.shape[1]
    count = lax.axis_size("seq")
    hops = count.bit_length() - 1
    factor = 1.0 / math.sqrt(pos * count)
    near_width = near_slots(pos)[1]
    far_shapes = [shape(MOST * TW, pos)] * (hops - 1)
    near_shape = shape(TW, near_width)
    half = -(-3 * (D + 8) // (8 * count)) * 8 * count
    masks = [1 << b for b in range(1, hops)]
    far_hops = [1 << k for k in range(1, hops)]
    index = lax.axis_index("seq")
    where = jnp.stack([index & 1, (index >> 1) & 1]).astype(i32)

    def travel(near, far):
        paired = exchange(far[0], 2)
        moved = [from_ahead(f, h) for f, h in zip(far[:0:-1], far_hops[:0:-1])][::-1]
        near = from_ahead(near, 1)
        passed = lax.ppermute(paired, "seq", [(s, (s - 4) % count) for s in range(count) if s & 2])
        return near, [paired, passed] + moved

    whole_s = pltpu.VMEM((D, pos), f32)
    gm3_s = pltpu.VMEM((3 * D, pos), bf16)
    join_s = pltpu.VMEM((4, TW, 2 * pos + LANES), f32)
    distances, out_grad_h = [pltpu.with_memory_space_constraint(v, pltpu.HBM) for v in (distances, out_grad)]
    tab_1, near, *far = pl.pallas_call(
        lambda *refs: pack_kernel(hops, pos, *refs),
        out_shape=[shape(32, dtype=i32), near_shape] + far_shapes,
        in_specs=[SM, HB],
        out_specs=[SM] + [VM] * hops,
        scratch_shapes=[whole_s, pltpu.SemaphoreType.DMA],
        **kernel_options("pack", 3, 2),
    )(distances, out_grad_h)
    near, far = travel(near, far)

    w_out_t = jnp.transpose(weight_out, (0, 2, 1))
    saved = [first_inputs, second_inputs]
    act_ins = []
    for layer in range(2):
        act_ins += [saved[layer], weight_in[layer], bias_in[layer][:, None], w_out_t[layer]]
    act_shapes = [
        stored(2 * D + 32, pos, dtype=bf16),
        stored(2 * HID, pos, dtype=bf16),
        stored(HID, pos),
        stored(D, 3 * HID, dtype=bf16),
        stored(HID, 3 * D, dtype=bf16),
    ]
    tab_0, *acts = pl.pallas_call(
        lambda *refs: act_kernel(hops, pos, *refs),
        out_shape=[shape(32, dtype=i32)] + act_shapes * 2,
        in_specs=[SM] + [VM] * 8,
        out_specs=[SM] + [VM] * 10,
        scratch_shapes=[pltpu.VMEM((3 * D, 256), bf16)],
        **kernel_options("act", 24, 5),
    )(distances, *act_ins)
    x2_0, h2_0, slope_0, wi3_0, wo3_0, x2_1, h2_1, slope_1, wi3_1, wo3_1 = acts

    gh3_s = pltpu.VMEM((3 * HID, pos), bf16)
    x2_s = pltpu.VMEM((2 * D + 32, pos), bf16)
    h2_s = pltpu.VMEM((2 * HID, pos), bf16)
    slope_s = pltpu.VMEM((HID, pos), f32)
    wi3_s = pltpu.VMEM((D, 3 * HID), bf16)
    wo3_s = pltpu.VMEM((HID, 3 * D), bf16)
    sems_s = pltpu.SemaphoreType.DMA((7,))
    near, *rest = pl.pallas_call(
        lambda *refs: upper_kernel(hops, pos, factor, *refs),
        out_shape=[near_shape] + far_shapes + [shape(half, LANES)] * 2 + [stored(D, pos)],
        in_specs=[SM] * 4 + [HB] * 6 + [VM] * (hops + 1),
        out_specs=[VM] * (hops + 2) + [HB],
        scratch_shapes=[whole_s, whole_s, wo3_s, slope_s, wi3_s, x2_s, h2_s, gm3_s, gh3_s, whole_s, join_s, sems_s],
        **kernel_options("upper", 16, 6),
    )(where, distances, tab_1, tab_0, *stay(out_grad, wo3_1, slope_1, wi3_1, x2_1, h2_1, where=pltpu.HBM), near, *far)
    far, (keep_1, send_1, grad_1) = rest[:hops - 1], rest[hops - 1:]
    near, far = travel(near, far)

    sum_1 = keep_1 + exchange(send_1, 1)
    sum_1, near, far = lax.optimization_barrier((sum_1, near, far))
    sum_1 = fold(sum_1, masks[0])

    keep, send, gm_0, gh3_0 = pl.pallas_call(
        lambda *refs: lower_kernel(hops, pos, factor, *refs),
        out_shape=[shape(half, LANES)] * 2 + [stored(D, pos), stored(3 * HID, pos, dtype=bf16)],
        in_specs=[SM] * 3 + [HB] * 5 + [VM] * (hops + 1),
        out_specs=[VM] * 2 + [HB] * 2,
        scratch_shapes=[whole_s, whole_s, gh3_s, wo3_s, slope_s, x2_s, h2_s, gm3_s, join_s, sems_s],
        **kernel_options("lower", 16, 5),
    )(where, distances, tab_0, *stay(grad_1, wo3_0, slope_0, x2_0, h2_0, where=pltpu.HBM), near, *far)
    sum_0 = keep + exchange(send, 1)
    sum_0, gm_0 = lax.optimization_barrier((sum_0, gm_0))

    input_grad = pl.pallas_call(
        lambda *refs: input_kernel(pos, *refs),
        out_shape=shape(D, pos),
        in_specs=[HB] * 3,
        out_specs=VM,
        scratch_shapes=[pltpu.VMEM((D, 3 * HID), bf16), whole_s, gh3_s, sems_s],
        **kernel_options("inward", 12, 3),
    )(*stay(wi3_0, gm_0, gh3_0, where=pltpu.HBM))
    sum_1, _ = lax.optimization_barrier((sum_1, sum_0))
    for number, mask in enumerate(masks):
        if number > 0:
            sum_1 = fold(sum_1, mask)
        if number == 1:
            sum_0, input_grad = lax.optimization_barrier((sum_0, input_grad))
        sum_0 = fold(sum_0, mask)
    for mask in masks[::-1]:
        sum_1 = spread(sum_1, mask)
        sum_0 = spread(sum_0, mask)
    other_1 = exchange(sum_1, 1)
    other_0 = exchange(sum_0, 1)

    w_in_grad, bias_grad, w_out_t_grad = pl.pallas_call(
        finish_kernel,
        out_shape=[shape(2, D, HID), shape(2, HID), shape(2, D, HID)],
        in_specs=[SM] + [VM] * 4,
        out_specs=[VM] * 3,
        **kernel_options("finish", 4, 1),
    )(where, sum_0, other_0, sum_1, other_1)
    return input_grad, w_in_grad, bias_grad, jnp.transpose(w_out_t_grad, (0, 2, 1))


def solution(mesh):
    whole = P(None, ("groups", "seq"))
    in_specs = (whole, whole, whole, P(), P(), P(), P())
    out_specs = (whole, P("groups", None, None), P("groups", None), P("groups", None, None))
    return jax.shard_map(body, mesh=mesh, in_specs=in_specs, out_specs=out_specs, check_vma=False)
```

```python
import math

import jax
import jax.numpy as jnp
from jax import lax
from jax.experimental import pallas as pl
from jax.experimental.pallas import tpu as pltpu
from jax.sharding import PartitionSpec as P

TRACKS = 18
TW = 16
MOST = 3
D = TRACKS * TW
HID = 384
INNER = TRACKS - MOST
LANES = 128
MIB = 1 << 20

ROOT_HALF = 0.7071067811865476
INV_ROOT_TWO_PI = 0.3989422804014327

f32, bf16, i32 = jnp.float32, jnp.bfloat16, jnp.int32
VM = pl.BlockSpec(memory_space=pltpu.VMEM)
SM = pl.BlockSpec(memory_space=pltpu.SMEM)
HB = pl.BlockSpec(memory_space=pltpu.HBM)


def kernel_options(name, mib, cost_us):
    return dict(
        name=name,
        compiler_params=pltpu.CompilerParams(vmem_limit_bytes=mib * MIB),
        cost_estimate=pl.CostEstimate(flops=int(cost_us * 1e9), bytes_accessed=int(cost_us * 3e6), transcendentals=0),
    )


def near_slots(pos):
    slots, offset = [], 0
    for slot in range(INNER):
        width = max(LANES, pos >> (slot // MOST))
        slots.append((offset, width))
        offset += width
    return slots, offset


def halves(value):
    high = value.astype(bf16)
    return high, (value - high.astype(f32)).astype(bf16)


def put_triple(ref, value, rows, cols, order):
    pair = halves(value)
    for place, which in enumerate(order):
        ref[place * rows:(place + 1) * rows, cols] = pair[which]


def fill_tables(dist, tab, layer, hops, pos):
    d = [dist[layer, t] for t in range(TRACKS)]
    key = [d[t] * 32 + (31 - t) for t in range(TRACKS)]
    rank = [jnp.int32(0)] * TRACKS
    for t in range(TRACKS):
        for u in range(t + 1, TRACKS):
            above = (key[u] > key[t]).astype(i32)
            rank[t] = rank[t] + above
            rank[u] = rank[u] + (1 - above)
    for t in range(TRACKS):
        tab[rank[t]] = jnp.int32(t)
    for k in range(hops):
        first = jnp.int32(0)
        for t in range(TRACKS):
            first = first + (d[t] > (pos << k)).astype(i32)
        tab[TRACKS + k] = first


def track_at(tab, k, slot):
    place = tab[TRACKS + k] + slot
    return place, tab[jnp.minimum(place, TRACKS - 1)]


def rows_of(track):
    return pl.ds(pl.multiple_of(track * TW, TW), TW)


def pack(src, tab, far, near, hops, pos):
    for k in range(hops - 1, 0, -1):
        for slot in range(MOST):
            _, t = track_at(tab, k, slot)
            far[k - 1][slot * TW:(slot + 1) * TW, :] = src[rows_of(t), :]
    for slot, (offset, width) in enumerate(near_slots(pos)[0]):
        _, t = track_at(tab, 0, slot)
        near[:, offset:offset + width] = src[rows_of(t), 0:width]


def unpack_far(where, dist, tab, layer, far, out, hops, pos):
    for k in range(1, hops):
        for slot in range(MOST):
            place, t = track_at(tab, k, slot)
            mine = (place < TRACKS) & (dist[layer, t] == (pos << k))
            sources = [(far[0], where[1] == 0), (far[1], where[1] == 1)] if k == 1 else [(far[k], True)]
            for source, here in sources:
                @pl.when(mine & here)
                def _(source=source, slot=slot, t=t):
                    out[rows_of(t), :] = source[slot * TW:(slot + 1) * TW, :]


def unpack_near(src, dist, tab, layer, near, out, join, pos):
    for slot, (offset, width) in enumerate(near_slots(pos)[0]):
        place, t = track_at(tab, 0, slot)

        @pl.when(place < TRACKS)
        def _(slot=slot, t=t, offset=offset, width=width):
            shift = dist[layer, t]
            join[slot % 4, :, :pos] = src[rows_of(t), :]
            join[slot % 4, :, pos:pos + width] = near[:, offset:offset + width]
            base = pl.multiple_of(shift // LANES * LANES, LANES)
            rest = shift % LANES
            window = join[slot % 4, :, pl.ds(base, pos + LANES)]
            turned = pltpu.roll(window, jnp.where(rest == 0, 0, pos + LANES - rest), 1)
            out[rows_of(t), :] = turned[:, :pos]


def pack_kernel(hops, pos, dist, src_h, tab, near, *refs):
    far, (src, sem) = refs[:-2], refs[-2:]
    load = pltpu.make_async_copy(src_h, src, sem)
    load.start()
    fill_tables(dist, tab, 1, hops, pos)
    load.wait()
    pack(src, tab, far, near, hops, pos)


def act_kernel(hops, pos, dist, *refs):
    ins, tab, outs, xs = refs[:8], refs[8], refs[9:19], refs[19]
    fill_tables(dist, tab, 0, hops, pos)
    for layer in range(2):
        act(pos, *ins[4 * layer:4 * layer + 4], *outs[5 * layer:5 * layer + 5], xs)


def act(pos, x, w_in, bias, w_out_t, x2, h2, slope, wi3, wo3, xs):
    step = 256
    wt = jnp.transpose(w_in[...], (1, 0))
    wt_hi, wt_lo = halves(wt)
    wt3 = jnp.concatenate([wt_hi, wt_hi, wt_lo], axis=1)
    w_hi, w_lo = halves(w_in[...])
    wi3[...] = jnp.concatenate([w_hi, w_hi, w_lo], axis=1)
    w_hi, w_lo = halves(jnp.transpose(w_out_t[...], (1, 0)))
    wo3[...] = jnp.concatenate([w_hi, w_hi, w_lo], axis=1)
    for start in range(0, pos, step):
        cols = slice(start, start + step)
        x_hi, x_lo = halves(x[:, cols])
        x2[0:D, cols] = x_hi
        x2[D:D + 16, cols] = jnp.ones((16, step), bf16)
        x2[D + 16:2 * D + 16, cols] = x_lo
        x2[2 * D + 16:2 * D + 32, cols] = jnp.zeros((16, step), bf16)
        xs[0:D, :] = x_hi
        xs[D:2 * D, :] = x_lo
        xs[2 * D:3 * D, :] = x_hi
        pre = jnp.dot(wt3, xs[...], preferred_element_type=f32) + bias[...]
        cdf = 0.5 * (1.0 + lax.erf(pre * ROOT_HALF))
        put_triple(h2, pre * cdf, HID, cols, (0, 1))
        slope[:, cols] = cdf + pre * jnp.exp(-0.5 * pre * pre) * INV_ROOT_TWO_PI


def hidden(pos, wo3, slope, gm, gm3, gh3):
    step = 512
    for start in range(0, pos, step):
        cols = slice(start, start + step)
        put_triple(gm3, gm[:, cols], D, cols, (0, 1, 0))
        gh = jnp.dot(wo3[...], gm3[:, cols], preferred_element_type=f32) * slope[:, cols]
        put_triple(gh3, gh, HID, cols, (0, 1, 0))


def inward(pos, wi3, gm, gh3, out):
    step = 512
    for start in range(0, pos, step):
        cols = slice(start, start + step)
        out[:, cols] = gm[:, cols] + jnp.dot(wi3[...], gh3[:, cols], preferred_element_type=f32)


def weight_terms(factor, odd, x2, gh, h2, gm, keep, send):
    def nt(a, b):
        return lax.dot_general(a, b, (((1,), (1,)), ((), ())), preferred_element_type=f32)

    d1 = D + 16
    first = nt(x2[0:d1, :], gh[0:HID, :]) + nt(x2[0:d1, :], gh[HID:2 * HID, :]) + nt(x2[d1:2 * d1, :], gh[0:HID, :])
    second = nt(gm[0:D, :], h2[0:HID, :]) + nt(gm[0:D, :], h2[HID:2 * HID, :]) + nt(gm[D:2 * D, :], h2[0:HID, :])
    first, second = first[0:D + 8] * factor, second * factor

    def put(part, out):
        rows, used = part.shape[0], 0
        for j in range(HID // LANES):
            out[used:used + rows, :] = part[:, j * LANES:(j + 1) * LANES]
            used += rows
        out[used:, :] = jnp.zeros((out.shape[0] - used, LANES), f32)

    @pl.when(odd == 0)
    def _():
        put(first, keep)
        put(second, send)

    @pl.when(odd == 1)
    def _():
        put(second, keep)
        put(first, send)


def start_loads(sems, sources, targets):
    loads = [pltpu.make_async_copy(src, dst, sems.at[n]) for n, (src, dst) in enumerate(zip(sources, targets))]
    for load in loads:
        load.start()
    return loads


def upper_kernel(hops, pos, factor, where, dist, tab1, tab0, src_h, wo3_h, slope_h, wi3_h, x2_h, h2_h, near_in, *refs):
    far_in, refs = refs[:hops], refs[hops:]
    near, refs = refs[0], refs[1:]
    far, refs = refs[:hops - 1], refs[hops - 1:]
    keep, send, grad_h, src, grad, wo3, slope, wi3, x2, h2, gm3, gh3, gm, join, sems = refs
    first, *loads = start_loads(sems, (src_h, wo3_h, slope_h, wi3_h, x2_h, h2_h), (src, wo3, slope, wi3, x2, h2))
    unpack_far(where, dist, tab1, 1, far_in, gm, hops, pos)
    first.wait()
    unpack_near(src, dist, tab1, 1, near_in, gm, join, pos)
    loads[0].wait()
    loads[1].wait()
    hidden(pos, wo3, slope, gm, gm3, gh3)
    loads[2].wait()
    inward(pos, wi3, gm, gh3, grad)
    store = pltpu.make_async_copy(grad, grad_h, sems.at[6])
    store.start()
    pack(grad, tab0, far, near, hops, pos)
    loads[3].wait()
    loads[4].wait()
    weight_terms(factor, where[0], x2, gh3, h2, gm3, keep, send)
    store.wait()


def lower_kernel(hops, pos, factor, where, dist, tab0, src_h, wo3_h, slope_h, x2_h, h2_h, near_in, *refs):
    far_in, refs = refs[:hops], refs[hops:]
    keep, send, gm_h, gh_h, src, gm, gh3, wo3, slope, x2, h2, gm3, join, sems = refs
    first, *loads = start_loads(sems, (src_h, wo3_h, slope_h, x2_h, h2_h), (src, wo3, slope, x2, h2))
    unpack_far(where, dist, tab0, 0, far_in, gm, hops, pos)
    first.wait()
    unpack_near(src, dist, tab0, 0, near_in, gm, join, pos)
    stores = [pltpu.make_async_copy(gm, gm_h, sems.at[5]), pltpu.make_async_copy(gh3, gh_h, sems.at[6])]
    stores[0].start()
    loads[0].wait()
    loads[1].wait()
    hidden(pos, wo3, slope, gm, gm3, gh3)
    stores[1].start()
    loads[2].wait()
    loads[3].wait()
    weight_terms(factor, where[0], x2, gh3, h2, gm3, keep, send)
    for store in stores:
        store.wait()


def input_kernel(pos, wi3_h, gm_h, gh_h, out, wi3, gm, gh3, sems):
    for load in start_loads(sems, (wi3_h, gm_h, gh_h), (wi3, gm, gh3)):
        load.wait()
    inward(pos, wi3, gm, gh3, out)


def finish_kernel(odd, *refs):
    sums, (w_in_grad, bias_grad, w_out_t_grad) = refs[:4], refs[4:]
    rows = D + 8

    def put(layer, first, second):
        for j in range(HID // LANES):
            lanes = slice(j * LANES, (j + 1) * LANES)
            w_in_grad[layer, :, lanes] = first[j * rows:j * rows + D, :]
            bias_grad[layer:layer + 1, lanes] = first[j * rows + D:j * rows + D + 1, :]
            w_out_t_grad[layer, :, lanes] = second[j * D:(j + 1) * D, :]

    for layer in range(2):
        mine, other = sums[2 * layer], sums[2 * layer + 1]

        @pl.when(odd[0] == 0)
        def _(layer=layer, mine=mine, other=other):
            put(layer, mine, other)

        @pl.when(odd[0] == 1)
        def _(layer=layer, mine=mine, other=other):
            put(layer, other, mine)


def from_ahead(value, steps):
    count = lax.axis_size("seq")
    return lax.ppermute(value, "seq", [(s, (s - steps) % count) for s in range(count)])


def exchange(value, mask):
    count = lax.axis_size("seq")
    return lax.ppermute(value, "seq", [(s, s ^ mask) for s in range(count)])


def fold(x, mask, send=None):
    half = x.shape[0] // 2
    bit = (lax.axis_index("seq") & mask) != 0
    low, high = x[:half], x[half:]
    return jnp.where(bit, high, low) + exchange(jnp.where(bit, low, high), mask)


def spread(x, mask):
    bit = (lax.axis_index("seq") & mask) != 0
    other = exchange(x, mask)
    return jnp.concatenate([jnp.where(bit, other, x), jnp.where(bit, x, other)], 0)


def shape(*dims, dtype=f32):
    return jax.ShapeDtypeStruct(dims, dtype)


def stay(*values, where=pltpu.VMEM):
    return [pltpu.with_memory_space_constraint(v, where) for v in values]


def stored(*dims, dtype=f32):
    return pltpu.HBM(dims, dtype)


def held(*dims, dtype=f32):
    return pltpu.VMEM(dims, dtype)


def body(first_inputs, second_inputs, out_grad, weight_in, bias_in, weight_out, distances):
    pos = first_inputs.shape[1]
    count = lax.axis_size("seq")
    hops = count.bit_length() - 1
    factor = 1.0 / math.sqrt(pos * count)
    near_width = near_slots(pos)[1]
    far_shapes = [shape(MOST * TW, pos)] * (hops - 1)
    near_shape = shape(TW, near_width)
    half = -(-3 * (D + 8) // (8 * count)) * 8 * count
    masks = [1 << b for b in range(1, hops)]
    far_hops = [1 << k for k in range(1, hops)]
    index = lax.axis_index("seq")
    where = jnp.stack([index & 1, (index >> 1) & 1]).astype(i32)

    def travel(near, far):
        paired = exchange(far[0], 2)
        moved = [from_ahead(f, h) for f, h in zip(far[:0:-1], far_hops[:0:-1])][::-1]
        near = from_ahead(near, 1)
        passed = lax.ppermute(paired, "seq", [(s, (s - 4) % count) for s in range(count) if s & 2])
        return near, [paired, passed] + moved

    whole_s = pltpu.VMEM((D, pos), f32)
    gm3_s = pltpu.VMEM((3 * D, pos), bf16)
    join_s = pltpu.VMEM((4, TW, 2 * pos + LANES), f32)
    distances, out_grad_h = [pltpu.with_memory_space_constraint(v, pltpu.HBM) for v in (distances, out_grad)]
    tab_1, near, *far = pl.pallas_call(
        lambda *refs: pack_kernel(hops, pos, *refs),
        out_shape=[shape(32, dtype=i32), near_shape] + far_shapes,
        in_specs=[SM, HB],
        out_specs=[SM] + [VM] * hops,
        scratch_shapes=[whole_s, pltpu.SemaphoreType.DMA],
        **kernel_options("pack", 3, 2),
    )(distances, out_grad_h)
    near, far = travel(near, far)

    w_out_t = jnp.transpose(weight_out, (0, 2, 1))
    saved = [first_inputs, second_inputs]
    act_ins = []
    for layer in range(2):
        act_ins += [saved[layer], weight_in[layer], bias_in[layer][:, None], w_out_t[layer]]
    act_shapes = [
        stored(2 * D + 32, pos, dtype=bf16),
        stored(2 * HID, pos, dtype=bf16),
        stored(HID, pos),
        stored(D, 3 * HID, dtype=bf16),
        stored(HID, 3 * D, dtype=bf16),
    ]
    tab_0, *acts = pl.pallas_call(
        lambda *refs: act_kernel(hops, pos, *refs),
        out_shape=[shape(32, dtype=i32)] + act_shapes * 2,
        in_specs=[SM] + [VM] * 8,
        out_specs=[SM] + [VM] * 10,
        scratch_shapes=[pltpu.VMEM((3 * D, 256), bf16)],
        **kernel_options("act", 24, 5),
    )(distances, *act_ins)
    x2_0, h2_0, slope_0, wi3_0, wo3_0, x2_1, h2_1, slope_1, wi3_1, wo3_1 = acts

    gh3_s = pltpu.VMEM((3 * HID, pos), bf16)
    x2_s = pltpu.VMEM((2 * D + 32, pos), bf16)
    h2_s = pltpu.VMEM((2 * HID, pos), bf16)
    slope_s = pltpu.VMEM((HID, pos), f32)
    wi3_s = pltpu.VMEM((D, 3 * HID), bf16)
    wo3_s = pltpu.VMEM((HID, 3 * D), bf16)
    sems_s = pltpu.SemaphoreType.DMA((7,))
    near, *rest = pl.pallas_call(
        lambda *refs: upper_kernel(hops, pos, factor, *refs),
        out_shape=[near_shape] + far_shapes + [shape(half, LANES)] * 2 + [stored(D, pos)],
        in_specs=[SM] * 4 + [HB] * 6 + [VM] * (hops + 1),
        out_specs=[VM] * (hops + 2) + [HB],
        scratch_shapes=[whole_s, whole_s, wo3_s, slope_s, wi3_s, x2_s, h2_s, gm3_s, gh3_s, whole_s, join_s, sems_s],
        **kernel_options("upper", 16, 6),
    )(where, distances, tab_1, tab_0, *stay(out_grad, wo3_1, slope_1, wi3_1, x2_1, h2_1, where=pltpu.HBM), near, *far)
    far, (keep_1, send_1, grad_1) = rest[:hops - 1], rest[hops - 1:]
    near, far = travel(near, far)

    sum_1 = keep_1 + exchange(send_1, 1)
    sum_1 = fold(sum_1, masks[0])

    keep, send, gm_0, gh3_0 = pl.pallas_call(
        lambda *refs: lower_kernel(hops, pos, factor, *refs),
        out_shape=[shape(half, LANES)] * 2 + [stored(D, pos), stored(3 * HID, pos, dtype=bf16)],
        in_specs=[SM] * 3 + [HB] * 5 + [VM] * (hops + 1),
        out_specs=[VM] * 2 + [HB] * 2,
        scratch_shapes=[whole_s, whole_s, gh3_s, wo3_s, slope_s, x2_s, h2_s, gm3_s, join_s, sems_s],
        **kernel_options("lower", 16, 5),
    )(where, distances, tab_0, *stay(grad_1, wo3_0, slope_0, x2_0, h2_0, where=pltpu.HBM), near, *far)
    sum_0 = keep + exchange(send, 1)
    steps = [(fold, mask) for mask in masks] + [(spread, mask) for mask in masks[::-1]]
    for (step, mask), (ahead, mask_1) in zip(steps[:-1], steps[1:]):
        sum_1, _ = lax.optimization_barrier((sum_1, sum_0))
        sum_1 = ahead(sum_1, mask_1)
        sum_0 = step(sum_0, mask)
    sum_0, gm_0 = lax.optimization_barrier((sum_0, gm_0))

    input_grad = pl.pallas_call(
        lambda *refs: input_kernel(pos, *refs),
        out_shape=shape(D, pos),
        in_specs=[HB] * 3,
        out_specs=VM,
        scratch_shapes=[pltpu.VMEM((D, 3 * HID), bf16), whole_s, gh3_s, sems_s],
        **kernel_options("inward", 12, 3),
    )(*stay(wi3_0, gm_0, gh3_0, where=pltpu.HBM))
    sum_1, _ = lax.optimization_barrier((sum_1, sum_0))
    other_1 = exchange(sum_1, 1)
    sum_0 = spread(sum_0, masks[0])
    sum_0, input_grad = lax.optimization_barrier((sum_0, input_grad))
    other_0 = exchange(sum_0, 1)

    w_in_grad, bias_grad, w_out_t_grad = pl.pallas_call(
        finish_kernel,
        out_shape=[shape(2, D, HID), shape(2, HID), shape(2, D, HID)],
        in_specs=[SM] + [VM] * 4,
        out_specs=[VM] * 3,
        **kernel_options("finish", 4, 1),
    )(where, sum_0, other_0, sum_1, other_1)
    return input_grad, w_in_grad, bias_grad, jnp.transpose(w_out_t_grad, (0, 2, 1))


def solution(mesh):
    whole = P(None, ("groups", "seq"))
    in_specs = (whole, whole, whole, P(), P(), P(), P())
    out_specs = (whole, P("groups", None, None), P("groups", None), P("groups", None, None))
    return jax.shard_map(body, mesh=mesh, in_specs=in_specs, out_specs=out_specs, check_vma=False)
```

```python
import math

import jax
import jax.numpy as jnp
from jax import lax
from jax.experimental import pallas as pl
from jax.experimental.pallas import tpu as pltpu
from jax.sharding import PartitionSpec as P

TRACKS = 18
TW = 16
MOST = 3
D = TRACKS * TW
HID = 384
INNER = TRACKS - MOST
LANES = 128
MIB = 1 << 20

ROOT_HALF = 0.7071067811865476
INV_ROOT_TWO_PI = 0.3989422804014327

f32, bf16, i32 = jnp.float32, jnp.bfloat16, jnp.int32
VM = pl.BlockSpec(memory_space=pltpu.VMEM)
SM = pl.BlockSpec(memory_space=pltpu.SMEM)
HB = pl.BlockSpec(memory_space=pltpu.HBM)


def kernel_options(name, mib, cost_us):
    return dict(
        name=name,
        compiler_params=pltpu.CompilerParams(vmem_limit_bytes=mib * MIB),
        cost_estimate=pl.CostEstimate(flops=int(cost_us * 1e9), bytes_accessed=int(cost_us * 3e6), transcendentals=0),
    )


def near_slots(pos):
    slots, offset = [], 0
    for slot in range(INNER):
        width = max(LANES, pos >> (slot // MOST))
        slots.append((offset, width))
        offset += width
    return slots, offset


def halves(value):
    high = value.astype(bf16)
    return high, (value - high.astype(f32)).astype(bf16)


def put_triple(ref, value, rows, cols, order):
    pair = halves(value)
    for place, which in enumerate(order):
        ref[place * rows:(place + 1) * rows, cols] = pair[which]


def fill_tables(dist, tab, layer, hops, pos):
    d = [dist[layer, t] for t in range(TRACKS)]
    key = [d[t] * 32 + (31 - t) for t in range(TRACKS)]
    rank = [jnp.int32(0)] * TRACKS
    for t in range(TRACKS):
        for u in range(t + 1, TRACKS):
            above = (key[u] > key[t]).astype(i32)
            rank[t] = rank[t] + above
            rank[u] = rank[u] + (1 - above)
    for t in range(TRACKS):
        tab[rank[t]] = jnp.int32(t)
    for k in range(hops):
        first = jnp.int32(0)
        for t in range(TRACKS):
            first = first + (d[t] > (pos << k)).astype(i32)
        tab[TRACKS + k] = first


def track_at(tab, k, slot):
    place = tab[TRACKS + k] + slot
    return place, tab[jnp.minimum(place, TRACKS - 1)]


def rows_of(track):
    return pl.ds(pl.multiple_of(track * TW, TW), TW)


def pack(src, tab, far, near, hops, pos):
    for k in range(hops - 1, 0, -1):
        for slot in range(MOST):
            _, t = track_at(tab, k, slot)
            far[k - 1][slot * TW:(slot + 1) * TW, :] = src[rows_of(t), :]
    for slot, (offset, width) in enumerate(near_slots(pos)[0]):
        _, t = track_at(tab, 0, slot)
        near[:, offset:offset + width] = src[rows_of(t), 0:width]


def unpack_far(where, dist, tab, layer, far, out, hops, pos):
    for k in range(1, hops):
        for slot in range(MOST):
            place, t = track_at(tab, k, slot)
            mine = (place < TRACKS) & (dist[layer, t] == (pos << k))
            sources = [(far[0], where[1] == 0), (far[1], where[1] == 1)] if k == 1 else [(far[k], True)]
            for source, here in sources:
                @pl.when(mine & here)
                def _(source=source, slot=slot, t=t):
                    out[rows_of(t), :] = source[slot * TW:(slot + 1) * TW, :]


def unpack_near(src, dist, tab, layer, near, out, join, pos):
    for slot, (offset, width) in enumerate(near_slots(pos)[0]):
        place, t = track_at(tab, 0, slot)

        @pl.when(place < TRACKS)
        def _(slot=slot, t=t, offset=offset, width=width):
            shift = dist[layer, t]
            join[slot % 4, :, :pos] = src[rows_of(t), :]
            join[slot % 4, :, pos:pos + width] = near[:, offset:offset + width]
            base = pl.multiple_of(shift // LANES * LANES, LANES)
            rest = shift % LANES
            window = join[slot % 4, :, pl.ds(base, pos + LANES)]
            turned = pltpu.roll(window, jnp.where(rest == 0, 0, pos + LANES - rest), 1)
            out[rows_of(t), :] = turned[:, :pos]


def pack_kernel(hops, pos, dist, src_h, tab, near, *refs):
    far, (src, sem) = refs[:-2], refs[-2:]
    load = pltpu.make_async_copy(src_h, src, sem)
    load.start()
    fill_tables(dist, tab, 1, hops, pos)
    load.wait()
    pack(src, tab, far, near, hops, pos)


def act_kernel(hops, pos, dist, *refs):
    ins, tab, outs, xs = refs[:8], refs[8], refs[9:19], refs[19]
    fill_tables(dist, tab, 0, hops, pos)
    for layer in range(2):
        act(pos, *ins[4 * layer:4 * layer + 4], *outs[5 * layer:5 * layer + 5], xs)


def act(pos, x, w_in, bias, w_out_t, x2, h2, slope, wi3, wo3, xs):
    step = 256
    wt = jnp.transpose(w_in[...], (1, 0))
    wt_hi, wt_lo = halves(wt)
    wt3 = jnp.concatenate([wt_hi, wt_hi, wt_lo], axis=1)
    w_hi, w_lo = halves(w_in[...])
    wi3[...] = jnp.concatenate([w_hi, w_hi, w_lo], axis=1)
    w_hi, w_lo = halves(jnp.transpose(w_out_t[...], (1, 0)))
    wo3[...] = jnp.concatenate([w_hi, w_hi, w_lo], axis=1)
    for start in range(0, pos, step):
        cols = slice(start, start + step)
        x_hi, x_lo = halves(x[:, cols])
        x2[0:D, cols] = x_hi
        x2[D:D + 16, cols] = jnp.ones((16, step), bf16)
        x2[D + 16:2 * D + 16, cols] = x_lo
        x2[2 * D + 16:2 * D + 32, cols] = jnp.zeros((16, step), bf16)
        xs[0:D, :] = x_hi
        xs[D:2 * D, :] = x_lo
        xs[2 * D:3 * D, :] = x_hi
        pre = jnp.dot(wt3, xs[...], preferred_element_type=f32) + bias[...]
        cdf = 0.5 * (1.0 + lax.erf(pre * ROOT_HALF))
        put_triple(h2, pre * cdf, HID, cols, (0, 1))
        slope[:, cols] = cdf + pre * jnp.exp(-0.5 * pre * pre) * INV_ROOT_TWO_PI


def hidden(pos, wo3, slope, gm, gm3, gh3):
    step = 512
    for start in range(0, pos, step):
        cols = slice(start, start + step)
        put_triple(gm3, gm[:, cols], D, cols, (0, 1, 0))
        gh = jnp.dot(wo3[...], gm3[:, cols], preferred_element_type=f32) * slope[:, cols]
        put_triple(gh3, gh, HID, cols, (0, 1, 0))


def inward(pos, wi3, gm, gh3, out):
    step = 512
    for start in range(0, pos, step):
        cols = slice(start, start + step)
        out[:, cols] = gm[:, cols] + jnp.dot(wi3[...], gh3[:, cols], preferred_element_type=f32)


def weight_terms(factor, odd, x2, gh, h2, gm, keep, send):
    def nt(a, b):
        return lax.dot_general(a, b, (((1,), (1,)), ((), ())), preferred_element_type=f32)

    d1 = D + 16
    first = nt(x2[0:d1, :], gh[0:HID, :]) + nt(x2[0:d1, :], gh[HID:2 * HID, :]) + nt(x2[d1:2 * d1, :], gh[0:HID, :])
    second = nt(gm[0:D, :], h2[0:HID, :]) + nt(gm[0:D, :], h2[HID:2 * HID, :]) + nt(gm[D:2 * D, :], h2[0:HID, :])
    first, second = first[0:D + 8] * factor, second * factor

    def put(part, out):
        rows, used = part.shape[0], 0
        for j in range(HID // LANES):
            out[used:used + rows, :] = part[:, j * LANES:(j + 1) * LANES]
            used += rows
        out[used:, :] = jnp.zeros((out.shape[0] - used, LANES), f32)

    @pl.when(odd == 0)
    def _():
        put(first, keep)
        put(second, send)

    @pl.when(odd == 1)
    def _():
        put(second, keep)
        put(first, send)


def start_loads(sems, sources, targets):
    loads = [pltpu.make_async_copy(src, dst, sems.at[n]) for n, (src, dst) in enumerate(zip(sources, targets))]
    for load in loads:
        load.start()
    return loads


def upper_kernel(hops, pos, factor, where, dist, tab1, tab0, src_h, wo3_h, slope_h, wi3_h, x2_h, h2_h, near_in, *refs):
    far_in, refs = refs[:hops], refs[hops:]
    near, refs = refs[0], refs[1:]
    far, refs = refs[:hops - 1], refs[hops - 1:]
    keep, send, grad_h, src, grad, wo3, slope, wi3, x2, h2, gm3, gh3, gm, join, sems = refs
    first, *loads = start_loads(sems, (src_h, wo3_h, slope_h, wi3_h, x2_h, h2_h), (src, wo3, slope, wi3, x2, h2))
    unpack_far(where, dist, tab1, 1, far_in, gm, hops, pos)
    first.wait()
    unpack_near(src, dist, tab1, 1, near_in, gm, join, pos)
    loads[0].wait()
    loads[1].wait()
    hidden(pos, wo3, slope, gm, gm3, gh3)
    loads[2].wait()
    inward(pos, wi3, gm, gh3, grad)
    store = pltpu.make_async_copy(grad, grad_h, sems.at[6])
    store.start()
    pack(grad, tab0, far, near, hops, pos)
    loads[3].wait()
    loads[4].wait()
    weight_terms(factor, where[0], x2, gh3, h2, gm3, keep, send)
    store.wait()


def lower_kernel(hops, pos, factor, where, dist, tab0, src_h, wo3_h, slope_h, x2_h, h2_h, near_in, *refs):
    far_in, refs = refs[:hops], refs[hops:]
    keep, send, gm_h, gh_h, src, gm, gh3, wo3, slope, x2, h2, gm3, join, sems = refs
    first, *loads = start_loads(sems, (src_h, wo3_h, slope_h, x2_h, h2_h), (src, wo3, slope, x2, h2))
    unpack_far(where, dist, tab0, 0, far_in, gm, hops, pos)
    first.wait()
    unpack_near(src, dist, tab0, 0, near_in, gm, join, pos)
    stores = [pltpu.make_async_copy(gm, gm_h, sems.at[5]), pltpu.make_async_copy(gh3, gh_h, sems.at[6])]
    stores[0].start()
    loads[0].wait()
    loads[1].wait()
    hidden(pos, wo3, slope, gm, gm3, gh3)
    stores[1].start()
    loads[2].wait()
    loads[3].wait()
    weight_terms(factor, where[0], x2, gh3, h2, gm3, keep, send)
    for store in stores:
        store.wait()


def input_kernel(pos, wi3_h, gm_h, gh_h, out, wi3, gm, gh3, sems):
    for load in start_loads(sems, (wi3_h, gm_h, gh_h), (wi3, gm, gh3)):
        load.wait()
    inward(pos, wi3, gm, gh3, out)


def finish_kernel(odd, *refs):
    sums, (w_in_grad, bias_grad, w_out_t_grad) = refs[:4], refs[4:]
    rows = D + 8

    def put(layer, first, second):
        for j in range(HID // LANES):
            lanes = slice(j * LANES, (j + 1) * LANES)
            w_in_grad[layer, :, lanes] = first[j * rows:j * rows + D, :]
            bias_grad[layer:layer + 1, lanes] = first[j * rows + D:j * rows + D + 1, :]
            w_out_t_grad[layer, :, lanes] = second[j * D:(j + 1) * D, :]

    for layer in range(2):
        mine, other = sums[2 * layer], sums[2 * layer + 1]

        @pl.when(odd[0] == 0)
        def _(layer=layer, mine=mine, other=other):
            put(layer, mine, other)

        @pl.when(odd[0] == 1)
        def _(layer=layer, mine=mine, other=other):
            put(layer, other, mine)


def from_ahead(value, steps):
    count = lax.axis_size("seq")
    return lax.ppermute(value, "seq", [(s, (s - steps) % count) for s in range(count)])


def exchange(value, mask):
    count = lax.axis_size("seq")
    return lax.ppermute(value, "seq", [(s, s ^ mask) for s in range(count)])


def fold(x, mask):
    half = x.shape[0] // 2
    bit = (lax.axis_index("seq") & mask) != 0
    low, high = x[:half], x[half:]
    return jnp.where(bit, high, low) + exchange(jnp.where(bit, low, high), mask)


def spread(x, mask):
    bit = (lax.axis_index("seq") & mask) != 0
    other = exchange(x, mask)
    return jnp.concatenate([jnp.where(bit, other, x), jnp.where(bit, x, other)], 0)


def groups_of_four(offset):
    count = lax.axis_size("seq")
    return [(s, (s + 4 * offset) % count) for s in range(count)]


def fold_far(x):
    number = lax.axis_size("seq") // 4
    mine = lax.axis_index("seq") >> 2
    rows = x.shape[0] // number

    def part(group):
        return lax.dynamic_slice_in_dim(x, (group % number) * rows, rows, 0)

    arrived = [lax.ppermute(part(mine + o), "seq", groups_of_four(o)) for o in range(1, number)]
    return sum(arrived, part(mine))


def spread_far(x):
    number = lax.axis_size("seq") // 4
    mine = lax.axis_index("seq") >> 2
    rows = x.shape[0]
    arrived = [lax.ppermute(x, "seq", groups_of_four(o)) for o in range(1, number)]
    turned = jnp.concatenate([x] + arrived[::-1], 0)
    return lax.dynamic_slice_in_dim(jnp.concatenate([turned, turned], 0), ((number - mine) % number) * rows, number * rows, 0)


def shape(*dims, dtype=f32):
    return jax.ShapeDtypeStruct(dims, dtype)


def stay(*values, where=pltpu.VMEM):
    return [pltpu.with_memory_space_constraint(v, where) for v in values]


def stored(*dims, dtype=f32):
    return pltpu.HBM(dims, dtype)


def held(*dims, dtype=f32):
    return pltpu.VMEM(dims, dtype)


def body(first_inputs, second_inputs, out_grad, weight_in, bias_in, weight_out, distances):
    pos = first_inputs.shape[1]
    count = lax.axis_size("seq")
    hops = count.bit_length() - 1
    factor = 1.0 / math.sqrt(pos * count)
    near_width = near_slots(pos)[1]
    far_shapes = [shape(MOST * TW, pos)] * (hops - 1)
    near_shape = shape(TW, near_width)
    half = -(-3 * (D + 8) // (8 * count)) * 8 * count
    far_hops = [1 << k for k in range(1, hops)]
    index = lax.axis_index("seq")
    where = jnp.stack([index & 1, (index >> 1) & 1]).astype(i32)

    def travel(near, far):
        paired = exchange(far[0], 2)
        moved = [from_ahead(f, h) for f, h in zip(far[:0:-1], far_hops[:0:-1])][::-1]
        near = from_ahead(near, 1)
        passed = lax.ppermute(paired, "seq", [(s, (s - 4) % count) for s in range(count) if s & 2])
        return near, [paired, passed] + moved

    whole_s = pltpu.VMEM((D, pos), f32)
    gm3_s = pltpu.VMEM((3 * D, pos), bf16)
    join_s = pltpu.VMEM((4, TW, 2 * pos + LANES), f32)
    distances, out_grad_h = [pltpu.with_memory_space_constraint(v, pltpu.HBM) for v in (distances, out_grad)]
    tab_1, near, *far = pl.pallas_call(
        lambda *refs: pack_kernel(hops, pos, *refs),
        out_shape=[shape(32, dtype=i32), near_shape] + far_shapes,
        in_specs=[SM, HB],
        out_specs=[SM] + [VM] * hops,
        scratch_shapes=[whole_s, pltpu.SemaphoreType.DMA],
        **kernel_options("pack", 3, 2),
    )(distances, out_grad_h)
    near, far = travel(near, far)

    w_out_t = jnp.transpose(weight_out, (0, 2, 1))
    saved = [first_inputs, second_inputs]
    act_ins = []
    for layer in range(2):
        act_ins += [saved[layer], weight_in[layer], bias_in[layer][:, None], w_out_t[layer]]
    act_shapes = [
        stored(2 * D + 32, pos, dtype=bf16),
        stored(2 * HID, pos, dtype=bf16),
        stored(HID, pos),
        stored(D, 3 * HID, dtype=bf16),
        stored(HID, 3 * D, dtype=bf16),
    ]
    tab_0, *acts = pl.pallas_call(
        lambda *refs: act_kernel(hops, pos, *refs),
        out_shape=[shape(32, dtype=i32)] + act_shapes * 2,
        in_specs=[SM] + [VM] * 8,
        out_specs=[SM] + [VM] * 10,
        scratch_shapes=[pltpu.VMEM((3 * D, 256), bf16)],
        **kernel_options("act", 24, 5),
    )(distances, *act_ins)
    x2_0, h2_0, slope_0, wi3_0, wo3_0, x2_1, h2_1, slope_1, wi3_1, wo3_1 = acts

    gh3_s = pltpu.VMEM((3 * HID, pos), bf16)
    x2_s = pltpu.VMEM((2 * D + 32, pos), bf16)
    h2_s = pltpu.VMEM((2 * HID, pos), bf16)
    slope_s = pltpu.VMEM((HID, pos), f32)
    wi3_s = pltpu.VMEM((D, 3 * HID), bf16)
    wo3_s = pltpu.VMEM((HID, 3 * D), bf16)
    sems_s = pltpu.SemaphoreType.DMA((7,))
    near, *rest = pl.pallas_call(
        lambda *refs: upper_kernel(hops, pos, factor, *refs),
        out_shape=[near_shape] + far_shapes + [shape(half, LANES)] * 2 + [stored(D, pos)],
        in_specs=[SM] * 4 + [HB] * 6 + [VM] * (hops + 1),
        out_specs=[VM] * (hops + 2) + [HB],
        scratch_shapes=[whole_s, whole_s, wo3_s, slope_s, wi3_s, x2_s, h2_s, gm3_s, gh3_s, whole_s, join_s, sems_s],
        **kernel_options("upper", 16, 6),
    )(where, distances, tab_1, tab_0, *stay(out_grad, wo3_1, slope_1, wi3_1, x2_1, h2_1, where=pltpu.HBM), near, *far)
    far, (keep_1, send_1, grad_1) = rest[:hops - 1], rest[hops - 1:]
    near, far = travel(near, far)

    sum_1 = keep_1 + exchange(send_1, 1)
    sum_1 = fold(sum_1, 2)

    keep, send, gm_0, gh3_0 = pl.pallas_call(
        lambda *refs: lower_kernel(hops, pos, factor, *refs),
        out_shape=[shape(half, LANES)] * 2 + [stored(D, pos), stored(3 * HID, pos, dtype=bf16)],
        in_specs=[SM] * 3 + [HB] * 5 + [VM] * (hops + 1),
        out_specs=[VM] * 2 + [HB] * 2,
        scratch_shapes=[whole_s, whole_s, gh3_s, wo3_s, slope_s, x2_s, h2_s, gm3_s, join_s, sems_s],
        **kernel_options("lower", 16, 5),
    )(where, distances, tab_0, *stay(grad_1, wo3_0, slope_0, x2_0, h2_0, where=pltpu.HBM), near, *far)
    sum_0 = keep + exchange(send, 1)
    steps = [lambda x: fold(x, 2), fold_far, spread_far, lambda x: spread(x, 2)]
    for step, ahead in zip(steps[:-1], steps[1:]):
        sum_1, _ = lax.optimization_barrier((sum_1, sum_0))
        sum_1 = ahead(sum_1)
        sum_0 = step(sum_0)
    sum_0, gm_0 = lax.optimization_barrier((sum_0, gm_0))

    input_grad = pl.pallas_call(
        lambda *refs: input_kernel(pos, *refs),
        out_shape=shape(D, pos),
        in_specs=[HB] * 3,
        out_specs=VM,
        scratch_shapes=[pltpu.VMEM((D, 3 * HID), bf16), whole_s, gh3_s, sems_s],
        **kernel_options("inward", 12, 3),
    )(*stay(wi3_0, gm_0, gh3_0, where=pltpu.HBM))
    sum_1, _ = lax.optimization_barrier((sum_1, sum_0))
    other_1 = exchange(sum_1, 1)
    sum_0 = spread(sum_0, 2)
    sum_0, input_grad = lax.optimization_barrier((sum_0, input_grad))
    other_0 = exchange(sum_0, 1)

    w_in_grad, bias_grad, w_out_t_grad = pl.pallas_call(
        finish_kernel,
        out_shape=[shape(2, D, HID), shape(2, HID), shape(2, D, HID)],
        in_specs=[SM] + [VM] * 4,
        out_specs=[VM] * 3,
        **kernel_options("finish", 4, 1),
    )(where, sum_0, other_0, sum_1, other_1)
    return input_grad, w_in_grad, bias_grad, jnp.transpose(w_out_t_grad, (0, 2, 1))


def solution(mesh):
    whole = P(None, ("groups", "seq"))
    in_specs = (whole, whole, whole, P(), P(), P(), P())
    out_specs = (whole, P("groups", None, None), P("groups", None), P("groups", None, None))
    return jax.shard_map(body, mesh=mesh, in_specs=in_specs, out_specs=out_specs, check_vma=False)
```

```python
import math

import jax
import jax.numpy as jnp
from jax import lax
from jax.experimental import pallas as pl
from jax.experimental.pallas import tpu as pltpu
from jax.sharding import PartitionSpec as P

TRACKS = 18
TW = 16
MOST = 3
D = TRACKS * TW
HID = 384
INNER = TRACKS - MOST
LANES = 128
MIB = 1 << 20

ROOT_HALF = 0.7071067811865476
INV_ROOT_TWO_PI = 0.3989422804014327

f32, bf16, i32 = jnp.float32, jnp.bfloat16, jnp.int32
VM = pl.BlockSpec(memory_space=pltpu.VMEM)
SM = pl.BlockSpec(memory_space=pltpu.SMEM)
HB = pl.BlockSpec(memory_space=pltpu.HBM)


def kernel_options(name, mib, cost_us):
    return dict(
        name=name,
        compiler_params=pltpu.CompilerParams(vmem_limit_bytes=mib * MIB),
        cost_estimate=pl.CostEstimate(flops=int(cost_us * 1e9), bytes_accessed=int(cost_us * 3e6), transcendentals=0),
    )


def near_slots(pos):
    slots, offset = [], 0
    for slot in range(INNER):
        width = max(LANES, pos >> (slot // MOST))
        slots.append((offset, width))
        offset += width
    return slots, offset


def halves(value):
    high = value.astype(bf16)
    return high, (value - high.astype(f32)).astype(bf16)


def put_triple(ref, value, rows, cols, order):
    pair = halves(value)
    for place, which in enumerate(order):
        ref[place * rows:(place + 1) * rows, cols] = pair[which]


def fill_tables(dist, tab, layer, hops, pos):
    d = [dist[layer, t] for t in range(TRACKS)]
    key = [d[t] * 32 + (31 - t) for t in range(TRACKS)]
    rank = [jnp.int32(0)] * TRACKS
    for t in range(TRACKS):
        for u in range(t + 1, TRACKS):
            above = (key[u] > key[t]).astype(i32)
            rank[t] = rank[t] + above
            rank[u] = rank[u] + (1 - above)
    for t in range(TRACKS):
        tab[rank[t]] = jnp.int32(t)
    for k in range(hops):
        first = jnp.int32(0)
        for t in range(TRACKS):
            first = first + (d[t] > (pos << k)).astype(i32)
        tab[TRACKS + k] = first
    for t in range(TRACKS):
        tab[32 + t] = d[t]


def track_at(tab, k, slot):
    place = tab[TRACKS + k] + slot
    return place, tab[jnp.minimum(place, TRACKS - 1)]


def rows_of(track):
    return pl.ds(pl.multiple_of(track * TW, TW), TW)


def pack(src, tab, far, near, hops, pos):
    for k in range(hops - 1, 0, -1):
        for slot in range(MOST):
            _, t = track_at(tab, k, slot)
            far[k - 1][slot * TW:(slot + 1) * TW, :] = src[rows_of(t), :]
    for slot, (offset, width) in enumerate(near_slots(pos)[0]):
        _, t = track_at(tab, 0, slot)
        near[:, offset:offset + width] = src[rows_of(t), 0:width]


def place_bits():
    index = lax.axis_index("seq")
    return index & 1, (index >> 1) & 1


def unpack_far(where, tab, far, out, hops, pos):
    for k in range(1, hops):
        for slot in range(MOST):
            place, t = track_at(tab, k, slot)
            mine = (place < TRACKS) & (tab[32 + t] == (pos << k))
            sources = [(far[0], where[1] == 0), (far[1], where[1] == 1)] if k == 1 else [(far[k], True)]
            for source, here in sources:
                @pl.when(mine & here)
                def _(source=source, slot=slot, t=t):
                    out[rows_of(t), :] = source[slot * TW:(slot + 1) * TW, :]


def unpack_near(src, tab, near, out, join, pos):
    for slot, (offset, width) in enumerate(near_slots(pos)[0]):
        place, t = track_at(tab, 0, slot)

        @pl.when(place < TRACKS)
        def _(slot=slot, t=t, offset=offset, width=width):
            shift = tab[32 + t]
            join[slot % 4, :, :pos] = src[rows_of(t), :]
            join[slot % 4, :, pos:pos + width] = near[:, offset:offset + width]
            base = pl.multiple_of(shift // LANES * LANES, LANES)
            rest = shift % LANES
            window = join[slot % 4, :, pl.ds(base, pos + LANES)]
            turned = pltpu.roll(window, jnp.where(rest == 0, 0, pos + LANES - rest), 1)
            out[rows_of(t), :] = turned[:, :pos]


def pack_kernel(hops, pos, dist, src_h, tab, near, *refs):
    far, (src, sem) = refs[:-2], refs[-2:]
    load = pltpu.make_async_copy(src_h, src, sem)
    load.start()
    fill_tables(dist, tab, 1, hops, pos)
    load.wait()
    pack(src, tab, far, near, hops, pos)


def act_kernel(hops, pos, dist, *refs):
    ins, tab, outs, xs = refs[:8], refs[8], refs[9:19], refs[19]
    fill_tables(dist, tab, 0, hops, pos)
    for layer in range(2):
        act(pos, *ins[4 * layer:4 * layer + 4], *outs[5 * layer:5 * layer + 5], xs)


def act(pos, x, w_in, bias, w_out_t, x2, h2, slope, wi3, wo3, xs):
    step = 256
    wt = jnp.transpose(w_in[...], (1, 0))
    wt_hi, wt_lo = halves(wt)
    wt3 = jnp.concatenate([wt_hi, wt_hi, wt_lo], axis=1)
    w_hi, w_lo = halves(w_in[...])
    wi3[...] = jnp.concatenate([w_hi, w_hi, w_lo], axis=1)
    w_hi, w_lo = halves(jnp.transpose(w_out_t[...], (1, 0)))
    wo3[...] = jnp.concatenate([w_hi, w_hi, w_lo], axis=1)
    for start in range(0, pos, step):
        cols = slice(start, start + step)
        x_hi, x_lo = halves(x[:, cols])
        x2[0:D, cols] = x_hi
        x2[D:D + 16, cols] = jnp.ones((16, step), bf16)
        x2[D + 16:2 * D + 16, cols] = x_lo
        x2[2 * D + 16:2 * D + 32, cols] = jnp.zeros((16, step), bf16)
        xs[0:D, :] = x_hi
        xs[D:2 * D, :] = x_lo
        xs[2 * D:3 * D, :] = x_hi
        pre = jnp.dot(wt3, xs[...], preferred_element_type=f32) + bias[...]
        cdf = 0.5 * (1.0 + lax.erf(pre * ROOT_HALF))
        put_triple(h2, pre * cdf, HID, cols, (0, 1))
        slope[:, cols] = cdf + pre * jnp.exp(-0.5 * pre * pre) * INV_ROOT_TWO_PI


def hidden(pos, wo3, slope, gm, gm3, gh3):
    step = 512
    for start in range(0, pos, step):
        cols = slice(start, start + step)
        put_triple(gm3, gm[:, cols], D, cols, (0, 1, 0))
        gh = jnp.dot(wo3[...], gm3[:, cols], preferred_element_type=f32) * slope[:, cols]
        put_triple(gh3, gh, HID, cols, (0, 1, 0))


def inward(pos, wi3, gm, gh3, out):
    step = 512
    for start in range(0, pos, step):
        cols = slice(start, start + step)
        out[:, cols] = gm[:, cols] + jnp.dot(wi3[...], gh3[:, cols], preferred_element_type=f32)


def weight_terms(factor, odd, x2, gh, h2, gm, keep, send):
    def nt(a, b):
        return lax.dot_general(a, b, (((1,), (1,)), ((), ())), preferred_element_type=f32)

    d1 = D + 16
    first = nt(x2[0:d1, :], gh[0:HID, :]) + nt(x2[0:d1, :], gh[HID:2 * HID, :]) + nt(x2[d1:2 * d1, :], gh[0:HID, :])
    second = nt(gm[0:D, :], h2[0:HID, :]) + nt(gm[0:D, :], h2[HID:2 * HID, :]) + nt(gm[D:2 * D, :], h2[0:HID, :])
    first, second = first[0:D + 8] * factor, second * factor

    def put(part, out):
        rows, used = part.shape[0], 0
        for j in range(HID // LANES):
            out[used:used + rows, :] = part[:, j * LANES:(j + 1) * LANES]
            used += rows
        out[used:, :] = jnp.zeros((out.shape[0] - used, LANES), f32)

    @pl.when(odd == 0)
    def _():
        put(first, keep)
        put(second, send)

    @pl.when(odd == 1)
    def _():
        put(second, keep)
        put(first, send)


def plan_loads(sems, sources, targets):
    return [pltpu.make_async_copy(src, dst, sems.at[n]) for n, (src, dst) in enumerate(zip(sources, targets))]


def upper_kernel(hops, pos, factor, tab1, tab0, src_h, wo3_h, slope_h, wi3_h, x2_h, h2_h, near_in, *refs):
    far_in, refs = refs[:hops], refs[hops:]
    near, refs = refs[0], refs[1:]
    far, refs = refs[:hops - 1], refs[hops - 1:]
    keep, send, grad_h, src, grad, wo3, slope, wi3, x2, h2, gm3, gh3, gm, join, sems = refs
    where = place_bits()
    first, *loads = plan_loads(sems, (src_h, wo3_h, slope_h, wi3_h, x2_h, h2_h), (src, wo3, slope, wi3, x2, h2))
    first.start()
    unpack_far(where, tab1, far_in, gm, hops, pos)
    first.wait()
    for load in loads:
        load.start()
    unpack_near(src, tab1, near_in, gm, join, pos)
    loads[0].wait()
    loads[1].wait()
    hidden(pos, wo3, slope, gm, gm3, gh3)
    loads[2].wait()
    inward(pos, wi3, gm, gh3, grad)
    store = pltpu.make_async_copy(grad, grad_h, sems.at[6])
    store.start()
    pack(grad, tab0, far, near, hops, pos)
    loads[3].wait()
    loads[4].wait()
    weight_terms(factor, where[0], x2, gh3, h2, gm3, keep, send)
    store.wait()


def lower_kernel(hops, pos, factor, tab0, src_h, wo3_h, slope_h, x2_h, h2_h, near_in, *refs):
    far_in, refs = refs[:hops], refs[hops:]
    keep, send, gm_h, gh_h, src, gm, gh3, wo3, slope, x2, h2, gm3, join, sems = refs
    where = place_bits()
    first, *loads = plan_loads(sems, (src_h, wo3_h, slope_h, x2_h, h2_h), (src, wo3, slope, x2, h2))
    first.start()
    unpack_far(where, tab0, far_in, gm, hops, pos)
    first.wait()
    for load in loads:
        load.start()
    unpack_near(src, tab0, near_in, gm, join, pos)
    stores = [pltpu.make_async_copy(gm, gm_h, sems.at[5]), pltpu.make_async_copy(gh3, gh_h, sems.at[6])]
    stores[0].start()
    loads[0].wait()
    loads[1].wait()
    hidden(pos, wo3, slope, gm, gm3, gh3)
    stores[1].start()
    loads[2].wait()
    loads[3].wait()
    weight_terms(factor, where[0], x2, gh3, h2, gm3, keep, send)
    for store in stores:
        store.wait()


def input_kernel(pos, wi3_h, gm_h, gh_h, out, wi3, gm, gh3, sems):
    loads = plan_loads(sems, (wi3_h, gm_h, gh_h), (wi3, gm, gh3))
    for load in loads:
        load.start()
    for load in loads:
        load.wait()
    inward(pos, wi3, gm, gh3, out)


def finish_kernel(*refs):
    sums, (w_in_grad, bias_grad, w_out_t_grad) = refs[:4], refs[4:]
    rows = D + 8
    odd, _ = place_bits()

    def put(layer, first, second):
        for j in range(HID // LANES):
            lanes = slice(j * LANES, (j + 1) * LANES)
            w_in_grad[layer, :, lanes] = first[j * rows:j * rows + D, :]
            bias_grad[layer:layer + 1, lanes] = first[j * rows + D:j * rows + D + 1, :]
            w_out_t_grad[layer, :, lanes] = second[j * D:(j + 1) * D, :]

    for layer in range(2):
        mine, other = sums[2 * layer], sums[2 * layer + 1]

        @pl.when(odd == 0)
        def _(layer=layer, mine=mine, other=other):
            put(layer, mine, other)

        @pl.when(odd == 1)
        def _(layer=layer, mine=mine, other=other):
            put(layer, other, mine)


def from_ahead(value, steps):
    count = lax.axis_size("seq")
    return lax.ppermute(value, "seq", [(s, (s - steps) % count) for s in range(count)])


def exchange(value, mask):
    count = lax.axis_size("seq")
    return lax.ppermute(value, "seq", [(s, s ^ mask) for s in range(count)])


def fold(x, mask):
    half = x.shape[0] // 2
    bit = (lax.axis_index("seq") & mask) != 0
    low, high = x[:half], x[half:]
    return jnp.where(bit, high, low) + exchange(jnp.where(bit, low, high), mask)


def spread(x, mask):
    bit = (lax.axis_index("seq") & mask) != 0
    other = exchange(x, mask)
    return jnp.concatenate([jnp.where(bit, other, x), jnp.where(bit, x, other)], 0)


def groups_of_four(offset):
    count = lax.axis_size("seq")
    return [(s, (s + 4 * offset) % count) for s in range(count)]


def fold_far(x):
    number = lax.axis_size("seq") // 4
    mine = lax.axis_index("seq") >> 2
    rows = x.shape[0] // number

    def part(group):
        return lax.dynamic_slice_in_dim(x, (group % number) * rows, rows, 0)

    arrived = [lax.ppermute(part(mine + o), "seq", groups_of_four(o)) for o in range(1, number)]
    return sum(arrived, part(mine))


def spread_far(x):
    number = lax.axis_size("seq") // 4
    mine = lax.axis_index("seq") >> 2
    rows = x.shape[0]
    arrived = [lax.ppermute(x, "seq", groups_of_four(o)) for o in range(1, number)]
    turned = jnp.concatenate([x] + arrived[::-1], 0)
    return lax.dynamic_slice_in_dim(jnp.concatenate([turned, turned], 0), ((number - mine) % number) * rows, number * rows, 0)


def shape(*dims, dtype=f32):
    return jax.ShapeDtypeStruct(dims, dtype)


def stay(*values, where=pltpu.VMEM):
    return [pltpu.with_memory_space_constraint(v, where) for v in values]


def stored(*dims, dtype=f32):
    return pltpu.HBM(dims, dtype)


def held(*dims, dtype=f32):
    return pltpu.VMEM(dims, dtype)


def body(first_inputs, second_inputs, out_grad, weight_in, bias_in, weight_out, distances):
    pos = first_inputs.shape[1]
    count = lax.axis_size("seq")
    hops = count.bit_length() - 1
    factor = 1.0 / math.sqrt(pos * count)
    near_width = near_slots(pos)[1]
    far_shapes = [shape(MOST * TW, pos)] * (hops - 1)
    near_shape = shape(TW, near_width)
    half = -(-3 * (D + 8) // (8 * count)) * 8 * count
    far_hops = [1 << k for k in range(1, hops)]

    def travel(near, far):
        paired = exchange(far[0], 2)
        moved = [from_ahead(f, h) for f, h in zip(far[:0:-1], far_hops[:0:-1])][::-1]
        near = from_ahead(near, 1)
        passed = lax.ppermute(paired, "seq", [(s, (s - 4) % count) for s in range(count) if s & 2])
        return near, [paired, passed] + moved

    whole_s = pltpu.VMEM((D, pos), f32)
    gm3_s = pltpu.VMEM((3 * D, pos), bf16)
    join_s = pltpu.VMEM((4, TW, 2 * pos + LANES), f32)
    distances, out_grad_h = [pltpu.with_memory_space_constraint(v, pltpu.HBM) for v in (distances, out_grad)]
    tab_1, near, *far = pl.pallas_call(
        lambda *refs: pack_kernel(hops, pos, *refs),
        out_shape=[shape(64, dtype=i32), near_shape] + far_shapes,
        in_specs=[SM, HB],
        out_specs=[SM] + [VM] * hops,
        scratch_shapes=[whole_s, pltpu.SemaphoreType.DMA],
        **kernel_options("pack", 3, 2),
    )(distances, out_grad_h)
    near, far = travel(near, far)

    w_out_t = jnp.transpose(weight_out, (0, 2, 1))
    saved = [first_inputs, second_inputs]
    act_ins = []
    for layer in range(2):
        act_ins += [saved[layer], weight_in[layer], bias_in[layer][:, None], w_out_t[layer]]
    act_shapes = [
        stored(2 * D + 32, pos, dtype=bf16),
        stored(2 * HID, pos, dtype=bf16),
        stored(HID, pos),
        stored(D, 3 * HID, dtype=bf16),
        stored(HID, 3 * D, dtype=bf16),
    ]
    tab_0, *acts = pl.pallas_call(
        lambda *refs: act_kernel(hops, pos, *refs),
        out_shape=[shape(64, dtype=i32)] + act_shapes * 2,
        in_specs=[SM] + [VM] * 8,
        out_specs=[SM] + [VM] * 10,
        scratch_shapes=[pltpu.VMEM((3 * D, 256), bf16)],
        **kernel_options("act", 24, 5),
    )(distances, *act_ins)
    x2_0, h2_0, slope_0, wi3_0, wo3_0, x2_1, h2_1, slope_1, wi3_1, wo3_1 = acts

    gh3_s = pltpu.VMEM((3 * HID, pos), bf16)
    x2_s = pltpu.VMEM((2 * D + 32, pos), bf16)
    h2_s = pltpu.VMEM((2 * HID, pos), bf16)
    slope_s = pltpu.VMEM((HID, pos), f32)
    wi3_s = pltpu.VMEM((D, 3 * HID), bf16)
    wo3_s = pltpu.VMEM((HID, 3 * D), bf16)
    sems_s = pltpu.SemaphoreType.DMA((7,))
    near, *rest = pl.pallas_call(
        lambda *refs: upper_kernel(hops, pos, factor, *refs),
        out_shape=[near_shape] + far_shapes + [shape(half, LANES)] * 2 + [stored(D, pos)],
        in_specs=[SM] * 2 + [HB] * 6 + [VM] * (hops + 1),
        out_specs=[VM] * (hops + 2) + [HB],
        scratch_shapes=[whole_s, whole_s, wo3_s, slope_s, wi3_s, x2_s, h2_s, gm3_s, gh3_s, whole_s, join_s, sems_s],
        **kernel_options("upper", 16, 6),
    )(tab_1, tab_0, *stay(out_grad, wo3_1, slope_1, wi3_1, x2_1, h2_1, where=pltpu.HBM), near, *far)
    far, (keep_1, send_1, grad_1) = rest[:hops - 1], rest[hops - 1:]
    near, far = travel(near, far)

    sum_1 = keep_1 + exchange(send_1, 1)
    sum_1 = fold(sum_1, 2)

    keep, send, gm_0, gh3_0 = pl.pallas_call(
        lambda *refs: lower_kernel(hops, pos, factor, *refs),
        out_shape=[shape(half, LANES)] * 2 + [stored(D, pos), stored(3 * HID, pos, dtype=bf16)],
        in_specs=[SM] + [HB] * 5 + [VM] * (hops + 1),
        out_specs=[VM] * 2 + [HB] * 2,
        scratch_shapes=[whole_s, whole_s, gh3_s, wo3_s, slope_s, x2_s, h2_s, gm3_s, join_s, sems_s],
        **kernel_options("lower", 16, 5),
    )(tab_0, *stay(grad_1, wo3_0, slope_0, x2_0, h2_0, where=pltpu.HBM), near, *far)
    sum_0 = keep + exchange(send, 1)
    steps = [lambda x: fold(x, 2), fold_far, spread_far, lambda x: spread(x, 2)]
    for step, ahead in zip(steps[:-1], steps[1:]):
        sum_1, _ = lax.optimization_barrier((sum_1, sum_0))
        sum_1 = ahead(sum_1)
        sum_0 = step(sum_0)
    sum_0, gm_0 = lax.optimization_barrier((sum_0, gm_0))

    input_grad = pl.pallas_call(
        lambda *refs: input_kernel(pos, *refs),
        out_shape=shape(D, pos),
        in_specs=[HB] * 3,
        out_specs=VM,
        scratch_shapes=[pltpu.VMEM((D, 3 * HID), bf16), whole_s, gh3_s, sems_s],
        **kernel_options("inward", 12, 3),
    )(*stay(wi3_0, gm_0, gh3_0, where=pltpu.HBM))
    sum_1, _ = lax.optimization_barrier((sum_1, sum_0))
    other_1 = exchange(sum_1, 1)
    sum_0 = spread(sum_0, 2)
    sum_0, input_grad = lax.optimization_barrier((sum_0, input_grad))
    other_0 = exchange(sum_0, 1)

    w_in_grad, bias_grad, w_out_t_grad = pl.pallas_call(
        finish_kernel,
        out_shape=[shape(2, D, HID), shape(2, HID), shape(2, D, HID)],
        in_specs=[VM] * 4,
        out_specs=[VM] * 3,
        **kernel_options("finish", 4, 1),
    )(sum_0, other_0, sum_1, other_1)
    return input_grad, w_in_grad, bias_grad, jnp.transpose(w_out_t_grad, (0, 2, 1))


def solution(mesh):
    whole = P(None, ("groups", "seq"))
    in_specs = (whole, whole, whole, P(), P(), P(), P())
    out_specs = (whole, P("groups", None, None), P("groups", None), P("groups", None, None))
    return jax.shard_map(body, mesh=mesh, in_specs=in_specs, out_specs=out_specs, check_vma=False)
```

```python
import math

import jax
import jax.numpy as jnp
from jax import lax
from jax.experimental import pallas as pl
from jax.experimental.pallas import tpu as pltpu
from jax.sharding import PartitionSpec as P

TRACKS = 18
TW = 16
MOST = 3
D = TRACKS * TW
HID = 384
INNER = TRACKS - MOST
LANES = 128
MIB = 1 << 20

ROOT_HALF = 0.7071067811865476
INV_ROOT_TWO_PI = 0.3989422804014327

f32, bf16, i32 = jnp.float32, jnp.bfloat16, jnp.int32
VM = pl.BlockSpec(memory_space=pltpu.VMEM)
SM = pl.BlockSpec(memory_space=pltpu.SMEM)
HB = pl.BlockSpec(memory_space=pltpu.HBM)


def kernel_options(name, mib, cost_us):
    return dict(
        name=name,
        compiler_params=pltpu.CompilerParams(vmem_limit_bytes=mib * MIB),
        cost_estimate=pl.CostEstimate(flops=int(cost_us * 1e9), bytes_accessed=int(cost_us * 3e6), transcendentals=0),
    )


def near_slots(pos):
    slots, offset = [], 0
    for slot in range(INNER):
        width = max(LANES, pos >> (slot // MOST))
        slots.append((offset, width))
        offset += width
    return slots, offset


def halves(value):
    high = value.astype(bf16)
    return high, (value - high.astype(f32)).astype(bf16)


def put_triple(ref, value, rows, cols, order):
    pair = halves(value)
    for place, which in enumerate(order):
        ref[place * rows:(place + 1) * rows, cols] = pair[which]


def fill_tables(dist, tab, layer, hops, pos):
    d = [dist[layer, t] for t in range(TRACKS)]
    key = [d[t] * 32 + (31 - t) for t in range(TRACKS)]
    rank = [jnp.int32(0)] * TRACKS
    for t in range(TRACKS):
        for u in range(t + 1, TRACKS):
            above = (key[u] > key[t]).astype(i32)
            rank[t] = rank[t] + above
            rank[u] = rank[u] + (1 - above)
    for t in range(TRACKS):
        tab[rank[t]] = jnp.int32(t)
    for k in range(hops):
        first = jnp.int32(0)
        for t in range(TRACKS):
            first = first + (d[t] > (pos << k)).astype(i32)
        tab[TRACKS + k] = first
    for t in range(TRACKS):
        tab[32 + t] = d[t]


def track_at(tab, k, slot):
    place = tab[TRACKS + k] + slot
    return place, tab[jnp.minimum(place, TRACKS - 1)]


def rows_of(track):
    return pl.ds(pl.multiple_of(track * TW, TW), TW)


def pack(src, tab, far, near, hops, pos):
    for k in range(hops - 1, 0, -1):
        for slot in range(MOST):
            _, t = track_at(tab, k, slot)
            far[k - 1][slot * TW:(slot + 1) * TW, :] = src[rows_of(t), :]
    for slot, (offset, width) in enumerate(near_slots(pos)[0]):
        _, t = track_at(tab, 0, slot)
        near[:, offset:offset + width] = src[rows_of(t), 0:width]


def place_bits():
    index = lax.axis_index("seq")
    return index & 1, (index >> 1) & 1


def unpack_far(where, tab, far, out, hops, pos):
    for k in range(1, hops):
        for slot in range(MOST):
            place, t = track_at(tab, k, slot)
            mine = (place < TRACKS) & (tab[32 + t] == (pos << k))
            sources = [(far[0], where[1] == 0), (far[1], where[1] == 1)] if k == 1 else [(far[k], True)]
            for source, here in sources:
                @pl.when(mine & here)
                def _(source=source, slot=slot, t=t):
                    out[rows_of(t), :] = source[slot * TW:(slot + 1) * TW, :]


def unpack_near(src, tab, near, out, join, pos):
    for slot, (offset, width) in enumerate(near_slots(pos)[0]):
        place, t = track_at(tab, 0, slot)

        @pl.when(place < TRACKS)
        def _(slot=slot, t=t, offset=offset, width=width):
            shift = tab[32 + t]
            join[slot % 4, :, :pos] = src[rows_of(t), :]
            join[slot % 4, :, pos:pos + width] = near[:, offset:offset + width]
            base = pl.multiple_of(shift // LANES * LANES, LANES)
            rest = shift % LANES
            window = join[slot % 4, :, pl.ds(base, pos + LANES)]
            turned = pltpu.roll(window, jnp.where(rest == 0, 0, pos + LANES - rest), 1)
            out[rows_of(t), :] = turned[:, :pos]


def pack_kernel(hops, pos, dist, src_h, tab, near, *refs):
    far, (src, sem) = refs[:-2], refs[-2:]
    load = pltpu.make_async_copy(src_h, src, sem)
    load.start()
    fill_tables(dist, tab, 1, hops, pos)
    load.wait()
    pack(src, tab, far, near, hops, pos)


def act_kernel(hops, pos, dist, *refs):
    ins, tab, outs, xs = refs[:8], refs[8], refs[9:19], refs[19]
    fill_tables(dist, tab, 0, hops, pos)
    for layer in range(2):
        act(pos, *ins[4 * layer:4 * layer + 4], *outs[5 * layer:5 * layer + 5], xs)


def act(pos, x, w_in, bias, w_out_t, x2, h2, slope, wi3, wo3, xs):
    step = 256
    wt = jnp.transpose(w_in[...], (1, 0))
    wt_hi, wt_lo = halves(wt)
    wt3 = jnp.concatenate([wt_hi, wt_hi, wt_lo], axis=1)
    w_hi, w_lo = halves(w_in[...])
    wi3[...] = jnp.concatenate([w_hi, w_hi, w_lo], axis=1)
    w_hi, w_lo = halves(jnp.transpose(w_out_t[...], (1, 0)))
    wo3[...] = jnp.concatenate([w_hi, w_hi, w_lo], axis=1)
    for start in range(0, pos, step):
        cols = slice(start, start + step)
        x_hi, x_lo = halves(x[:, cols])
        x2[0:D, cols] = x_hi
        x2[D:D + 16, cols] = jnp.ones((16, step), bf16)
        x2[D + 16:2 * D + 16, cols] = x_lo
        x2[2 * D + 16:2 * D + 32, cols] = jnp.zeros((16, step), bf16)
        xs[0:D, :] = x_hi
        xs[D:2 * D, :] = x_lo
        xs[2 * D:3 * D, :] = x_hi
        pre = jnp.dot(wt3, xs[...], preferred_element_type=f32) + bias[...]
        cdf = 0.5 * (1.0 + lax.erf(pre * ROOT_HALF))
        put_triple(h2, pre * cdf, HID, cols, (0, 1))
        slope[:, cols] = cdf + pre * jnp.exp(-0.5 * pre * pre) * INV_ROOT_TWO_PI


def hidden(pos, wo3, slope, gm, gm3, gh3):
    step = 512
    for start in range(0, pos, step):
        cols = slice(start, start + step)
        put_triple(gm3, gm[:, cols], D, cols, (0, 1, 0))
        gh = jnp.dot(wo3[...], gm3[:, cols], preferred_element_type=f32) * slope[:, cols]
        put_triple(gh3, gh, HID, cols, (0, 1, 0))


def inward(pos, wi3, gm, gh3, out):
    step = 512
    for start in range(0, pos, step):
        cols = slice(start, start + step)
        out[:, cols] = gm[:, cols] + jnp.dot(wi3[...], gh3[:, cols], preferred_element_type=f32)


def weight_terms(factor, odd, x2, gh, h2, gm, keep, send):
    def nt(a, b):
        return lax.dot_general(a, b, (((1,), (1,)), ((), ())), preferred_element_type=f32)

    d1 = D + 16
    first = nt(x2[0:d1, :], gh[0:HID, :]) + nt(x2[0:d1, :], gh[HID:2 * HID, :]) + nt(x2[d1:2 * d1, :], gh[0:HID, :])
    second = nt(gm[0:D, :], h2[0:HID, :]) + nt(gm[0:D, :], h2[HID:2 * HID, :]) + nt(gm[D:2 * D, :], h2[0:HID, :])
    first, second = first[0:D + 8] * factor, second * factor

    def put(part, out):
        rows, used = part.shape[0], 0
        for j in range(HID // LANES):
            out[used:used + rows, :] = part[:, j * LANES:(j + 1) * LANES]
            used += rows
        out[used:, :] = jnp.zeros((out.shape[0] - used, LANES), f32)

    @pl.when(odd == 0)
    def _():
        put(first, keep)
        put(second, send)

    @pl.when(odd == 1)
    def _():
        put(second, keep)
        put(first, send)


def plan_loads(sems, sources, targets):
    return [pltpu.make_async_copy(src, dst, sems.at[n]) for n, (src, dst) in enumerate(zip(sources, targets))]


def upper_kernel(hops, pos, factor, tab1, tab0, src_h, wo3_h, slope_h, wi3_h, x2_h, h2_h, near_in, *refs):
    far_in, refs = refs[:hops], refs[hops:]
    near, refs = refs[0], refs[1:]
    far, refs = refs[:hops - 1], refs[hops - 1:]
    keep, send, grad_h, src, grad, wo3, slope, wi3, x2, h2, gm3, gh3, gm, join, sems = refs
    where = place_bits()
    first, *loads = plan_loads(sems, (src_h, wo3_h, slope_h, wi3_h, x2_h, h2_h), (src, wo3, slope, wi3, x2, h2))
    first.start()
    unpack_far(where, tab1, far_in, gm, hops, pos)
    first.wait()
    for load in loads:
        load.start()
    unpack_near(src, tab1, near_in, gm, join, pos)
    loads[0].wait()
    loads[1].wait()
    hidden(pos, wo3, slope, gm, gm3, gh3)
    loads[2].wait()
    inward(pos, wi3, gm, gh3, grad)
    store = pltpu.make_async_copy(grad, grad_h, sems.at[6])
    store.start()
    pack(grad, tab0, far, near, hops, pos)
    loads[3].wait()
    loads[4].wait()
    weight_terms(factor, where[0], x2, gh3, h2, gm3, keep, send)
    store.wait()


def lower_kernel(hops, pos, factor, tab0, src_h, wo3_h, slope_h, x2_h, h2_h, near_in, *refs):
    far_in, refs = refs[:hops], refs[hops:]
    keep, send, gm_h, gh_h, src, gm, gh3, wo3, slope, x2, h2, gm3, join, sems = refs
    where = place_bits()
    first, *loads = plan_loads(sems, (src_h, wo3_h, slope_h, x2_h, h2_h), (src, wo3, slope, x2, h2))
    first.start()
    unpack_far(where, tab0, far_in, gm, hops, pos)
    first.wait()
    for load in loads:
        load.start()
    unpack_near(src, tab0, near_in, gm, join, pos)
    stores = [pltpu.make_async_copy(gm, gm_h, sems.at[5]), pltpu.make_async_copy(gh3, gh_h, sems.at[6])]
    stores[0].start()
    loads[0].wait()
    loads[1].wait()
    hidden(pos, wo3, slope, gm, gm3, gh3)
    stores[1].start()
    loads[2].wait()
    loads[3].wait()
    weight_terms(factor, where[0], x2, gh3, h2, gm3, keep, send)
    for store in stores:
        store.wait()


def input_kernel(pos, wi3_h, gm_h, gh_h, out, wi3, gm, gh3, sems):
    loads = plan_loads(sems, (wi3_h, gm_h, gh_h), (wi3, gm, gh3))
    for load in loads:
        load.start()
    for load in loads:
        load.wait()
    inward(pos, wi3, gm, gh3, out)


def finish_kernel(*refs):
    sums, (w_in_grad, bias_grad, w_out_t_grad) = refs[:4], refs[4:]
    rows = D + 8
    odd, _ = place_bits()

    def put(layer, first, second):
        for j in range(HID // LANES):
            lanes = slice(j * LANES, (j + 1) * LANES)
            w_in_grad[layer, :, lanes] = first[j * rows:j * rows + D, :]
            bias_grad[layer:layer + 1, lanes] = first[j * rows + D:j * rows + D + 1, :]
            w_out_t_grad[layer, :, lanes] = second[j * D:(j + 1) * D, :]

    for layer in range(2):
        mine, other = sums[2 * layer], sums[2 * layer + 1]

        @pl.when(odd == 0)
        def _(layer=layer, mine=mine, other=other):
            put(layer, mine, other)

        @pl.when(odd == 1)
        def _(layer=layer, mine=mine, other=other):
            put(layer, other, mine)


def from_ahead(value, steps):
    count = lax.axis_size("seq")
    return lax.ppermute(value, "seq", [(s, (s - steps) % count) for s in range(count)])


def exchange(value, mask):
    count = lax.axis_size("seq")
    return lax.ppermute(value, "seq", [(s, s ^ mask) for s in range(count)])


def fold(x, mask):
    half = x.shape[0] // 2
    bit = (lax.axis_index("seq") & mask) != 0
    low, high = x[:half], x[half:]
    return jnp.where(bit, high, low) + exchange(jnp.where(bit, low, high), mask)


def spread(x, mask):
    bit = (lax.axis_index("seq") & mask) != 0
    other = exchange(x, mask)
    return jnp.concatenate([jnp.where(bit, other, x), jnp.where(bit, x, other)], 0)


def groups_of_four(offset):
    count = lax.axis_size("seq")
    return [(s, (s + 4 * offset) % count) for s in range(count)]


def fold_far(x):
    number = lax.axis_size("seq") // 4
    mine = lax.axis_index("seq") >> 2
    rows = x.shape[0] // number

    def part(group):
        return lax.dynamic_slice_in_dim(x, (group % number) * rows, rows, 0)

    arrived = [lax.ppermute(part(mine + o), "seq", groups_of_four(o)) for o in range(1, number)]
    return sum(arrived, part(mine))


def spread_far(x):
    number = lax.axis_size("seq") // 4
    mine = lax.axis_index("seq") >> 2
    rows = x.shape[0]
    arrived = [lax.ppermute(x, "seq", groups_of_four(o)) for o in range(1, number)]
    turned = jnp.concatenate([x] + arrived[::-1], 0)
    return lax.dynamic_slice_in_dim(jnp.concatenate([turned, turned], 0), ((number - mine) % number) * rows, number * rows, 0)


def shape(*dims, dtype=f32):
    return jax.ShapeDtypeStruct(dims, dtype)


def stay(*values, where=pltpu.VMEM):
    return [pltpu.with_memory_space_constraint(v, where) for v in values]


def stored(*dims, dtype=f32):
    return pltpu.HBM(dims, dtype)


def held(*dims, dtype=f32):
    return pltpu.VMEM(dims, dtype)


def body(first_inputs, second_inputs, out_grad, weight_in, bias_in, weight_out, distances):
    pos = first_inputs.shape[1]
    count = lax.axis_size("seq")
    hops = count.bit_length() - 1
    factor = 1.0 / math.sqrt(pos * count)
    near_width = near_slots(pos)[1]
    far_shapes = [shape(MOST * TW, pos)] * (hops - 1)
    near_shape = shape(TW, near_width)
    half = -(-3 * (D + 8) // (8 * count)) * 8 * count
    far_hops = [1 << k for k in range(1, hops)]

    def travel(near, far):
        paired = exchange(far[0], 2)
        moved = [from_ahead(f, h) for f, h in zip(far[:0:-1], far_hops[:0:-1])][::-1]
        near = from_ahead(near, 1)
        passed = lax.ppermute(paired, "seq", [(s, (s - 4) % count) for s in range(count) if s & 2])
        return near, [paired, passed] + moved

    whole_s = pltpu.VMEM((D, pos), f32)
    gm3_s = pltpu.VMEM((3 * D, pos), bf16)
    join_s = pltpu.VMEM((4, TW, 2 * pos + LANES), f32)
    distances, out_grad_h = [pltpu.with_memory_space_constraint(v, pltpu.HBM) for v in (distances, out_grad)]
    tab_1, near, *far = pl.pallas_call(
        lambda *refs: pack_kernel(hops, pos, *refs),
        out_shape=[shape(64, dtype=i32), near_shape] + far_shapes,
        in_specs=[SM, HB],
        out_specs=[SM] + [VM] * hops,
        scratch_shapes=[whole_s, pltpu.SemaphoreType.DMA],
        **kernel_options("pack", 3, 2),
    )(distances, out_grad_h)
    near, far = travel(near, far)

    w_out_t = jnp.transpose(weight_out, (0, 2, 1))
    saved = [first_inputs, second_inputs]
    act_ins = []
    for layer in range(2):
        act_ins += [saved[layer], weight_in[layer], bias_in[layer][:, None], w_out_t[layer]]
    act_shapes = [
        stored(2 * D + 32, pos, dtype=bf16),
        stored(2 * HID, pos, dtype=bf16),
        stored(HID, pos),
        stored(D, 3 * HID, dtype=bf16),
        stored(HID, 3 * D, dtype=bf16),
    ]
    tab_0, *acts = pl.pallas_call(
        lambda *refs: act_kernel(hops, pos, *refs),
        out_shape=[shape(64, dtype=i32)] + act_shapes * 2,
        in_specs=[SM] + [VM] * 8,
        out_specs=[SM] + [VM] * 10,
        scratch_shapes=[pltpu.VMEM((3 * D, 256), bf16)],
        **kernel_options("act", 24, 5),
    )(distances, *act_ins)
    x2_0, h2_0, slope_0, wi3_0, wo3_0, x2_1, h2_1, slope_1, wi3_1, wo3_1 = acts

    gh3_s = pltpu.VMEM((3 * HID, pos), bf16)
    x2_s = pltpu.VMEM((2 * D + 32, pos), bf16)
    h2_s = pltpu.VMEM((2 * HID, pos), bf16)
    slope_s = pltpu.VMEM((HID, pos), f32)
    wi3_s = pltpu.VMEM((D, 3 * HID), bf16)
    wo3_s = pltpu.VMEM((HID, 3 * D), bf16)
    sems_s = pltpu.SemaphoreType.DMA((7,))
    near, *rest = pl.pallas_call(
        lambda *refs: upper_kernel(hops, pos, factor, *refs),
        out_shape=[near_shape] + far_shapes + [shape(half, LANES)] * 2 + [stored(D, pos)],
        in_specs=[SM] * 2 + [HB] * 6 + [VM] * (hops + 1),
        out_specs=[VM] * (hops + 2) + [HB],
        scratch_shapes=[whole_s, whole_s, wo3_s, slope_s, wi3_s, x2_s, h2_s, gm3_s, gh3_s, whole_s, join_s, sems_s],
        **kernel_options("upper", 16, 6),
    )(tab_1, tab_0, *stay(out_grad, wo3_1, slope_1, wi3_1, x2_1, h2_1, where=pltpu.HBM), near, *far)
    far, (keep_1, send_1, grad_1) = rest[:hops - 1], rest[hops - 1:]
    near, far = travel(near, far)

    sum_1 = keep_1 + exchange(send_1, 1)
    sum_1 = fold(sum_1, 2)

    keep, send, gm_0, gh3_0 = pl.pallas_call(
        lambda *refs: lower_kernel(hops, pos, factor, *refs),
        out_shape=[shape(half, LANES)] * 2 + [stored(D, pos), stored(3 * HID, pos, dtype=bf16)],
        in_specs=[SM] + [HB] * 5 + [VM] * (hops + 1),
        out_specs=[VM] * 2 + [HB] * 2,
        scratch_shapes=[whole_s, whole_s, gh3_s, wo3_s, slope_s, x2_s, h2_s, gm3_s, join_s, sems_s],
        **kernel_options("lower", 16, 5),
    )(tab_0, *stay(grad_1, wo3_0, slope_0, x2_0, h2_0, where=pltpu.HBM), near, *far)
    sum_0 = keep + exchange(send, 1)
    steps = [lambda x: fold(x, 2), fold_far, spread_far, lambda x: spread(x, 2)]
    for number, (step, ahead) in enumerate(zip(steps[:-1], steps[1:])):
        if number > 0:
            sum_1, _ = lax.optimization_barrier((sum_1, sum_0))
        sum_1 = ahead(sum_1)
        sum_0 = step(sum_0)
    sum_0, gm_0 = lax.optimization_barrier((sum_0, gm_0))

    input_grad = pl.pallas_call(
        lambda *refs: input_kernel(pos, *refs),
        out_shape=shape(D, pos),
        in_specs=[HB] * 3,
        out_specs=VM,
        scratch_shapes=[pltpu.VMEM((D, 3 * HID), bf16), whole_s, gh3_s, sems_s],
        **kernel_options("inward", 12, 3),
    )(*stay(wi3_0, gm_0, gh3_0, where=pltpu.HBM))
    sum_1, _ = lax.optimization_barrier((sum_1, sum_0))
    other_1 = exchange(sum_1, 1)
    sum_0 = spread(sum_0, 2)
    sum_0, input_grad = lax.optimization_barrier((sum_0, input_grad))
    other_0 = exchange(sum_0, 1)

    w_in_grad, bias_grad, w_out_t_grad = pl.pallas_call(
        finish_kernel,
        out_shape=[shape(2, D, HID), shape(2, HID), shape(2, D, HID)],
        in_specs=[VM] * 4,
        out_specs=[VM] * 3,
        **kernel_options("finish", 4, 1),
    )(sum_0, other_0, sum_1, other_1)
    return input_grad, w_in_grad, bias_grad, jnp.transpose(w_out_t_grad, (0, 2, 1))


def solution(mesh):
    whole = P(None, ("groups", "seq"))
    in_specs = (whole, whole, whole, P(), P(), P(), P())
    out_specs = (whole, P("groups", None, None), P("groups", None), P("groups", None, None))
    return jax.shard_map(body, mesh=mesh, in_specs=in_specs, out_specs=out_specs, check_vma=False)
```

```python
import math

import jax
import jax.numpy as jnp
from jax import lax
from jax.experimental import pallas as pl
from jax.experimental.pallas import tpu as pltpu
from jax.sharding import PartitionSpec as P

TRACKS = 18
TW = 16
MOST = 3
D = TRACKS * TW
HID = 384
INNER = TRACKS - MOST
LANES = 128
MIB = 1 << 20

ROOT_HALF = 0.7071067811865476
INV_ROOT_TWO_PI = 0.3989422804014327

f32, bf16, i32 = jnp.float32, jnp.bfloat16, jnp.int32
VM = pl.BlockSpec(memory_space=pltpu.VMEM)
SM = pl.BlockSpec(memory_space=pltpu.SMEM)
HB = pl.BlockSpec(memory_space=pltpu.HBM)


def kernel_options(name, mib, cost_us):
    return dict(
        name=name,
        compiler_params=pltpu.CompilerParams(vmem_limit_bytes=mib * MIB),
        cost_estimate=pl.CostEstimate(flops=int(cost_us * 1e9), bytes_accessed=int(cost_us * 3e6), transcendentals=0),
    )


def near_slots(pos):
    slots, offset = [], 0
    for slot in range(INNER):
        width = max(LANES, pos >> (slot // MOST))
        slots.append((offset, width))
        offset += width
    return slots, offset


def halves(value):
    high = value.astype(bf16)
    return high, (value - high.astype(f32)).astype(bf16)


def put_triple(ref, value, rows, cols, order):
    pair = halves(value)
    for place, which in enumerate(order):
        ref[place * rows:(place + 1) * rows, cols] = pair[which]


def fill_tables(dist, tab, layer, hops, pos):
    d = [dist[layer, t] for t in range(TRACKS)]
    key = [d[t] * 32 + (31 - t) for t in range(TRACKS)]
    rank = [jnp.int32(0)] * TRACKS
    for t in range(TRACKS):
        for u in range(t + 1, TRACKS):
            above = (key[u] > key[t]).astype(i32)
            rank[t] = rank[t] + above
            rank[u] = rank[u] + (1 - above)
    for t in range(TRACKS):
        tab[rank[t]] = jnp.int32(t)
    for k in range(hops):
        first = jnp.int32(0)
        for t in range(TRACKS):
            first = first + (d[t] > (pos << k)).astype(i32)
        tab[TRACKS + k] = first
    for t in range(TRACKS):
        tab[32 + t] = d[t]


def track_at(tab, k, slot):
    place = tab[TRACKS + k] + slot
    return place, tab[jnp.minimum(place, TRACKS - 1)]


def rows_of(track):
    return pl.ds(pl.multiple_of(track * TW, TW), TW)


def pack(src, tab, far, near, hops, pos):
    for k in range(hops - 1, 0, -1):
        for slot in range(MOST):
            _, t = track_at(tab, k, slot)
            far[k - 1][slot * TW:(slot + 1) * TW, :] = src[rows_of(t), :]
    for slot, (offset, width) in enumerate(near_slots(pos)[0]):
        _, t = track_at(tab, 0, slot)
        near[:, offset:offset + width] = src[rows_of(t), 0:width]


def place_bits():
    index = lax.axis_index("seq")
    return index & 1, (index >> 1) & 1


def unpack_far(where, tab, far, out, hops, pos):
    for k in range(1, hops):
        for slot in range(MOST):
            place, t = track_at(tab, k, slot)
            mine = (place < TRACKS) & (tab[32 + t] == (pos << k))
            sources = [(far[0], where[1] == 0), (far[1], where[1] == 1)] if k == 1 else [(far[k], True)]
            for source, here in sources:
                @pl.when(mine & here)
                def _(source=source, slot=slot, t=t):
                    out[rows_of(t), :] = source[slot * TW:(slot + 1) * TW, :]


def unpack_near(src, tab, near, out, join, pos):
    for slot, (offset, width) in enumerate(near_slots(pos)[0]):
        place, t = track_at(tab, 0, slot)

        @pl.when(place < TRACKS)
        def _(slot=slot, t=t, offset=offset, width=width):
            shift = tab[32 + t]
            join[slot % 4, :, :pos] = src[rows_of(t), :]
            join[slot % 4, :, pos:pos + width] = near[:, offset:offset + width]
            base = pl.multiple_of(shift // LANES * LANES, LANES)
            rest = shift % LANES
            window = join[slot % 4, :, pl.ds(base, pos + LANES)]
            turned = pltpu.roll(window, jnp.where(rest == 0, 0, pos + LANES - rest), 1)
            out[rows_of(t), :] = turned[:, :pos]


def pack_kernel(hops, pos, dist, src_h, tab, near, *refs):
    far, (src, sem) = refs[:-2], refs[-2:]
    load = pltpu.make_async_copy(src_h, src, sem)
    load.start()
    fill_tables(dist, tab, 1, hops, pos)
    load.wait()
    pack(src, tab, far, near, hops, pos)


def act_kernel(hops, pos, dist, *refs):
    ins, tab, outs, xs = refs[:8], refs[8], refs[9:19], refs[19]
    fill_tables(dist, tab, 0, hops, pos)
    for layer in range(2):
        act(pos, *ins[4 * layer:4 * layer + 4], *outs[5 * layer:5 * layer + 5], xs)


def act(pos, x, w_in, bias, w_out_t, x2, h2, slope, wi3, wo3, xs):
    step = 256
    wt = jnp.transpose(w_in[...], (1, 0))
    wt_hi, wt_lo = halves(wt)
    wt3 = jnp.concatenate([wt_hi, wt_hi, wt_lo], axis=1)
    w_hi, w_lo = halves(w_in[...])
    wi3[...] = jnp.concatenate([w_hi, w_hi, w_lo], axis=1)
    w_hi, w_lo = halves(jnp.transpose(w_out_t[...], (1, 0)))
    wo3[...] = jnp.concatenate([w_hi, w_hi, w_lo], axis=1)
    for start in range(0, pos, step):
        cols = slice(start, start + step)
        x_hi, x_lo = halves(x[:, cols])
        x2[0:D, cols] = x_hi
        x2[D:D + 16, cols] = jnp.ones((16, step), bf16)
        x2[D + 16:2 * D + 16, cols] = x_lo
        x2[2 * D + 16:2 * D + 32, cols] = jnp.zeros((16, step), bf16)
        xs[0:D, :] = x_hi
        xs[D:2 * D, :] = x_lo
        xs[2 * D:3 * D, :] = x_hi
        pre = jnp.dot(wt3, xs[...], preferred_element_type=f32) + bias[...]
        cdf = 0.5 * (1.0 + lax.erf(pre * ROOT_HALF))
        put_triple(h2, pre * cdf, HID, cols, (0, 1))
        slope[:, cols] = cdf + pre * jnp.exp(-0.5 * pre * pre) * INV_ROOT_TWO_PI


def hidden(pos, wo3, slope, gm, gm3, gh3):
    step = 512
    for start in range(0, pos, step):
        cols = slice(start, start + step)
        put_triple(gm3, gm[:, cols], D, cols, (0, 1, 0))
        gh = jnp.dot(wo3[...], gm3[:, cols], preferred_element_type=f32) * slope[:, cols]
        put_triple(gh3, gh, HID, cols, (0, 1, 0))


def inward(pos, wi3, gm, gh3, out):
    step = 512
    for start in range(0, pos, step):
        cols = slice(start, start + step)
        out[:, cols] = gm[:, cols] + jnp.dot(wi3[...], gh3[:, cols], preferred_element_type=f32)


def weight_terms(factor, odd, x2, gh, h2, gm, keep, send):
    def nt(a, b):
        return lax.dot_general(a, b, (((1,), (1,)), ((), ())), preferred_element_type=f32)

    d1 = D + 16
    first = nt(x2[0:d1, :], gh[0:HID, :]) + nt(x2[0:d1, :], gh[HID:2 * HID, :]) + nt(x2[d1:2 * d1, :], gh[0:HID, :])
    second = nt(gm[0:D, :], h2[0:HID, :]) + nt(gm[0:D, :], h2[HID:2 * HID, :]) + nt(gm[D:2 * D, :], h2[0:HID, :])
    first, second = first[0:D + 8] * factor, second * factor

    def put(part, out):
        rows, used = part.shape[0], 0
        for j in range(HID // LANES):
            out[used:used + rows, :] = part[:, j * LANES:(j + 1) * LANES]
            used += rows
        out[used:, :] = jnp.zeros((out.shape[0] - used, LANES), f32)

    @pl.when(odd == 0)
    def _():
        put(first, keep)
        put(second, send)

    @pl.when(odd == 1)
    def _():
        put(second, keep)
        put(first, send)


def plan_loads(sems, sources, targets):
    return [pltpu.make_async_copy(src, dst, sems.at[n]) for n, (src, dst) in enumerate(zip(sources, targets))]


def upper_kernel(hops, pos, factor, tab1, tab0, src_h, wo3_h, slope_h, wi3_h, x2_h, h2_h, near_in, *refs):
    far_in, refs = refs[:hops], refs[hops:]
    near, refs = refs[0], refs[1:]
    far, refs = refs[:hops - 1], refs[hops - 1:]
    keep, send, grad_h, src, grad, wo3, slope, wi3, x2, h2, gm3, gh3, gm, join, sems = refs
    where = place_bits()
    first, *loads = plan_loads(sems, (src_h, wo3_h, slope_h, wi3_h, x2_h, h2_h), (src, wo3, slope, wi3, x2, h2))
    first.start()
    unpack_far(where, tab1, far_in, gm, hops, pos)
    first.wait()
    for load in loads:
        load.start()
    unpack_near(src, tab1, near_in, gm, join, pos)
    loads[0].wait()
    loads[1].wait()
    hidden(pos, wo3, slope, gm, gm3, gh3)
    loads[2].wait()
    inward(pos, wi3, gm, gh3, grad)
    store = pltpu.make_async_copy(grad, grad_h, sems.at[6])
    store.start()
    pack(grad, tab0, far, near, hops, pos)
    loads[3].wait()
    loads[4].wait()
    weight_terms(factor, where[0], x2, gh3, h2, gm3, keep, send)
    store.wait()


def lower_kernel(hops, pos, factor, tab0, src_h, wo3_h, slope_h, x2_h, h2_h, near_in, *refs):
    far_in, refs = refs[:hops], refs[hops:]
    keep, send, gm_h, gh_h, src, gm, gh3, wo3, slope, x2, h2, gm3, join, sems = refs
    where = place_bits()
    first, *loads = plan_loads(sems, (src_h, wo3_h, slope_h, x2_h, h2_h), (src, wo3, slope, x2, h2))
    first.start()
    unpack_far(where, tab0, far_in, gm, hops, pos)
    first.wait()
    for load in loads:
        load.start()
    unpack_near(src, tab0, near_in, gm, join, pos)
    stores = [pltpu.make_async_copy(gm, gm_h, sems.at[5]), pltpu.make_async_copy(gh3, gh_h, sems.at[6])]
    stores[0].start()
    loads[0].wait()
    loads[1].wait()
    hidden(pos, wo3, slope, gm, gm3, gh3)
    stores[1].start()
    loads[2].wait()
    loads[3].wait()
    weight_terms(factor, where[0], x2, gh3, h2, gm3, keep, send)
    for store in stores:
        store.wait()


def input_kernel(pos, wi3_h, gm_h, gh_h, out, wi3, gm, gh3, sems):
    loads = plan_loads(sems, (wi3_h, gm_h, gh_h), (wi3, gm, gh3))
    for load in loads:
        load.start()
    for load in loads:
        load.wait()
    inward(pos, wi3, gm, gh3, out)


def finish_kernel(*refs):
    sums, (w_in_grad, bias_grad, w_out_t_grad) = refs[:4], refs[4:]
    rows = D + 8
    odd, _ = place_bits()

    def put(layer, first, second):
        for j in range(HID // LANES):
            lanes = slice(j * LANES, (j + 1) * LANES)
            w_in_grad[layer, :, lanes] = first[j * rows:j * rows + D, :]
            bias_grad[layer:layer + 1, lanes] = first[j * rows + D:j * rows + D + 1, :]
            w_out_t_grad[layer, :, lanes] = second[j * D:(j + 1) * D, :]

    for layer in range(2):
        mine, other = sums[2 * layer], sums[2 * layer + 1]

        @pl.when(odd == 0)
        def _(layer=layer, mine=mine, other=other):
            put(layer, mine, other)

        @pl.when(odd == 1)
        def _(layer=layer, mine=mine, other=other):
            put(layer, other, mine)


def from_ahead(value, steps):
    count = lax.axis_size("seq")
    return lax.ppermute(value, "seq", [(s, (s - steps) % count) for s in range(count)])


def exchange(value, mask):
    count = lax.axis_size("seq")
    return lax.ppermute(value, "seq", [(s, s ^ mask) for s in range(count)])


def fold(x, mask):
    half = x.shape[0] // 2
    bit = (lax.axis_index("seq") & mask) != 0
    low, high = x[:half], x[half:]
    return jnp.where(bit, high, low) + exchange(jnp.where(bit, low, high), mask)


def spread(x, mask):
    bit = (lax.axis_index("seq") & mask) != 0
    other = exchange(x, mask)
    return jnp.concatenate([jnp.where(bit, other, x), jnp.where(bit, x, other)], 0)


def groups_of_four(offset):
    count = lax.axis_size("seq")
    return [(s, (s + 4 * offset) % count) for s in range(count)]


def fold_far(x):
    number = lax.axis_size("seq") // 4
    mine = lax.axis_index("seq") >> 2
    rows = x.shape[0] // number

    def part(group):
        return lax.dynamic_slice_in_dim(x, (group % number) * rows, rows, 0)

    arrived = [lax.ppermute(part(mine + o), "seq", groups_of_four(o)) for o in range(1, number)]
    return sum(arrived, part(mine))


def spread_far(x):
    number = lax.axis_size("seq") // 4
    mine = lax.axis_index("seq") >> 2
    rows = x.shape[0]
    arrived = [lax.ppermute(x, "seq", groups_of_four(o)) for o in range(1, number)]
    turned = jnp.concatenate([x] + arrived[::-1], 0)
    return lax.dynamic_slice_in_dim(jnp.concatenate([turned, turned], 0), ((number - mine) % number) * rows, number * rows, 0)


def shape(*dims, dtype=f32):
    return jax.ShapeDtypeStruct(dims, dtype)


def stay(*values, where=pltpu.VMEM):
    return [pltpu.with_memory_space_constraint(v, where) for v in values]


def stored(*dims, dtype=f32):
    return pltpu.HBM(dims, dtype)


def held(*dims, dtype=f32):
    return pltpu.VMEM(dims, dtype)


def body(first_inputs, second_inputs, out_grad, weight_in, bias_in, weight_out, distances):
    pos = first_inputs.shape[1]
    count = lax.axis_size("seq")
    hops = count.bit_length() - 1
    factor = 1.0 / math.sqrt(pos * count)
    near_width = near_slots(pos)[1]
    far_shapes = [shape(MOST * TW, pos)] * (hops - 1)
    near_shape = shape(TW, near_width)
    half = -(-3 * (D + 8) // (8 * count)) * 8 * count
    far_hops = [1 << k for k in range(1, hops)]

    def travel(near, far):
        paired = exchange(far[0], 2)
        moved = [from_ahead(f, h) for f, h in zip(far[:0:-1], far_hops[:0:-1])][::-1]
        near = from_ahead(near, 1)
        passed = lax.ppermute(paired, "seq", [(s, (s - 4) % count) for s in range(count) if s & 2])
        return near, [paired, passed] + moved

    whole_s = pltpu.VMEM((D, pos), f32)
    gm3_s = pltpu.VMEM((3 * D, pos), bf16)
    join_s = pltpu.VMEM((4, TW, 2 * pos + LANES), f32)
    distances, out_grad_h = [pltpu.with_memory_space_constraint(v, pltpu.HBM) for v in (distances, out_grad)]
    tab_1, near, *far = pl.pallas_call(
        lambda *refs: pack_kernel(hops, pos, *refs),
        out_shape=[shape(64, dtype=i32), near_shape] + far_shapes,
        in_specs=[SM, HB],
        out_specs=[SM] + [VM] * hops,
        scratch_shapes=[whole_s, pltpu.SemaphoreType.DMA],
        **kernel_options("pack", 3, 2),
    )(distances, out_grad_h)
    near, far = travel(near, far)

    w_out_t = jnp.transpose(weight_out, (0, 2, 1))
    saved = [first_inputs, second_inputs]
    act_ins = []
    for layer in range(2):
        act_ins += [saved[layer], weight_in[layer], bias_in[layer][:, None], w_out_t[layer]]
    act_shapes = [
        stored(2 * D + 32, pos, dtype=bf16),
        stored(2 * HID, pos, dtype=bf16),
        stored(HID, pos),
        stored(D, 3 * HID, dtype=bf16),
        stored(HID, 3 * D, dtype=bf16),
    ]
    tab_0, *acts = pl.pallas_call(
        lambda *refs: act_kernel(hops, pos, *refs),
        out_shape=[shape(64, dtype=i32)] + act_shapes * 2,
        in_specs=[SM] + [VM] * 8,
        out_specs=[SM] + [VM] * 10,
        scratch_shapes=[pltpu.VMEM((3 * D, 256), bf16)],
        **kernel_options("act", 24, 5),
    )(distances, *act_ins)
    x2_0, h2_0, slope_0, wi3_0, wo3_0, x2_1, h2_1, slope_1, wi3_1, wo3_1 = acts

    gh3_s = pltpu.VMEM((3 * HID, pos), bf16)
    x2_s = pltpu.VMEM((2 * D + 32, pos), bf16)
    h2_s = pltpu.VMEM((2 * HID, pos), bf16)
    slope_s = pltpu.VMEM((HID, pos), f32)
    wi3_s = pltpu.VMEM((D, 3 * HID), bf16)
    wo3_s = pltpu.VMEM((HID, 3 * D), bf16)
    sems_s = pltpu.SemaphoreType.DMA((7,))
    near, *rest = pl.pallas_call(
        lambda *refs: upper_kernel(hops, pos, factor, *refs),
        out_shape=[near_shape] + far_shapes + [shape(half, LANES)] * 2 + [stored(D, pos)],
        in_specs=[SM] * 2 + [HB] * 6 + [VM] * (hops + 1),
        out_specs=[VM] * (hops + 2) + [HB],
        scratch_shapes=[whole_s, whole_s, wo3_s, slope_s, wi3_s, x2_s, h2_s, gm3_s, gh3_s, whole_s, join_s, sems_s],
        **kernel_options("upper", 16, 6),
    )(tab_1, tab_0, *stay(out_grad, wo3_1, slope_1, wi3_1, x2_1, h2_1, where=pltpu.HBM), near, *far)
    far, (keep_1, send_1, grad_1) = rest[:hops - 1], rest[hops - 1:]
    near, far = travel(near, far)

    sum_1 = keep_1 + exchange(send_1, 1)
    sum_1 = fold(sum_1, 2)

    keep, send, gm_0, gh3_0 = pl.pallas_call(
        lambda *refs: lower_kernel(hops, pos, factor, *refs),
        out_shape=[shape(half, LANES)] * 2 + [stored(D, pos), stored(3 * HID, pos, dtype=bf16)],
        in_specs=[SM] + [HB] * 5 + [VM] * (hops + 1),
        out_specs=[VM] * 2 + [HB] * 2,
        scratch_shapes=[whole_s, whole_s, gh3_s, wo3_s, slope_s, x2_s, h2_s, gm3_s, join_s, sems_s],
        **kernel_options("lower", 16, 5),
    )(tab_0, *stay(grad_1, wo3_0, slope_0, x2_0, h2_0, where=pltpu.HBM), near, *far)
    sum_0 = keep + exchange(send, 1)
    steps = [lambda x: fold(x, 2), fold_far, spread_far, lambda x: spread(x, 2)]
    for number, (step, ahead) in enumerate(zip(steps[:-1], steps[1:])):
        if number > 1:
            sum_1, _ = lax.optimization_barrier((sum_1, sum_0))
        sum_1 = ahead(sum_1)
        sum_0 = step(sum_0)
    sum_0, gm_0 = lax.optimization_barrier((sum_0, gm_0))

    input_grad = pl.pallas_call(
        lambda *refs: input_kernel(pos, *refs),
        out_shape=shape(D, pos),
        in_specs=[HB] * 3,
        out_specs=VM,
        scratch_shapes=[pltpu.VMEM((D, 3 * HID), bf16), whole_s, gh3_s, sems_s],
        **kernel_options("inward", 12, 3),
    )(*stay(wi3_0, gm_0, gh3_0, where=pltpu.HBM))
    sum_1, _ = lax.optimization_barrier((sum_1, sum_0))
    other_1 = exchange(sum_1, 1)
    sum_0 = spread(sum_0, 2)
    sum_0, input_grad = lax.optimization_barrier((sum_0, input_grad))
    other_0 = exchange(sum_0, 1)

    w_in_grad, bias_grad, w_out_t_grad = pl.pallas_call(
        finish_kernel,
        out_shape=[shape(2, D, HID), shape(2, HID), shape(2, D, HID)],
        in_specs=[VM] * 4,
        out_specs=[VM] * 3,
        **kernel_options("finish", 4, 1),
    )(sum_0, other_0, sum_1, other_1)
    return input_grad, w_in_grad, bias_grad, jnp.transpose(w_out_t_grad, (0, 2, 1))


def solution(mesh):
    whole = P(None, ("groups", "seq"))
    in_specs = (whole, whole, whole, P(), P(), P(), P())
    out_specs = (whole, P("groups", None, None), P("groups", None), P("groups", None, None))
    return jax.shard_map(body, mesh=mesh, in_specs=in_specs, out_specs=out_specs, check_vma=False)
```
